32 devices in a mesh: replica: 4 (over y, core), shard: 8 (over z, x).
Axes of the slice: x: 2, y: 2, z: 4, core: 2. Of those that a mesh axis runs over, the one named last changes fastest.
Arguments:
- layer_input: bfloat16 [8192, 2048], P(('replica', 'shard')), may hold values from -6 to 6
- out_cotangent: bfloat16 [8192, 2048], P(('replica', 'shard')), may hold values from -6 to 6
- seq_lengths: int32 [4, 8, 2], P('replica'), may hold values from 1 to 192, 256 in all within a row
- seq_order: int32 [4, 16], P('replica'), may hold values from 0 to 15, each once within a row
- w_query: bfloat16 [2048, 2048], P('shard'), may hold values from -0.125 to 0.125
- w_key: bfloat16 [2048, 2048], P('shard'), may hold values from -0.125 to 0.125
- w_value: bfloat16 [2048, 2048], P('shard'), may hold values from -0.125 to 0.125
- w_beta: bfloat16 [2048, 16], P('shard'), may hold values from -0.125 to 0.125
- w_outgate: bfloat16 [2048, 2048], P('shard'), may hold values from -0.125 to 0.125
- w_output: bfloat16 [2048, 2048], P('shard'), may hold values from -0.125 to 0.125
- conv_query: bfloat16 [4, 2048], P(None, 'shard'), may hold values from -3 to 3
- conv_key: bfloat16 [4, 2048], P(None, 'shard'), may hold values from -3 to 3
- conv_value: bfloat16 [4, 2048], P(None, 'shard'), may hold values from -3 to 3
- attn_gain: bfloat16 [2048], P('shard'), may hold values from 0.5 to 1.5
- head_gain: bfloat16 [128], P('shard'), may hold values from 0.5 to 1.5
- mlp_gain: bfloat16 [2048], P('shard'), may hold values from 0.5 to 1.5
- w_gate: bfloat16 [2048, 5632], P('shard'), may hold values from -0.125 to 0.125
- w_up: bfloat16 [2048, 5632], P('shard'), may hold values from -0.125 to 0.125
- w_down: bfloat16 [5632, 2048], P('shard'), may hold values from -0.078125 to 0.078125
Outputs:
- layer_output: bfloat16 [8192, 2048], P(('replica', 'shard'))
- input_grad: bfloat16 [8192, 2048], P(('replica', 'shard'))
- g_query: float32 [2048, 2048], P('shard')
- g_key: float32 [2048, 2048], P('shard')
- g_value: float32 [2048, 2048], P('shard')
- g_beta: float32 [2048, 16], P('shard')
- g_outgate: float32 [2048, 2048], P('shard')
- g_output: float32 [2048, 2048], P('shard')
- g_conv_query: float32 [4, 2048], P(None, 'shard')
- g_conv_key: float32 [4, 2048], P(None, 'shard')
- g_conv_value: float32 [4, 2048], P(None, 'shard')
- g_attn_gain: float32 [2048], P('shard')
- g_head_gain: float32 [128], P('shard')
- g_mlp_gain: float32 [2048], P('shard')
- g_gate: float32 [2048, 5632], P('shard')
- g_up: float32 [2048, 5632], P('shard')
- g_down: float32 [5632, 2048], P('shard')
The draws below stay inside these ranges and needn't reach their ends.
Inputs may be any that keep to these rules, and one draw needn't show every extreme that they name: `seq_lengths`: entry [g, d, k] is the length of slot d * 2 + k of group g; the 2 lengths of each [g, d] add up to 256, and the largest of them is at most 192. `seq_order`: row g lists, for the runs of group g's stream in order, the slot of each run's sequence; every slot once.
All inputs are finite; a program needn't handle non-finite values.
Results may differ from the reference program's by a relative error of at most 0.025.
Values may be sent and summed in bfloat16 or wider, within the bound.
A program may use at most 512 MiB of HBM per device.

```python
import math
import jax
import jax.numpy as jnp
import numpy as np
from jax import lax

D = 2048
H = 16
HD = 128
FF = 5632
KW = 4
SPAN = 64
TOK_DEV = 256
SEQ_DEV = 2
MAXLEN = 192
SEQS = 16
GROUP_TOK = 2048
TOKENS = 8192
PACKED = 320
N_REPLICA = 4
N_SHARD = 8


def block_levels(stream_key, shape, cuts, least, top_value):
    gain, own = 1.0, jax.random.fold_in(stream_key, 6)
    for axis_at, blocks in cuts:
        heights = jnp.exp(jax.random.uniform(jax.random.fold_in(own, axis_at), (blocks,), jnp.float32, least / len(cuts), top_value / len(cuts)))
        gain = gain * jnp.repeat(heights, shape[axis_at] // blocks).reshape([-1 if axis == axis_at else 1 for axis in range(len(shape))])
    return gain


def split_up(amount, total, limit, slope):
    portions = [(1 << 20) // math.isqrt(grade ** slope) + 1 for grade in range(2, amount + 1)]
    rest, given = total - limit - (amount - 1), [1] * (amount - 1)
    while rest > 0:
        free = [i for i in range(amount - 1) if given[i] < limit]
        pool, left = sum([portions[i] for i in free]), rest
        for i in free:
            more = min(limit - given[i], max(1, left * portions[i] // pool), rest)
            given[i] = given[i] + more
            rest = rest - more
    return np.array([limit] + given)


def uneven_parts(rng, count, total, reach, slope):
    if count == 2:
        one = jax.random.randint(rng, (), max(1, total - reach), min(reach, total - 1) + 1)
        return jnp.stack([one, total - one])
    sizes = jnp.asarray(split_up(count, total, reach, slope), jnp.int32)
    couples = (count - 1) // 2
    donor, receiver = sizes[1:1 + 2 * couples:2], sizes[2:2 + 2 * couples:2]
    margin = jnp.minimum(donor - 1, reach - receiver)
    passed = jax.random.randint(jax.random.fold_in(rng, 1), (couples,), 0, 1 << 20) % (margin + 1)
    sizes = sizes.at[1:1 + 2 * couples:2].set(donor - passed).at[2:2 + 2 * couples:2].set(receiver + passed)
    return sizes[jax.random.permutation(jax.random.fold_in(rng, 2), count)]


def scatter_about(key, extent, width, limit, shards=(), held_as=jnp.bfloat16):
    entries = jax.random.normal(key, extent, jnp.float32) * width
    if len(shards) > 0:
        entries = block_levels(key, extent, shards, -0.22, 0.18) * entries
    return jnp.clip(entries, min=-limit, max=limit).astype(held_as)


def setup_inputs(seed: int = 0) -> dict:
    key_list = jax.random.split(jax.random.key(seed), 20)
    return {
        "layer_input": scatter_about(key_list[0], (TOKENS, D), 1.0, 6.0, ((0, 32),)),
        "out_cotangent": scatter_about(key_list[1], (TOKENS, D), 1.0, 6.0, ((0, 32),)),
        "seq_lengths": jax.vmap(lambda own: uneven_parts(own, SEQ_DEV, TOK_DEV, MAXLEN, 2))(jax.random.split(key_list[2], N_REPLICA * N_SHARD)).reshape((N_REPLICA, N_SHARD, SEQ_DEV)).astype(jnp.int32),
        "seq_order": jax.vmap(lambda own: jax.random.permutation(own, SEQS))(jax.random.split(key_list[3], N_REPLICA)).reshape((N_REPLICA, SEQS)).astype(jnp.int32),
        "w_query": scatter_about(key_list[4], (D, D), D ** -0.5, 0.125, ((0, 8),)),
        "w_key": scatter_about(key_list[5], (D, D), D ** -0.5, 0.125, ((0, 8),)),
        "w_value": scatter_about(key_list[6], (D, D), D ** -0.5, 0.125, ((0, 8),)),
        "w_beta": scatter_about(key_list[7], (D, H), D ** -0.5, 0.125, ((0, 8),)),
        "w_outgate": scatter_about(key_list[8], (D, D), D ** -0.5, 0.125, ((0, 8),)),
        "w_output": scatter_about(key_list[9], (D, D), D ** -0.5, 0.125, ((0, 8),)),
        "conv_query": scatter_about(key_list[10], (KW, D), KW ** -0.5, 3.0, ((1, 8),)),
        "conv_key": scatter_about(key_list[11], (KW, D), KW ** -0.5, 3.0, ((1, 8),)),
        "conv_value": scatter_about(key_list[12], (KW, D), KW ** -0.5, 3.0, ((1, 8),)),
        "attn_gain": jnp.clip(1.0 + 0.1 * jax.random.normal(key_list[13], (D,), jnp.float32), 0.5, 1.5).astype(jnp.bfloat16),
        "head_gain": jnp.clip(1.0 + 0.1 * jax.random.normal(key_list[14], (HD,), jnp.float32), 0.5, 1.5).astype(jnp.bfloat16),
        "mlp_gain": jnp.clip(1.0 + 0.1 * jax.random.normal(key_list[15], (D,), jnp.float32), 0.5, 1.5).astype(jnp.bfloat16),
        "w_gate": scatter_about(key_list[16], (D, FF), D ** -0.5, 0.125, ((0, 8),)),
        "w_up": scatter_about(key_list[17], (D, FF), D ** -0.5, 0.125, ((0, 8),)),
        "w_down": scatter_about(key_list[18], (FF, D), FF ** -0.5, 0.078125, ((0, 8),)),
    }


norm_eps = 1e-06
head_eps = 1e-05
unit_eps = 1e-06

@jax.custom_vjp
def low(v):
    return lax.optimization_barrier(v.astype(jnp.bfloat16)).astype(jnp.float32)

@jax.custom_vjp
def low_back(v):
    return v

def low_keep(v):
    return (low(v), None)

def low_pass(kept, grad):
    return (grad,)

def back_keep(v):
    return (v, None)

def back_low(kept, grad):
    return (low(grad),)
low.defvjp(low_keep, low_pass)
low_back.defvjp(back_keep, back_low)

def matmul(left_side, right_side):
    return jnp.dot(left_side, right_side, precision=lax.Precision.HIGHEST)

def rms_scale(values, scales, epsilon):
    return values * lax.rsqrt(lax.optimization_barrier(jnp.mean(values * values, axis=-1, keepdims=True)) + epsilon) * scales

def unit_rows(values):
    return values * lax.rsqrt(lax.optimization_barrier(jnp.sum(values * values, axis=-1, keepdims=True)) + unit_eps)

def causal_conv(signal, filters, positions):
    tap_count = filters.shape[0]
    row_count = signal.shape[0]
    padded = jnp.pad(signal, ((tap_count - 1, 0), (0, 0)))
    summed = signal * filters[0]
    for offset in range(1, tap_count):
        shifted = padded[tap_count - 1 - offset:tap_count - 1 - offset + row_count]
        summed = summed + jnp.where(positions[:, None] >= offset, shifted, jnp.zeros_like(shifted)) * filters[offset]
    return summed

def span_step(carried, pieces):
    queries, key_rows, value_rows, strength, restart = pieces
    carried = jnp.where(restart, jnp.zeros_like(carried), carried)
    highest = lax.Precision.HIGHEST
    span_len = key_rows.shape[1]
    row_ids = lax.broadcasted_iota(jnp.int32, (span_len, span_len), 0)
    col_ids = lax.broadcasted_iota(jnp.int32, (span_len, span_len), 1)
    identity = jnp.eye(span_len, dtype=jnp.float32)
    key_inner = jnp.einsum('hid,hjd->hij', key_rows, key_rows, precision=highest)
    strict_low = jnp.where(row_ids > col_ids, -strength[:, :, None] * key_inner, 0.0)
    inverse = identity + strict_low
    powered = strict_low
    for doubling in range(span_len.bit_length() - 2):
        powered = jnp.einsum('hij,hjk->hik', powered, powered, precision=highest)
        inverse = jnp.einsum('hij,hjk->hik', inverse, identity + powered, precision=highest)
    mixed_keys = jnp.einsum('hij,hjd->hid', inverse, strength[:, :, None] * key_rows, precision=highest)
    mixed_values = jnp.einsum('hij,hjd->hid', inverse, strength[:, :, None] * value_rows, precision=highest)
    fresh_rows = mixed_values - jnp.einsum('hid,hde->hie', mixed_keys, carried, precision=highest)
    scores = jnp.where(row_ids >= col_ids, jnp.einsum('hid,hjd->hij', queries, key_rows, precision=highest), 0.0)
    head_scale = queries.shape[-1] ** (-0.5)
    outputs = (jnp.einsum('hid,hde->hie', queries, carried, precision=highest) + jnp.einsum('hij,hje->hie', scores, fresh_rows, precision=highest)) * head_scale
    carried = carried + jnp.einsum('hid,hie->hde', key_rows, fresh_rows, precision=highest)
    return (carried, outputs)

def mixer(query_in, key_in, value_in, logit_in, query_taps, key_taps, value_taps, positions, restarts):
    row_count = query_in.shape[0]
    blocks = row_count // SPAN

    def prepare(signal, filters):
        return jax.nn.silu(causal_conv(signal, filters, positions)).reshape(row_count, H, HD)

    def to_blocks(heads_in):
        return heads_in.reshape(blocks, SPAN, H, HD).transpose(0, 2, 1, 3)
    queries = unit_rows(prepare(query_in, query_taps))
    key_rows = unit_rows(prepare(key_in, key_taps))
    value_rows = prepare(value_in, value_taps)
    strength = jax.nn.sigmoid(logit_in).reshape(blocks, SPAN, H).transpose(0, 2, 1)
    initial = jnp.zeros((H, HD, HD), jnp.float32)
    carried_end, outputs = lax.scan(jax.checkpoint(span_step), initial, (to_blocks(queries), to_blocks(key_rows), to_blocks(value_rows), strength, restarts))
    return outputs.transpose(0, 2, 1, 3).reshape(row_count, H * HD)

def packing(seq_lengths, seq_order):
    lengths = seq_lengths.reshape(N_REPLICA, SEQS)
    stream_len = jnp.take_along_axis(lengths, seq_order, axis=1)
    starts = jnp.cumsum(stream_len, axis=1) - stream_len
    inverse_order = jnp.argsort(seq_order, axis=1).astype(jnp.int32)
    slot_start = jnp.take_along_axis(starts, inverse_order, axis=1)
    count_grid = (seq_lengths + SPAN - 1) // SPAN
    first_grid = jnp.cumsum(count_grid, axis=2) - count_grid
    row_ids = jnp.arange(PACKED, dtype=jnp.int32)
    seq_index = lax.optimization_barrier(jnp.sum((first_grid[:, :, None, :] <= (row_ids // SPAN)[None, None, :, None]).astype(jnp.int32), axis=3)) - 1
    first_row = jnp.take_along_axis(first_grid, seq_index, axis=2) * SPAN
    offset_in = row_ids[None, None, :] - first_row
    filled = offset_in < jnp.take_along_axis(seq_lengths, seq_index, axis=2)
    positions = jnp.where(filled, offset_in, 0)
    slot_of = (jnp.arange(N_SHARD, dtype=jnp.int32)[None, :, None] * SEQ_DEV + seq_index).reshape(N_REPLICA, N_SHARD * PACKED)
    stream_at = jnp.take_along_axis(slot_start, slot_of, axis=1).reshape(N_REPLICA, N_SHARD, PACKED) + offset_in
    stream_at = jnp.where(filled, stream_at, 0)
    group_ids = jnp.arange(N_REPLICA, dtype=jnp.int32)[:, None, None]
    fetch_rows = ((group_ids * N_SHARD + stream_at % N_SHARD) * TOK_DEV + stream_at // N_SHARD).reshape(-1)
    block_ids = jnp.arange(PACKED // SPAN, dtype=jnp.int32)
    restarts = jnp.any(first_grid[:, :, None, :] == block_ids[None, None, :, None], axis=3).reshape(N_REPLICA * N_SHARD, PACKED // SPAN)
    token_ids = jnp.arange(TOK_DEV, dtype=jnp.int32)[None, :] * N_SHARD + jnp.arange(N_SHARD, dtype=jnp.int32)[:, None]
    stream_pos = jnp.broadcast_to(token_ids.reshape(1, GROUP_TOK), (N_REPLICA, GROUP_TOK))
    run_index = lax.optimization_barrier(jnp.sum((starts[:, None, :] <= stream_pos[:, :, None]).astype(jnp.int32), axis=2)) - 1
    token_slot = jnp.take_along_axis(seq_order, run_index, axis=1)
    token_off = stream_pos - jnp.take_along_axis(starts, run_index, axis=1)
    slot_first = jnp.take_along_axis(first_grid.reshape(N_REPLICA, SEQS), token_slot, axis=1)
    home_rows = ((group_ids[:, :, 0] * N_SHARD + token_slot // SEQ_DEV) * PACKED + slot_first * SPAN + token_off).reshape(-1)
    return (fetch_rows, filled.reshape(N_REPLICA * N_SHARD, PACKED), positions.reshape(N_REPLICA * N_SHARD, PACKED), restarts, home_rows)

def reference(layer_input, out_cotangent, seq_lengths, seq_order, w_query, w_key, w_value, w_beta, w_outgate, w_output, conv_query, conv_key, conv_value, attn_gain, head_gain, mlp_gain, w_gate, w_up, w_down):
    fetch_rows, filled, positions, restarts, home_rows = packing(seq_lengths, seq_order)

    def forward(params):
        source, query_w, key_w, value_w, beta_w, outgate_w, output_w, query_taps, key_taps, value_taps, attn_scale, head_scale, mlp_scale, gate_w, up_w, down_w = params
        normed = low(rms_scale(source, attn_scale, norm_eps))
        query_in = low(low_back(matmul(normed, query_w)))
        key_in = low(low_back(matmul(normed, key_w)))
        value_in = low(low_back(matmul(normed, value_w)))
        logit_in = low(low_back(matmul(normed, beta_w)))
        gate_pre = low_back(matmul(normed, outgate_w))

        def to_packed(rows_in):
            shaped = rows_in[fetch_rows].reshape(N_REPLICA * N_SHARD, PACKED, rows_in.shape[-1])
            return jnp.where(filled[:, :, None], shaped, 0.0)

        def group_mix(pieces):
            return mixer(pieces[0], pieces[1], pieces[2], pieces[3], query_taps, key_taps, value_taps, pieces[4], pieces[5])
        mixed = lax.map(jax.checkpoint(group_mix), (to_packed(query_in), to_packed(key_in), to_packed(value_in), to_packed(logit_in), positions, restarts))
        mixed_rows = low(low_back(mixed.reshape(-1, D)[home_rows]))
        head_normed = rms_scale(mixed_rows.reshape(TOKENS, H, HD), head_scale, head_eps).reshape(TOKENS, D)
        zed = low(head_normed * jax.nn.silu(gate_pre))
        hidden = source + low_back(matmul(zed, output_w))
        mlp_in = low(rms_scale(hidden, mlp_scale, norm_eps))
        gate_lin = low_back(matmul(mlp_in, gate_w))
        up_lin = low_back(matmul(mlp_in, up_w))
        product = low(jax.nn.silu(gate_lin) * up_lin)
        return hidden + matmul(product, down_w)
    params = (layer_input.astype(jnp.float32), w_query.astype(jnp.float32), w_key.astype(jnp.float32), w_value.astype(jnp.float32), w_beta.astype(jnp.float32), w_outgate.astype(jnp.float32), w_output.astype(jnp.float32), conv_query.astype(jnp.float32), conv_key.astype(jnp.float32), conv_value.astype(jnp.float32), attn_gain.astype(jnp.float32), head_gain.astype(jnp.float32), mlp_gain.astype(jnp.float32), w_gate.astype(jnp.float32), w_up.astype(jnp.float32), w_down.astype(jnp.float32))
    result, pullback = jax.vjp(forward, params)
    all_grads, = pullback(out_cotangent.astype(jnp.float32))
    return (result.astype(jnp.bfloat16), all_grads[0].astype(jnp.bfloat16), all_grads[1], all_grads[2], all_grads[3], all_grads[4], all_grads[5], all_grads[6], all_grads[7], all_grads[8], all_grads[9], all_grads[10], all_grads[11], all_grads[12], all_grads[13], all_grads[14], all_grads[15])
```

```python
import functools

import jax
import jax.numpy as jnp
from jax import lax
from jax.experimental import pallas as pl
from jax.experimental.pallas import tpu as pltpu
from jax.sharding import PartitionSpec as P

MESH = pl.DeviceIdType.MESH


def grid_of(axis):
    count = lax.axis_size(axis)
    if axis == "replica":
        across = 2 if count % 2 == 0 else 1
        return count // across, across
    depth = 4 if count % 4 == 0 else count
    return depth, count // depth


def line_neighbours(z, x, Z, X):
    return ((z + 1) * X + x, (z - 1) * X + x, z * X + x + 1, z * X + x - 1), (
        z < Z - 1,
        z > 0,
        x < X - 1,
        x > 0,
    )


def greet(axis, targets, exists):
    barrier = pltpu.get_barrier_semaphore()
    count = jnp.int32(0)
    for target, there in zip(targets, exists):

        @pl.when(there)
        def _(target=target):
            pl.semaphore_signal(
                barrier, inc=1, device_id={axis: target}, device_id_type=MESH
            )

        count = count + jnp.where(there, 1, 0)
    pl.semaphore_wait(barrier, count)


def gather_kernel(axis, Z, X, NC, x_ref, out_ref, own_sem, send_sem, recv_sem):
    me = lax.axis_index(axis)
    z, x = lax.div(me, X), lax.rem(me, X)
    rows = x_ref.shape[0] // NC
    targets, exists = line_neighbours(z, x, Z, X)
    own = pltpu.make_async_copy(x_ref, out_ref.at[me], own_sem)
    own.start()
    greet(axis, targets, exists)

    def copy(way, origin, c):
        part = pl.ds(c * rows, rows)
        return pltpu.make_async_remote_copy(
            src_ref=out_ref.at[origin, part],
            dst_ref=out_ref.at[origin, part],
            send_sem=send_sem.at[way, origin, c],
            recv_sem=recv_sem.at[origin, c],
            device_id={axis: targets[way]},
            device_id_type=MESH,
        )

    for c in range(NC):
        for way in range(4):

            @pl.when(exists[way])
            def _(way=way, c=c):
                part = pl.ds(c * rows, rows)
                pltpu.make_async_remote_copy(
                    src_ref=x_ref.at[part],
                    dst_ref=out_ref.at[me, part],
                    send_sem=send_sem.at[way, me, c],
                    recv_sem=recv_sem.at[me, c],
                    device_id={axis: targets[way]},
                    device_id_type=MESH,
                ).start()

    for d in range(1, Z):
        for c in range(NC):
            for way, here in ((0, z - d >= 0), (1, z + d < Z)):

                @pl.when(here)
                def _(way=way, c=c, d=d):
                    origin = (z - d if way == 0 else z + d) * X + x
                    copy(way, origin, c).wait_recv()
                    for onward in (way, 2, 3):

                        @pl.when(exists[onward])
                        def _(onward=onward):
                            copy(onward, origin, c).start()

    for e in range(1, X):
        for dz in range(Z):
            level = lax.rem(z + dz, Z)
            for c in range(NC):
                for way, here in ((2, x - e >= 0), (3, x + e < X)):

                    @pl.when(here)
                    def _(way=way, c=c, e=e, level=level):
                        origin = level * X + (x - e if way == 2 else x + e)
                        copy(way, origin, c).wait_recv()

                        @pl.when(exists[way])
                        def _():
                            copy(way, origin, c).start()

    own.wait()
    for c in range(NC):
        for zz in range(Z):
            for way, here in ((0, zz <= z), (1, zz >= z)):

                @pl.when(exists[way] & here)
                def _(way=way, zz=zz, c=c):
                    copy(way, zz * X + x, c).wait_send()

            for xx in range(X):
                for way, here in ((2, xx <= x), (3, xx >= x)):

                    @pl.when(exists[way] & here)
                    def _(way=way, zz=zz, xx=xx, c=c):
                        copy(way, zz * X + xx, c).wait_send()


def gather_rows(block, axis, ident, chunks=4):
    Z, X = grid_of(axis)
    shards = Z * X
    rows, width = block.shape
    return pl.pallas_call(
        functools.partial(gather_kernel, axis, Z, X, chunks),
        out_shape=jax.ShapeDtypeStruct((shards, rows, width), block.dtype),
        in_specs=[pl.BlockSpec(memory_space=pl.ANY)],
        out_specs=pl.BlockSpec(memory_space=pl.ANY),
        scratch_shapes=[
            pltpu.SemaphoreType.DMA,
            pltpu.SemaphoreType.DMA((4, shards, chunks)),
            pltpu.SemaphoreType.DMA((shards, chunks)),
        ],
        compiler_params=pltpu.CompilerParams(
            collective_id=ident, has_side_effects=True
        ),
    )(block)


def scatter_kernel(axis, Z, X, NC, p_ref, out_ref, mine, from_x, from_z, load_sem, xs_sem, xr_sem, zs_sem, zr_sem):
    me = lax.axis_index(axis)
    z, x = lax.div(me, X), lax.rem(me, X)
    rows = p_ref.shape[1] // NC
    step = 16
    targets, exists = line_neighbours(z, x, Z, X)

    def load(slot):
        return pltpu.make_async_copy(p_ref.at[slot], mine.at[slot], load_sem.at[slot])

    for slot in range(Z * X):
        load(slot).start()
    greet(axis, targets, exists)

    def x_copy(up, zz, xx, c):
        part = pl.ds(c * rows, rows)
        spot = xx if up else jnp.where(xx == x - 1, X, xx)
        spot = zz * (X + 1) + spot
        return pltpu.make_async_remote_copy(
            src_ref=mine.at[zz * X + xx, part],
            dst_ref=from_x.at[spot, part],
            send_sem=xs_sem.at[zz * X + xx, c],
            recv_sem=xr_sem.at[spot, c],
            device_id={axis: targets[2 if up else 3]},
            device_id_type=MESH,
        )

    def z_copy(up, zz, c):
        part = pl.ds(c * rows, rows)
        spot = zz if up else jnp.where(zz == z - 1, Z, zz)
        return pltpu.make_async_remote_copy(
            src_ref=mine.at[zz * X + x, part],
            dst_ref=from_z.at[spot, part],
            send_sem=zs_sem.at[zz, c],
            recv_sem=zr_sem.at[spot, c],
            device_id={axis: targets[0 if up else 1]},
            device_id_type=MESH,
        )

    def wait_in(buffer, sem, spot, c):
        part = pl.ds(c * rows, rows)
        pltpu.make_async_copy(buffer.at[spot, part], buffer.at[spot, part], sem.at[spot, c]).wait()

    def add_in(slot, buffer, spot, c):
        def body(i, carry):
            part = pl.ds(pl.multiple_of(c * rows + i * step, step), step)
            mine[slot, part] = (
                mine[slot, part].astype(jnp.float32) + buffer[spot, part].astype(jnp.float32)
            ).astype(mine.dtype)
            return carry

        lax.fori_loop(0, rows // step, body, 0)

    def x_line(zz):
        for k in range(X - 1):
            for up, xx, here in ((True, X - 1 - k, X - 1 - k > x), (False, k, k < x)):

                @pl.when(here)
                def _(up=up, xx=xx):
                    load(zz * X + xx).wait()
                    for c in range(NC):

                        @pl.when(exists[3 if up else 2])
                        def _(c=c):
                            spot = zz * (X + 1) + xx
                            wait_in(from_x, xr_sem, spot, c)
                            add_in(zz * X + xx, from_x, spot, c)

                        x_copy(up, zz, xx, c).start()

    def x_join(zz, c):
        if X == 1:
            return
        slot = zz * X + x

        @pl.when(x > 0)
        def _():
            wait_in(from_x, xr_sem, zz * (X + 1) + x, c)
            add_in(slot, from_x, zz * (X + 1) + x, c)

        @pl.when(x < X - 1)
        def _():
            wait_in(from_x, xr_sem, zz * (X + 1) + X, c)
            add_in(slot, from_x, zz * (X + 1) + X, c)

    def in_order(visit):
        for k in range(Z - 1):
            for up, zz, here in ((True, Z - 1 - k, Z - 1 - k > z), (False, k, k < z)):

                @pl.when(here)
                def _(up=up, zz=zz):
                    visit(up, zz)

    in_order(lambda up, zz: x_line(zz))
    x_line(z)

    for k in range(Z - 1):
        for up, zz, here in ((True, Z - 1 - k, Z - 1 - k > z), (False, k, k < z)):

            @pl.when(here)
            def _(up=up, zz=zz):
                load(zz * X + x).wait()

        for c in range(NC):
            for up, zz, here in ((True, Z - 1 - k, Z - 1 - k > z), (False, k, k < z)):

                @pl.when(here)
                def _(up=up, zz=zz, c=c):
                    x_join(zz, c)

                    @pl.when(exists[1 if up else 0])
                    def _():
                        wait_in(from_z, zr_sem, zz, c)
                        add_in(zz * X + x, from_z, zz, c)

                    z_copy(up, zz, c).start()

    load(me).wait()
    for c in range(NC):
        x_join(z, c)

        @pl.when(z > 0)
        def _(c=c):
            wait_in(from_z, zr_sem, z, c)

        @pl.when(z < Z - 1)
        def _(c=c):
            wait_in(from_z, zr_sem, Z, c)

        def body(i, carry, c=c):
            part = pl.ds(pl.multiple_of(c * rows + i * step, step), step)
            total = mine[me, part].astype(jnp.float32)
            below = from_z[z, part].astype(jnp.float32)
            above = from_z[Z, part].astype(jnp.float32)
            total = total + jnp.where(z > 0, below, 0.0)
            total = total + jnp.where(z < Z - 1, above, 0.0)
            out_ref[part] = total.astype(out_ref.dtype)
            return carry

        lax.fori_loop(0, rows // step, body, 0)

    for zz in range(Z):
        for c in range(NC):
            for xx in range(X):

                @pl.when(xx != x)
                def _(zz=zz, xx=xx, c=c):
                    x_copy(True, zz, xx, c).wait_send()

            @pl.when(zz != z)
            def _(zz=zz, c=c):
                z_copy(True, zz, c).wait_send()


def scatter_rows(partial, axis, ident, chunks=4, dtype=jnp.float32):
    Z, X = grid_of(axis)
    shards = Z * X
    rows, width = partial.shape[0] // shards, partial.shape[1]
    kind = partial.dtype
    return pl.pallas_call(
        functools.partial(scatter_kernel, axis, Z, X, chunks),
        out_shape=jax.ShapeDtypeStruct((rows, width), dtype),
        in_specs=[pl.BlockSpec(memory_space=pl.ANY)],
        out_specs=pl.BlockSpec(memory_space=pltpu.VMEM),
        scratch_shapes=[
            pltpu.VMEM((shards, rows, width), kind),
            pltpu.VMEM((Z * (X + 1), rows, width), kind),
            pltpu.VMEM((Z + 1, rows, width), kind),
            pltpu.SemaphoreType.DMA((shards,)),
            pltpu.SemaphoreType.DMA((shards, chunks)),
            pltpu.SemaphoreType.DMA((Z * (X + 1), chunks)),
            pltpu.SemaphoreType.DMA((Z, chunks)),
            pltpu.SemaphoreType.DMA((Z + 1, chunks)),
        ],
        compiler_params=pltpu.CompilerParams(
            collective_id=ident, has_side_effects=True, vmem_limit_bytes=60 * 1024 * 1024
        ),
    )(partial.reshape(shards, rows, width))


HD = 128


def dot_nn(a, b):
    return lax.dot_general(
        a.astype(jnp.bfloat16), b.astype(jnp.bfloat16), (((1,), (0,)), ((), ())),
        preferred_element_type=jnp.float32,
    )


def dot_nt(a, b):
    return lax.dot_general(
        a.astype(jnp.bfloat16), b.astype(jnp.bfloat16), (((1,), (1,)), ((), ())),
        preferred_element_type=jnp.float32,
    )


def dot_tn(a, b):
    return lax.dot_general(
        a.astype(jnp.bfloat16), b.astype(jnp.bfloat16), (((0,), (0,)), ((), ())),
        preferred_element_type=jnp.float32,
    )


def split2(a):
    high = a.astype(jnp.bfloat16)
    return high, (a - high.astype(jnp.float32)).astype(jnp.bfloat16)


def fine(dot, a, b):
    a_high, a_low = split2(a)
    b_high, b_low = split2(b)
    return dot(a_high, b_high) + (dot(a_high, b_low) + dot(a_low, b_high))


def time_of(shape, dim, lanes):
    index = lax.broadcasted_iota(jnp.int32, shape, dim)
    return lax.rem(index, 8) * lanes + lax.div(index, 8)


def lower_inverse(a, lanes):
    size = a.shape[0]
    row_t = time_of((size, size), 0, lanes)
    col_t = time_of((size, size), 1, lanes)
    eye = jnp.where(row_t == col_t, 1.0, 0.0)

    def same(width):
        return lax.div(row_t, width) == lax.div(col_t, width)

    first = jnp.where(same(8), a, 0.0)
    second = fine(dot_nn, first, first)
    inverse = eye + first + second + fine(dot_nn, first, second)
    inverse = inverse + fine(dot_nn, inverse, fine(dot_nn, second, second))
    width = 16
    while width <= size:
        joint = jnp.where(same(width) & jnp.logical_not(same(width // 2)), a, 0.0)
        inverse = inverse + fine(dot_nn, fine(dot_nn, inverse, joint), inverse)
        width *= 2
    return inverse


def delta_forward(lanes, heads, group, q_ref, k_ref, v_ref, b_ref, low_ref, c_ref, m_ref,
                  o_ref, s_ref, t_ref, mk_ref, mv_ref, u_ref, state):
    size = lanes * 8
    scale = HD ** (-0.5)

    @pl.when(pl.program_id(0) == 0)
    def _():
        state[...] = jnp.zeros_like(state)

    row_t = time_of((size, size), 0, lanes)
    col_t = time_of((size, size), 1, lanes)
    ready = {}
    for g in range(group):
        rows = pl.ds(g * 8, 8)
        low = low_ref[g]
        strict = jnp.where(row_t == col_t, 0.0, low)
        for h in range(heads):
            cols = pl.ds(h * HD, HD)

            def take(ref):
                return ref[:, rows, cols].reshape(size, HD)

            k, q, v, beta = take(k_ref), take(q_ref), take(v_ref), take(b_ref)
            kb = beta * k
            a = -strict * fine(dot_nt, kb, k)
            inverse = lower_inverse(a, lanes)
            mk = fine(dot_nn, inverse, kb)
            mv = fine(dot_nn, inverse, beta * v)
            scores = low * dot_nt(q, k)
            t_ref[g, h] = inverse
            mk_ref[g, h] = mk.astype(mk_ref.dtype)
            mv_ref[g, h] = mv.astype(mv_ref.dtype)
            ready[g, h] = (q, k, mk, mv, scores)
    for g in range(group):
        rows = pl.ds(g * 8, 8)
        carry = c_ref[:, rows].reshape(size, HD)
        keep = m_ref[:, rows].reshape(size, HD)
        for h in range(heads):
            q, k, mk, mv, scores = ready[g, h]
            held = state[h]
            s_ref[g, h] = held
            u = mv - carry * dot_nn(mk, held)
            u_ref[g, h] = u.astype(u_ref.dtype)
            state[h] = (carry[0:1] * keep[0:1]) * held + dot_tn(k, keep * u)
            out = (carry * dot_nn(q, held) + dot_nn(scores, u)) * scale
            o_ref[:, rows, pl.ds(h * HD, HD)] = out.reshape(lanes, 8, HD).astype(o_ref.dtype)


def delta_backward(lanes, heads, group, q_ref, k_ref, v_ref, b_ref, low_ref, c_ref, m_ref, do_ref,
                   s_ref, t_ref, mk_ref, mv_ref, u_ref,
                   dq_ref, dk_ref, dv_ref, db_ref, state):
    size = lanes * 8
    scale = HD ** (-0.5)

    @pl.when(pl.program_id(0) == 0)
    def _():
        state[...] = jnp.zeros_like(state)

    row_t = time_of((size, size), 0, lanes)
    col_t = time_of((size, size), 1, lanes)
    ready = {}
    for g in range(group):
        rows = pl.ds(g * 8, 8)
        low = low_ref[g]
        carry = c_ref[:, rows].reshape(size, HD)
        for h in range(heads):
            cols = pl.ds(h * HD, HD)

            def take(ref):
                return ref[:, rows, cols].reshape(size, HD)

            k, q = take(k_ref), take(q_ref)
            do = take(do_ref).astype(jnp.float32) * scale
            held = s_ref[g, h]
            u = u_ref[g, h]
            scores = low * dot_nt(q, k)
            du = dot_tn(scores, do)
            ds = low * dot_nt(do, u)
            cdo = carry * do
            dq = dot_nt(cdo, held) + dot_nn(ds, k)
            dk = dot_tn(ds, q)
            gain = dot_tn(q, cdo)
            dq_ref[:, rows, cols] = dq.reshape(lanes, 8, HD)
            ready[g, h] = (k, du, dk, gain)
    after = {}
    for g in reversed(range(group)):
        rows = pl.ds(g * 8, 8)
        carry = c_ref[:, rows].reshape(size, HD)
        keep = m_ref[:, rows].reshape(size, HD)
        for h in range(heads):
            k, du, dk, gain = ready[g, h]
            later = state[h]
            du = du + keep * dot_nn(k, later)
            state[h] = (carry[0:1] * keep[0:1]) * later + gain - dot_tn(carry * mk_ref[g, h].astype(jnp.float32), du)
            after[g, h] = (du, later)
    for g in range(group):
        rows = pl.ds(g * 8, 8)
        low = low_ref[g]
        strict = jnp.where(row_t == col_t, 0.0, low)
        carry = c_ref[:, rows].reshape(size, HD)
        keep = m_ref[:, rows].reshape(size, HD)
        for h in range(heads):
            cols = pl.ds(h * HD, HD)

            def take(ref):
                return ref[:, rows, cols].reshape(size, HD)

            k, du, dk, gain = ready[g, h]
            v, beta = take(v_ref), take(b_ref)
            du, later = after[g, h]
            u = u_ref[g, h].astype(jnp.float32)
            inverse = t_ref[g, h]
            dk = dk + dot_nt(keep * u, later)
            dmk = -carry * dot_nt(du, s_ref[g, h])
            xx = dot_tn(inverse, dmk)
            yy = dot_tn(inverse, du)
            da = strict * (dot_nt(xx, mk_ref[g, h]) + dot_nt(yy, mv_ref[g, h]))
            dkb = xx - dot_nn(da, k)
            dk = dk - dot_tn(da, beta * k) + beta * dkb
            dk_ref[:, rows, cols] = dk.reshape(lanes, 8, HD)
            dv_ref[:, rows, cols] = (beta * yy).reshape(lanes, 8, HD)
            db = jnp.sum(dkb * k + yy * v, axis=1, keepdims=True)
            db_ref[:, rows, cols] = jnp.broadcast_to(db, (size, HD)).reshape(lanes, 8, HD)


def block_specs(lanes, heads, group, flip):
    size = lanes * 8
    wide = heads * HD
    at = (lambda i: flip - 1 - i) if flip else (lambda i: i)
    token = pl.BlockSpec((lanes, 8 * group, wide), lambda i: (0, at(i), 0))
    flag = pl.BlockSpec((lanes, 8 * group, HD), lambda i: (0, at(i), 0))
    square = pl.BlockSpec((group, size, size), lambda i: (at(i), 0, 0))
    held = pl.BlockSpec((group, heads, HD, HD), lambda i: (at(i), 0, 0, 0))
    tri = pl.BlockSpec((group, heads, size, size), lambda i: (at(i), 0, 0, 0))
    rows = pl.BlockSpec((group, heads, size, HD), lambda i: (at(i), 0, 0, 0))
    return token, flag, square, held, tri, rows


def mixer_forward(q, k, v, beta, low, carry, keep, group=4):
    lanes, tokens, wide = q.shape
    heads, blocks, size = wide // HD, tokens // 8, lanes * 8
    token, flag, square, held, tri, rows = block_specs(lanes, heads, group, 0)
    row_shape = jax.ShapeDtypeStruct((blocks, heads, size, HD), jnp.bfloat16)
    return pl.pallas_call(
        functools.partial(delta_forward, lanes, heads, group),
        grid=(blocks // group,),
        in_specs=[token, token, token, token, square, flag, flag],
        out_specs=[token, held, tri, rows, rows, rows],
        out_shape=[
            jax.ShapeDtypeStruct((lanes, tokens, wide), jnp.float32),
            jax.ShapeDtypeStruct((blocks, heads, HD, HD), jnp.float32),
            jax.ShapeDtypeStruct((blocks, heads, size, size), jnp.float32),
            row_shape, row_shape, row_shape,
        ],
        scratch_shapes=[pltpu.VMEM((heads, HD, HD), jnp.float32)],
        compiler_params=pltpu.CompilerParams(vmem_limit_bytes=48 * 1024 * 1024),
    )(q, k, v, beta, low, carry, keep)


def mixer_backward(q, k, v, beta, low, carry, keep, d_out, saved, group=4):
    lanes, tokens, wide = q.shape
    heads, blocks, size = wide // HD, tokens // 8, lanes * 8
    token, flag, square, held, tri, rows = block_specs(lanes, heads, group, blocks // group)
    shape = jax.ShapeDtypeStruct((lanes, tokens, wide), jnp.float32)
    return pl.pallas_call(
        functools.partial(delta_backward, lanes, heads, group),
        grid=(blocks // group,),
        in_specs=[token, token, token, token, square, flag, flag, token, held, tri, rows, rows, rows],
        out_specs=[token] * 4,
        out_shape=[shape] * 4,
        scratch_shapes=[pltpu.VMEM((heads, HD, HD), jnp.float32)],
        compiler_params=pltpu.CompilerParams(vmem_limit_bytes=48 * 1024 * 1024),
    )(q, k, v, beta, low, carry, keep, d_out, *saved)


def segment_masks(lengths_grid, order_row, lanes, tokens):
    slots = order_row.shape[0]
    flat = lengths_grid.reshape(slots)
    match = order_row[:, None] == lax.broadcasted_iota(jnp.int32, (slots, slots), 1)
    run_len = jnp.sum(jnp.where(match, flat[None, :], 0), axis=1)
    upto = lax.broadcasted_iota(jnp.int32, (slots, slots), 0) >= lax.broadcasted_iota(jnp.int32, (slots, slots), 1)
    ends = jnp.sum(jnp.where(upto, run_len[None, :], 0), axis=1)
    starts = ends - run_len
    size = lanes * 8
    blocks = tokens // 8
    lane = lax.broadcasted_iota(jnp.int32, (lanes, tokens), 0)
    step = lax.broadcasted_iota(jnp.int32, (lanes, tokens), 1)
    place = step * lanes + lane
    inside = (starts[:, None, None] <= place[None]) & (place[None] < ends[:, None, None])
    start_at = jnp.sum(jnp.where(inside, starts[:, None, None], 0), axis=0)
    end_at = jnp.sum(jnp.where(inside, ends[:, None, None], 0), axis=0)
    block = step // 8
    carry = (start_at < block * size).astype(jnp.float32)
    keep = (end_at >= (block + 1) * size).astype(jnp.float32)

    def blocked(values):
        return values.reshape(lanes, blocks, 8).transpose(1, 0, 2).reshape(blocks, size)

    start_b, place_b = blocked(start_at), blocked(place)
    low = (start_b[:, :, None] == start_b[:, None, :]) & (place_b[:, :, None] >= place_b[:, None, :])
    offset = place - start_at
    wide = (lanes, tokens, HD)
    return (
        low.astype(jnp.float32),
        jnp.broadcast_to(carry[:, :, None], wide),
        jnp.broadcast_to(keep[:, :, None], wide),
        offset,
    )


def back_in_stream(values, hops):
    lanes, tokens, wide = values.shape
    moved = jnp.pad(values[lanes - hops :, : tokens - 1], ((0, 0), (1, 0), (0, 0)))
    return jnp.concatenate([moved, values[: lanes - hops]], axis=0)


def ahead_in_stream(values, hops):
    moved = jnp.pad(values[:hops, 1:], ((0, 0), (0, 1), (0, 0)))
    return jnp.concatenate([values[hops:], moved], axis=0)


def conv_sums(signal, taps, offset):
    total = signal * taps[0]
    for hop in range(1, taps.shape[0]):
        moved = jnp.where((offset >= hop)[:, :, None], back_in_stream(signal, hop), 0.0)
        total = total + moved * taps[hop]
    return total


def conv_back(err, signal, taps, offset):
    d_signal = err * taps[0]
    d_taps = [jnp.sum(err * signal, axis=(0, 1))]
    for hop in range(1, taps.shape[0]):
        live = jnp.where((offset >= hop)[:, :, None], err, 0.0)
        d_taps.append(jnp.sum(live * back_in_stream(signal, hop), axis=(0, 1)))
        d_signal = d_signal + ahead_in_stream(live, hop) * taps[hop]
    return d_signal, jnp.stack(d_taps)


def unit_heads(pre):
    lanes, tokens, wide = pre.shape
    split = pre.reshape(lanes, tokens, wide // HD, HD)
    inverse = lax.rsqrt(jnp.sum(split * split, axis=-1, keepdims=True) + 1e-6)
    return (split * inverse).reshape(pre.shape)


def unit_back(pre, grad):
    lanes, tokens, wide = pre.shape
    split = pre.reshape(lanes, tokens, wide // HD, HD)
    g = grad.reshape(split.shape)
    inverse = lax.rsqrt(jnp.sum(split * split, axis=-1, keepdims=True) + 1e-6)
    inner = jnp.sum(split * g, axis=-1, keepdims=True)
    return (inverse * g - split * (inverse * inverse * inverse) * inner).reshape(pre.shape)


def silu_slope(total):
    s = jax.nn.sigmoid(total)
    return s * (1.0 + total * (1.0 - s))


def prepare(q0, k0, v0, logits, taps, offset):
    sums = [conv_sums(signal, tap, offset) for signal, tap in zip((q0, k0, v0), taps)]
    pre = [jax.nn.silu(t) for t in sums]
    lanes, tokens, heads = logits.shape
    strength = jax.nn.sigmoid(logits)
    beta = jnp.broadcast_to(strength[..., None], (lanes, tokens, heads, HD)).reshape(lanes, tokens, heads * HD)
    return unit_heads(pre[0]), unit_heads(pre[1]), pre[2], beta


def unprepare(q0, k0, v0, logits, taps, offset, dq, dk, dv, db):
    signals = (q0, k0, v0)
    sums = [conv_sums(signal, tap, offset) for signal, tap in zip(signals, taps)]
    pre = [jax.nn.silu(t) for t in sums]
    grads = (unit_back(pre[0], dq), unit_back(pre[1], dk), dv)
    errs = [g * silu_slope(t) for g, t in zip(grads, sums)]
    backs = [conv_back(e, signal, tap, offset) for e, signal, tap in zip(errs, signals, taps)]
    lanes, tokens, heads = logits.shape
    strength = jax.nn.sigmoid(logits)
    d_strength = db.reshape(lanes, tokens, heads, HD)[..., 0]
    d_logits = d_strength * strength * (1.0 - strength)
    return [b[0] for b in backs], d_logits, [b[1] for b in backs]


def project(left_side, right_side):
    return jnp.dot(left_side, right_side, preferred_element_type=jnp.float32)


def times_t(left_side, right_side):
    return lax.dot_general(
        left_side, right_side, (((1,), (1,)), ((), ())), preferred_element_type=jnp.float32
    )


def contract_rows(left_side, right_side):
    return lax.dot_general(
        left_side, right_side, (((0,), (0,)), ((), ())), preferred_element_type=jnp.float32
    )


def rms(values, gain, eps):
    return values * lax.rsqrt(jnp.mean(values * values, axis=-1, keepdims=True) + eps) * gain


def rms_back(values, gain, eps, grad):
    r = lax.rsqrt(jnp.mean(values * values, axis=-1, keepdims=True) + eps)
    inner = jnp.mean(values * gain * grad, axis=-1, keepdims=True)
    return r * gain * grad - values * (r * r * r) * inner, grad * values * r


def heads_of(values):
    return values.reshape(values.shape[0], -1, HD)


def deal(stacked):
    return lax.all_to_all(stacked, "shard", split_axis=0, concat_axis=0, tiled=True)


def body(
    layer_input,
    out_cotangent,
    seq_lengths,
    seq_order,
    w_query,
    w_key,
    w_value,
    w_beta,
    w_outgate,
    w_output,
    conv_query,
    conv_key,
    conv_value,
    attn_gain,
    head_gain,
    mlp_gain,
    w_gate,
    w_up,
    w_down,
):
    bf16, f32 = jnp.bfloat16, jnp.float32
    shards, replicas = lax.axis_size("shard"), lax.axis_size("replica")
    rows, width = layer_input.shape
    tokens = shards * rows
    own = w_output.shape[0]
    heads = own // HD
    hidden_own = w_down.shape[0]
    ffn = w_gate.shape[1]

    def by_columns(weight):
        return weight.reshape(weight.shape[0], shards, -1).transpose(1, 0, 2)

    attn_weights = jnp.concatenate(
        [by_columns(w) for w in (w_query, w_key, w_value, w_outgate)]
        + [jnp.pad(by_columns(w_beta), ((0, 0), (0, 0), (0, HD - heads)))],
        axis=2,
    )
    attn_weights = deal(attn_weights).reshape(width, -1)
    mlp_weights = deal(jnp.concatenate([by_columns(w_gate), by_columns(w_up)], axis=2))
    mlp_weights = mlp_weights.reshape(width, -1)
    gains = lax.all_gather(jnp.stack([attn_gain, mlp_gain]), "shard", axis=1, tiled=True).astype(f32)
    full_attn_gain, full_mlp_gain = gains[0], gains[1]
    full_head_gain = lax.all_gather(head_gain, "shard", axis=0, tiled=True).astype(f32)
    low, carry, keep, offset = segment_masks(seq_lengths[0], seq_order[0], shards, rows)

    source = layer_input.astype(f32)
    all_source = gather_rows(layer_input, "shard", 0).reshape(tokens, width)
    normed = rms(all_source.astype(f32), full_attn_gain, 1e-6).astype(bf16)
    projected = project(normed, attn_weights)

    def stream(values):
        return values.astype(bf16).astype(f32).reshape(shards, rows, -1)

    query0 = stream(projected[:, :own])
    key0 = stream(projected[:, own : 2 * own])
    value0 = stream(projected[:, 2 * own : 3 * own])
    gate = projected[:, 3 * own : 4 * own]
    logits = stream(projected[:, 4 * own : 4 * own + heads])
    taps = [t.astype(f32) for t in (conv_query, conv_key, conv_value)]
    q, k, v, beta = prepare(query0, key0, value0, logits, taps, offset)
    mixed, *saved = mixer_forward(q, k, v, beta, low, carry, keep)
    mixed = mixed.astype(bf16).astype(f32).reshape(tokens, heads, HD)
    gate_heads = heads_of(gate)
    head_normed = rms(mixed, full_head_gain, 1e-5)
    zed = (head_normed * jax.nn.silu(gate_heads)).astype(bf16).reshape(tokens, own)
    hidden = source + scatter_rows(project(zed, w_output).astype(bf16), "shard", 1)

    mlp_in = gather_rows(rms(hidden, full_mlp_gain, 1e-6).astype(bf16), "shard", 2)
    mlp_in = mlp_in.reshape(tokens, width)
    lin = project(mlp_in, mlp_weights)
    gate_lin, up_lin = lin[:, :hidden_own], lin[:, hidden_own:]
    s = jax.nn.sigmoid(gate_lin)
    product = (gate_lin * s * up_lin).astype(bf16)
    layer_output = hidden + scatter_rows(project(product, w_down).astype(bf16), "shard", 3)

    dy = gather_rows(out_cotangent, "shard", 4).reshape(tokens, width)
    d_product = times_t(dy, w_down)
    d_gate = (d_product * up_lin * s * (1.0 + gate_lin * (1.0 - s))).astype(bf16)
    d_up = (d_product * gate_lin * s).astype(bf16)
    d_lin = jnp.concatenate([d_gate, d_up], axis=1)
    d_mlp_in = scatter_rows(times_t(d_lin, mlp_weights).astype(bf16), "shard", 5)
    d_hidden_norm, g_mlp_rows = rms_back(hidden, full_mlp_gain, 1e-6, d_mlp_in)
    d_hidden = out_cotangent.astype(f32) + d_hidden_norm
    g_down = contract_rows(product, dy)
    g_lin = contract_rows(mlp_in, d_lin)

    d_attn = gather_rows(d_hidden.astype(bf16), "shard", 6).reshape(tokens, width)
    g_output = contract_rows(zed, d_attn)
    d_zed = heads_of(times_t(d_attn, w_output))
    d_mixed, g_head_rows = rms_back(mixed, full_head_gain, 1e-5, d_zed * jax.nn.silu(gate_heads))
    d_gate_pre = (d_zed * head_normed * silu_slope(gate_heads)).astype(bf16).reshape(tokens, own)
    d_mixed = d_mixed.astype(bf16).astype(f32).reshape(shards, rows, own)
    d_all = mixer_backward(q, k, v, beta, low, carry, keep, d_mixed, saved)
    signals, d_logits, g_taps = unprepare(query0, key0, value0, logits, taps, offset, *d_all)
    d_logits = jnp.pad(d_logits.reshape(tokens, heads), ((0, 0), (0, HD - heads)))
    d_proj = jnp.concatenate(
        [d.reshape(tokens, own).astype(bf16) for d in signals] + [d_gate_pre, d_logits.astype(bf16)],
        axis=1,
    )
    d_normed = scatter_rows(times_t(d_proj, attn_weights).astype(bf16), "shard", 7)
    d_source, g_attn_rows = rms_back(source, full_attn_gain, 1e-6, d_normed)
    input_grad = (d_hidden + d_source).astype(bf16)
    g_proj = contract_rows(normed, d_proj)

    part = width // shards // replicas
    split_grads = jnp.concatenate([g_proj, g_lin], axis=1).astype(bf16)
    wide = split_grads.shape[1]
    split_grads = split_grads.reshape(shards, replicas, part, wide).transpose(1, 0, 2, 3)
    split_grads = scatter_rows(split_grads.reshape(-1, wide), "replica", 8, 4, bf16)
    split_grads = deal(split_grads.reshape(shards, part, wide)).reshape(-1, wide)
    split_grads = gather_rows(split_grads, "replica", 9, 4).reshape(replicas, shards, part, wide)

    def assemble(first, count):
        taken = split_grads[..., first : first + count].transpose(0, 2, 1, 3)
        return taken.reshape(replicas * part, shards * count).astype(f32)

    lone = jnp.concatenate([g_output, g_down], axis=0).astype(bf16)
    fill = -lone.shape[0] % (replicas * 16)
    lone = jnp.pad(lone, ((0, fill), (0, 0)))
    lone = gather_rows(scatter_rows(lone, "replica", 10, 1, bf16), "replica", 11, 1)
    lone = lone.reshape(-1, width).astype(f32)

    def small(values):
        total = lax.psum(values.astype(f32), ("replica", "shard"))
        count = total.shape[0] // shards
        return lax.dynamic_slice_in_dim(total, lax.axis_index("shard") * count, count)

    g_taps = lax.psum(jnp.stack(g_taps), "replica")
    return (
        layer_output.astype(bf16),
        input_grad,
        assemble(0, own),
        assemble(own, own),
        assemble(2 * own, own),
        assemble(4 * own, heads),
        assemble(3 * own, own),
        lone[:own],
        g_taps[0],
        g_taps[1],
        g_taps[2],
        small(jnp.sum(g_attn_rows, axis=0)),
        small(jnp.sum(g_head_rows, axis=(0, 1))),
        small(jnp.sum(g_mlp_rows, axis=0)),
        assemble(4 * own + HD, hidden_own),
        assemble(4 * own + HD + hidden_own, hidden_own),
        lone[own : own + hidden_own],
    )


def solution(mesh):
    tokens = P(("replica", "shard"), None)
    whole, columns, vector = P("shard", None), P(None, "shard"), P("shard")
    in_specs = (tokens, tokens, P("replica", None, None), P("replica", None)) + (whole,) * 6
    in_specs += (columns,) * 3 + (vector,) * 3 + (whole,) * 3
    out_specs = (tokens, tokens) + (whole,) * 6 + (columns,) * 3 + (vector,) * 3 + (whole,) * 3
    return jax.shard_map(body, mesh=mesh, in_specs=in_specs, out_specs=out_specs, check_vma=False)
```

```python
import functools

import jax
import jax.numpy as jnp
from jax import lax
from jax.experimental import pallas as pl
from jax.experimental.pallas import tpu as pltpu
from jax.sharding import PartitionSpec as P

MESH = pl.DeviceIdType.MESH
ANY = pl.BlockSpec(memory_space=pl.ANY)
VMEM = pl.BlockSpec(memory_space=pltpu.VMEM)
DMA = pltpu.SemaphoreType.DMA
UP, DOWN, RIGHT, LEFT = range(4)


def grid_of(axis):
    count = lax.axis_size(axis)
    if axis == "replica":
        across = 2 if count % 2 == 0 else 1
        return count // across, across
    depth = 4 if count % 4 == 0 else count
    return depth, count // depth


class Lines:
    def __init__(self, axis):
        self.axis = axis
        self.Z, self.X = grid_of(axis)
        self.count = self.Z * self.X
        self.me = lax.axis_index(axis)
        self.z, self.x = lax.div(self.me, self.X), lax.rem(self.me, self.X)
        z, x, X = self.z, self.x, self.X
        self.targets = ((z + 1) * X + x, (z - 1) * X + x, z * X + x + 1, z * X + x - 1)
        self.exists = (z < self.Z - 1, z > 0, x < X - 1, x > 0)

    def to(self, way):
        return {self.axis: self.targets[way]}

    def other(self, k):
        return lax.rem(self.me + k, self.count)


def greet(lines, everyone):
    barrier = pltpu.get_barrier_semaphore()
    count = jnp.int32(0)
    for line in lines:
        if line.axis in everyone:
            for k in range(1, line.count):
                pl.semaphore_signal(
                    barrier, inc=1, device_id={line.axis: line.other(k)}, device_id_type=MESH
                )
            count = count + (line.count - 1)
            continue
        for way in range(4):

            @pl.when(line.exists[way])
            def _(line=line, way=way):
                pl.semaphore_signal(barrier, inc=1, device_id=line.to(way), device_id_type=MESH)

            count = count + jnp.where(line.exists[way], 1, 0)
    pl.semaphore_wait(barrier, count)


def remote(src, dst, send_sem, recv_sem, device):
    return pltpu.make_async_remote_copy(
        src_ref=src,
        dst_ref=dst,
        send_sem=send_sem,
        recv_sem=recv_sem,
        device_id=device,
        device_id_type=MESH,
    )


def in_place(view, sem):
    return pltpu.make_async_copy(view, view, sem)


def gather_sems(axis, chunks):
    Z, X = grid_of(axis)
    return [DMA((4, Z * X, chunks)), DMA((Z * X, chunks))]


def gather_steps(line, chunks, view, source, ready, sems, start, pace):
    send_sem, recv_sem = sems
    Z, X, z, x, me = line.Z, line.X, line.z, line.x, line.me
    exists = line.exists

    def copy(way, origin, c, src=None):
        spot = view(origin, c)
        return remote(
            spot if src is None else src,
            spot,
            send_sem.at[way, origin, c],
            recv_sem.at[origin, c],
            line.to(way),
        )

    def first(c):
        ready(c)
        for way in range(4):

            @pl.when(exists[way])
            def _(way=way):
                copy(way, me, c, source(c)).start()

    def hop(d, c):
        for way, here in ((UP, z - d >= 0), (DOWN, z + d < Z)):

            @pl.when(here)
            def _(way=way):
                origin = (z - d if way == UP else z + d) * X + x
                copy(way, origin, c).wait_recv()
                for onward in (way, RIGHT, LEFT):

                    @pl.when(exists[onward])
                    def _(onward=onward):
                        copy(onward, origin, c).start()

    def across(e, level, c):
        for way, here in ((RIGHT, x - e >= 0), (LEFT, x + e < X)):

            @pl.when(here)
            def _(way=way):
                origin = level * X + (x - e if way == RIGHT else x + e)
                copy(way, origin, c).wait_recv()
                if X > 2:

                    @pl.when(exists[way])
                    def _():
                        copy(way, origin, c).start()

    def finish():
        for c in range(chunks):
            for zz in range(Z):
                for way, here in ((UP, zz <= z), (DOWN, zz >= z)):

                    @pl.when(exists[way] & here)
                    def _(way=way, zz=zz, c=c):
                        copy(way, zz * X + x, c).wait_send()

                for xx in range(X):
                    for way, here in ((RIGHT, xx <= x), (LEFT, xx >= x)):

                        @pl.when(exists[way] & here)
                        def _(way=way, zz=zz, xx=xx, c=c):
                            copy(way, zz * X + xx, c).wait_send()

    steps = []
    for c in range(chunks):
        steps.append((start + pace * c / chunks, functools.partial(first, c)))
    for d in range(1, Z):
        for c in range(chunks):
            steps.append((start + pace * (d + (c + 1) / chunks), functools.partial(hop, d, c)))
    for e in range(1, X):
        for dz in range(Z):
            level = lax.rem(z + dz, Z)
            for c in range(chunks):
                when = start + pace * (Z + e + (dz * chunks + c) / (Z * chunks))
                steps.append((when, functools.partial(across, e, level, c)))
    steps.append((start + pace * (Z + X + 1), finish))
    return steps


def scatter_slots(axis):
    Z, X = grid_of(axis)
    if X <= 2:
        return Z, Z
    return Z * X, Z * (X + 1)


def scatter_scratch(axis, chunks, rows, width, kind):
    Z, X = grid_of(axis)
    held, across = scatter_slots(axis)
    return [
        pltpu.VMEM((held, chunks, rows, width), kind),
        pltpu.VMEM((across, chunks, rows, width), kind),
        pltpu.VMEM((Z + 1, chunks, rows, width), kind),
        DMA((held,)),
        DMA((Z * X, chunks)),
        DMA((across, chunks)),
        DMA((Z, chunks)),
        DMA((Z + 1, chunks)),
    ]


STEP = 16


def scatter_steps(line, chunks, block, piece, scratch, store, done, start, pace):
    mine, from_x, from_z, load_sem, xs_sem, xr_sem, zs_sem, zr_sem = scratch
    Z, X, z, x = line.Z, line.X, line.z, line.x
    exists = line.exists
    rows = mine.shape[2]

    def spot(zz, xx):
        return zz if X <= 2 else zz * X + xx

    def load(zz, xx):
        at = spot(zz, xx)
        return pltpu.make_async_copy(block(zz * X + xx), mine.at[at], load_sem.at[at])

    def x_landing(zz, xx, right, receiver):
        if X <= 2:
            return zz
        return zz * (X + 1) + (xx if right else jnp.where(xx == receiver, X, xx))

    def x_copy(right, zz, xx, c):
        landing = x_landing(zz, xx, right, x + 1 if right else x - 1)
        src = piece(zz * X + xx, c) if X <= 2 else mine.at[spot(zz, xx), c]
        return remote(
            src,
            from_x.at[landing, c],
            xs_sem.at[zz * X + xx, c],
            xr_sem.at[landing, c],
            line.to(RIGHT if right else LEFT),
        )

    def z_copy(up, zz, c):
        landing = zz if up else jnp.where(zz == z - 1, Z, zz)
        return remote(
            mine.at[spot(zz, x), c],
            from_z.at[landing, c],
            zs_sem.at[zz, c],
            zr_sem.at[landing, c],
            line.to(UP if up else DOWN),
        )

    def wait_in(buffer, sem, at, c):
        in_place(buffer.at[at, c], sem.at[at, c]).wait()

    def add_in(at, buffer, landing, c):
        def body(i, carry):
            part = pl.ds(pl.multiple_of(i * STEP, STEP), STEP)
            mine[at, c, part] = (
                mine[at, c, part].astype(jnp.float32) + buffer[landing, c, part].astype(jnp.float32)
            ).astype(mine.dtype)
            return carry

        lax.fori_loop(0, rows // STEP, body, 0)

    def x_line(zz):
        for k in range(X - 1):
            for right, xx, here in ((True, X - 1 - k, X - 1 - k > x), (False, k, k < x)):

                @pl.when(here)
                def _(right=right, xx=xx):
                    if X > 2:
                        load(zz, xx).wait()
                    for c in range(chunks):
                        if X > 2:

                            @pl.when(exists[LEFT if right else RIGHT])
                            def _(c=c):
                                landing = x_landing(zz, xx, right, jnp.int32(-1))
                                wait_in(from_x, xr_sem, landing, c)
                                add_in(spot(zz, xx), from_x, landing, c)

                        x_copy(right, zz, xx, c).start()

    def x_join(zz, c):
        at = spot(zz, x)
        if X == 2:
            wait_in(from_x, xr_sem, zz, c)
            add_in(at, from_x, zz, c)
        elif X > 2:
            for right in (True, False):

                @pl.when(exists[LEFT if right else RIGHT])
                def _(right=right):
                    landing = zz * (X + 1) + (x if right else X)
                    wait_in(from_x, xr_sem, landing, c)
                    add_in(at, from_x, landing, c)

    def ways(k):
        return ((True, Z - 1 - k, Z - 1 - k > z), (False, k, k < z))

    def begin():
        for zz in range(Z):
            for xx in range(X):
                if X > 2:
                    load(zz, xx).start()
            if X <= 2:
                load(zz, x).start()
        for k in range(Z - 1):
            for up, zz, here in ways(k):

                @pl.when(here)
                def _(zz=zz):
                    x_line(zz)

        x_line(z)

    def pass_on(k, c):
        for up, zz, here in ways(k):

            @pl.when(here)
            def _(up=up, zz=zz):
                if c == 0:
                    load(zz, x).wait()
                x_join(zz, c)

                @pl.when(exists[DOWN if up else UP])
                def _():
                    wait_in(from_z, zr_sem, zz, c)
                    add_in(spot(zz, x), from_z, zz, c)

                z_copy(up, zz, c).start()

    def settle(c):
        if c == 0:
            load(z, x).wait()
        x_join(z, c)

        @pl.when(exists[DOWN])
        def _():
            wait_in(from_z, zr_sem, z, c)

        @pl.when(exists[UP])
        def _():
            wait_in(from_z, zr_sem, Z, c)

        def body(i, carry):
            part = pl.ds(pl.multiple_of(i * STEP, STEP), STEP)
            total = mine[spot(z, x), c, part].astype(jnp.float32)
            below = from_z[z, c, part].astype(jnp.float32)
            above = from_z[Z, c, part].astype(jnp.float32)
            total = total + jnp.where(z > 0, below, 0.0)
            total = total + jnp.where(z < Z - 1, above, 0.0)
            store(c, part, total)
            return carry

        lax.fori_loop(0, rows // STEP, body, 0)
        done(c)

    def finish():
        for zz in range(Z):
            for c in range(chunks):
                for xx in range(X):

                    @pl.when(xx != x)
                    def _(zz=zz, xx=xx, c=c):
                        x_copy(True, zz, xx, c).wait_send()

                @pl.when(zz != z)
                def _(zz=zz, c=c):
                    z_copy(True, zz, c).wait_send()

    steps = [(start, begin)]
    for k in range(Z - 1):
        for c in range(chunks):
            steps.append(
                (start + pace * (1 + k + (c + 1) / chunks), functools.partial(pass_on, k, c))
            )
    for c in range(chunks):
        steps.append((start + pace * (Z + (c + 1) / chunks), functools.partial(settle, c)))
    steps.append((start + pace * (Z + 2), finish))
    return steps


class Gather:
    def __init__(self, axis, block, chunks, start=0.0, pace=21.0):
        self.axis, self.chunks, self.start, self.pace = axis, chunks, start, pace
        self.inputs = [block]
        self.everyone = ()
        count = lax.axis_size(axis)
        self.outputs = [(ANY, jax.ShapeDtypeStruct((count,) + block.shape, block.dtype))]
        self.scratch = [DMA] + gather_sems(axis, chunks)

    def steps(self, lines, ins, outs, scratch):
        line, (x_ref,), (out_ref,) = lines[self.axis], ins, outs
        own_sem, *sems = scratch
        rows = x_ref.shape[0] // self.chunks
        own = pltpu.make_async_copy(x_ref, out_ref.at[line.me], own_sem)

        def part(c):
            return pl.ds(c * rows, rows)

        steps = gather_steps(
            line,
            self.chunks,
            lambda origin, c: out_ref.at[origin, part(c)],
            lambda c: x_ref.at[part(c)],
            lambda c: None,
            sems,
            self.start,
            self.pace,
        )
        return [(self.start, own.start)] + steps + [(steps[-1][0], own.wait)]


class Scatter:
    def __init__(self, axis, terms, chunks, start=0.0, pace=21.0):
        self.axis, self.chunks, self.start, self.pace = axis, chunks, start, pace
        count = lax.axis_size(axis)
        rows, width = terms.shape[0] // count // chunks, terms.shape[1]
        self.inputs = [terms.reshape(count, chunks, rows, width)]
        self.everyone = ()
        self.outputs = [(VMEM, jax.ShapeDtypeStruct((chunks * rows, width), jnp.float32))]
        self.scratch = scatter_scratch(axis, chunks, rows, width, terms.dtype)

    def steps(self, lines, ins, outs, scratch):
        (p_ref,), (out_ref,) = ins, outs
        rows = p_ref.shape[2]

        def store(c, part, total):
            out_ref[pl.ds(pl.multiple_of(c * rows + part.start, STEP), STEP)] = total

        return scatter_steps(
            lines[self.axis],
            self.chunks,
            lambda slot: p_ref.at[slot],
            lambda slot, c: p_ref.at[slot, c],
            scratch,
            store,
            lambda c: None,
            self.start,
            self.pace,
        )


class Spread:
    def __init__(self, weights, window, first, start=0.0, pace=6.0):
        self.inputs = list(weights)
        self.window, self.first, self.start, self.pace = window, first, start, pace
        self.everyone = ("shard",)
        shards, replicas = lax.axis_size("shard"), lax.axis_size("replica")
        self.part = weights[0].shape[0] // replicas
        wide = len(weights) * window
        shape = (shards, replicas, self.part, wide)
        self.outputs = [(ANY, jax.ShapeDtypeStruct(shape, weights[0].dtype))]
        self.scratch = [
            DMA((len(weights),)),
            DMA((len(weights), shards)),
            DMA((len(weights), shards)),
        ] + gather_sems("replica", shards)

    def steps(self, lines, ins, outs, scratch):
        own_sem, deal_send, deal_recv, *sems = scratch
        (out_ref,) = outs
        group, copies = lines["shard"], lines["replica"]
        rows = pl.ds(pl.multiple_of(copies.me * self.part, self.part), self.part)
        kinds = range(len(ins))

        def source(kind, target):
            return ins[kind].at[rows, pl.ds(pl.multiple_of(self.first(target), 128), self.window)]

        def landing(kind, origin):
            return out_ref.at[origin, copies.me, :, pl.ds(kind * self.window, self.window)]

        def own(kind):
            return pltpu.make_async_copy(
                source(kind, group.me), landing(kind, group.me), own_sem.at[kind]
            )

        def deal(kind, k):
            target = group.other(k)
            return remote(
                source(kind, target),
                landing(kind, group.me),
                deal_send.at[kind, k],
                deal_recv.at[kind, group.me],
                {"shard": target},
            )

        def begin():
            for k in range(1, group.count):
                for kind in kinds:
                    deal(kind, k).start()
            for kind in kinds:
                own(kind).start()

        def ready(c):
            @pl.when(c == group.me)
            def _():
                for kind in kinds:
                    own(kind).wait()

            @pl.when(c != group.me)
            def _():
                for kind in kinds:
                    in_place(landing(kind, c), deal_recv.at[kind, c]).wait()

        def finish():
            for k in range(1, group.count):
                for kind in kinds:
                    deal(kind, k).wait_send()

        steps = gather_steps(
            copies,
            group.count,
            lambda origin, c: out_ref.at[c, origin],
            lambda c: out_ref.at[c, copies.me],
            ready,
            sems,
            self.start + 2 * self.pace,
            self.pace,
        )
        return [(self.start, begin)] + steps + [(steps[-1][0], finish)]


class Collect:
    def __init__(self, terms, start=0.0, pace=6.0):
        shards, replicas = lax.axis_size("shard"), lax.axis_size("replica")
        part, wide = terms.shape[0] // shards // replicas, terms.shape[1]
        self.inputs = [terms.reshape(shards, replicas, part, wide)]
        self.start, self.pace = start, pace
        self.everyone = ("shard",)
        kind = terms.dtype
        self.outputs = [(ANY, jax.ShapeDtypeStruct((replicas, shards, part, wide), kind))]
        self.own_scratch = [
            pltpu.VMEM((shards, part, wide), kind),
            DMA,
            DMA((shards,)),
            DMA((shards,)),
        ] + gather_sems("replica", shards)
        self.scratch = self.own_scratch + scatter_scratch("replica", shards, part, wide, kind)

    def steps(self, lines, ins, outs, scratch):
        (p_ref,), (out_ref,) = ins, outs
        total_ref, own_sem, send_sem, recv_sem = scratch[:4]
        sems = scratch[4:6]
        group, copies = lines["shard"], lines["replica"]

        def own():
            return pltpu.make_async_copy(
                total_ref.at[group.me], out_ref.at[copies.me, group.me], own_sem
            )

        def deal(c):
            return remote(
                total_ref.at[c],
                out_ref.at[copies.me, group.me],
                send_sem.at[c],
                recv_sem.at[group.me],
                {"shard": jnp.int32(c)},
            )

        def store(c, part, total):
            total_ref[c, part] = total.astype(total_ref.dtype)

        def done(c):
            @pl.when(c == group.me)
            def _():
                own().start()

            @pl.when(c != group.me)
            def _():
                deal(c).start()

        def ready(c):
            @pl.when(c == group.me)
            def _():
                own().wait()

            @pl.when(c != group.me)
            def _():
                in_place(out_ref.at[copies.me, c], recv_sem.at[c]).wait()

        def finish():
            for c in range(group.count):

                @pl.when(c != group.me)
                def _(c=c):
                    deal(c).wait_send()

        summing = scatter_steps(
            copies,
            group.count,
            lambda slot: p_ref.at[:, slot],
            lambda slot, c: p_ref.at[c, slot],
            scratch[6:],
            store,
            done,
            self.start,
            self.pace,
        )
        again = self.start + self.pace * (copies.Z + 3)
        sharing = gather_steps(
            copies,
            group.count,
            lambda origin, c: out_ref.at[origin, c],
            lambda c: out_ref.at[copies.me, c],
            ready,
            sems,
            again,
            self.pace,
        )
        return summing + sharing + [(sharing[-1][0], finish)]


class Total:
    def __init__(self, terms, start=0.0, pace=6.0):
        replicas = lax.axis_size("replica")
        share, wide = terms.shape[0] // replicas, terms.shape[1]
        chunks = max(n for n in (1, 2, 3, 4) if share % (n * STEP) == 0)
        rows = share // chunks
        self.inputs = [terms.reshape(replicas, chunks, rows, wide)]
        self.start, self.pace, self.chunks = start, pace, chunks
        self.everyone = ()
        kind = terms.dtype
        self.outputs = [(ANY, jax.ShapeDtypeStruct((replicas, chunks, rows, wide), kind))]
        self.scratch = [pltpu.VMEM((chunks, rows, wide), kind), DMA((chunks,))]
        self.scratch += gather_sems("replica", chunks)
        self.scratch += scatter_scratch("replica", chunks, rows, wide, kind)

    def steps(self, lines, ins, outs, scratch):
        (p_ref,), (out_ref,) = ins, outs
        total_ref, own_sem = scratch[:2]
        copies = lines["replica"]

        def own(c):
            return pltpu.make_async_copy(
                total_ref.at[c], out_ref.at[copies.me, c], own_sem.at[c]
            )

        def store(c, part, total):
            total_ref[c, part] = total.astype(total_ref.dtype)

        def finish():
            for c in range(self.chunks):
                own(c).wait()

        summing = scatter_steps(
            copies,
            self.chunks,
            lambda slot: p_ref.at[slot],
            lambda slot, c: p_ref.at[slot, c],
            scratch[4:],
            store,
            lambda c: own(c).start(),
            self.start,
            self.pace,
        )
        sharing = gather_steps(
            copies,
            self.chunks,
            lambda origin, c: out_ref.at[origin, c],
            lambda c: total_ref.at[c],
            lambda c: None,
            scratch[2:4],
            self.start + self.pace * (copies.Z + 2),
            self.pace,
        )
        return summing + sharing + [(sharing[-1][0], finish)]


class Small:
    def __init__(self, dealt, shared, start=0.0):
        shards, replicas = lax.axis_size("shard"), lax.axis_size("replica")
        self.inputs = [dealt, shared]
        self.start = start
        self.everyone = ("shard", "replica")
        one = dealt.shape[1:]
        self.outputs = [
            (VMEM, jax.ShapeDtypeStruct(one, jnp.float32)),
            (VMEM, jax.ShapeDtypeStruct(shared.shape, jnp.float32)),
        ]
        self.scratch = [
            pltpu.VMEM((shards,) + one, jnp.float32),
            pltpu.VMEM((replicas,) + one, jnp.float32),
            pltpu.VMEM((replicas,) + shared.shape, jnp.float32),
            DMA((shards,)), DMA((shards,)),
            DMA((2, replicas)), DMA((2, replicas)), DMA((2,)),
        ]

    def steps(self, lines, ins, outs, scratch):
        dealt, shared = ins
        out_one, out_rows = outs
        got, got_one, got_rows, send, recv, send2, recv2, own = scratch
        group, copies = lines["shard"], lines["replica"]

        def deal(k):
            target = group.other(k)
            return remote(
                dealt.at[target], got.at[group.me], send.at[k], recv.at[group.me], {"shard": target}
            )

        def share(which, k):
            buffer = (got_one, got_rows)[which]
            return remote(
                buffer.at[copies.me] if which == 0 else shared,
                buffer.at[copies.me],
                send2.at[which, k],
                recv2.at[which, copies.me],
                {"replica": copies.other(k)},
            )

        def keep():
            return pltpu.make_async_copy(dealt.at[group.me], got.at[group.me], own.at[0])

        def keep_rows():
            return pltpu.make_async_copy(shared, got_rows.at[copies.me], own.at[1])

        def begin():
            keep().start()
            keep_rows().start()
            for k in range(1, group.count):
                deal(k).start()
            for k in range(1, copies.count):
                share(1, k).start()

        def middle():
            keep().wait()
            for k in range(1, group.count):
                origin = group.other(k)
                in_place(got.at[origin], recv.at[origin]).wait()
            total = got[0]
            for s in range(1, group.count):
                total = total + got[s]
            got_one[copies.me] = total
            for k in range(1, copies.count):
                share(0, k).start()

        def end():
            keep_rows().wait()
            for k in range(1, copies.count):
                origin = copies.other(k)
                in_place(got_one.at[origin], recv2.at[0, origin]).wait()
                in_place(got_rows.at[origin], recv2.at[1, origin]).wait()
            one, rows = got_one[0], got_rows[0]
            for r in range(1, copies.count):
                one, rows = one + got_one[r], rows + got_rows[r]
            out_one[...] = one
            out_rows[...] = rows
            for k in range(1, group.count):
                deal(k).wait_send()
            for k in range(1, copies.count):
                share(0, k).wait_send()
                share(1, k).wait_send()

        return [(self.start, begin), (self.start + 5.0, middle), (self.start + 10.0, end)]


def layout_of(tasks):
    inputs, outputs, scratch, spans = [], [], [], []
    for task in tasks:
        spans.append((len(inputs), len(outputs), len(scratch)))
        inputs += task.inputs
        outputs += task.outputs
        scratch += task.scratch
    return inputs, outputs, scratch, spans


def task_steps(tasks, spans, axes, ins, outs, scratch):
    lines = {axis: Lines(axis) for axis in axes}
    everyone = {axis for task in tasks for axis in task.everyone}
    steps = []
    for task, (i, o, s) in zip(tasks, spans):
        steps += task.steps(
            lines,
            ins[i : i + len(task.inputs)],
            outs[o : o + len(task.outputs)],
            scratch[s : s + len(task.scratch)],
        )
    steps.sort(key=lambda step: step[0])
    return [(-1.0, lambda: greet(list(lines.values()), everyone))] + steps


def exchange(tasks, axes, ident):
    inputs, outputs, scratch, spans = layout_of(tasks)

    def kernel(*refs):
        ins = refs[: len(inputs)]
        outs = refs[len(inputs) : len(inputs) + len(outputs)]
        rest = refs[len(inputs) + len(outputs) :]
        for _, step in task_steps(tasks, spans, axes, ins, outs, rest):
            step()

    return pl.pallas_call(
        kernel,
        in_specs=[ANY] * len(inputs),
        out_specs=[spec for spec, _ in outputs],
        out_shape=[shape for _, shape in outputs],
        scratch_shapes=scratch,
        compiler_params=pltpu.CompilerParams(
            collective_id=ident, has_side_effects=True, vmem_limit_bytes=60 * 1024 * 1024
        ),
    )(*inputs)


HD = 128
TAPS = 4
KINDS = 3


def dot_nn(a, b):
    return lax.dot_general(
        a.astype(jnp.bfloat16),
        b.astype(jnp.bfloat16),
        (((1,), (0,)), ((), ())),
        preferred_element_type=jnp.float32,
    )


def dot_nt(a, b):
    return lax.dot_general(
        a.astype(jnp.bfloat16),
        b.astype(jnp.bfloat16),
        (((1,), (1,)), ((), ())),
        preferred_element_type=jnp.float32,
    )


def dot_tn(a, b):
    return lax.dot_general(
        a.astype(jnp.bfloat16),
        b.astype(jnp.bfloat16),
        (((0,), (0,)), ((), ())),
        preferred_element_type=jnp.float32,
    )


def time_of(shape, dim, lanes):
    index = lax.broadcasted_iota(jnp.int32, shape, dim)
    return lax.rem(index, 8) * lanes + lax.div(index, 8)


def lower_inverses(lowers, lanes):
    size = lowers[0].shape[0]
    row_t = time_of((size, size), 0, lanes)
    col_t = time_of((size, size), 1, lanes)
    eye = jnp.where(row_t == col_t, 1.0, 0.0)

    def same(width):
        return lax.div(row_t, width) == lax.div(col_t, width)

    first = [jnp.where(same(8), a, 0.0) for a in lowers]
    second = [dot_nn(f, f) for f in first]
    inverse = [eye + f + s + dot_nn(f, s) for f, s in zip(first, second)]
    fourth = [dot_nn(s, s) for s in second]
    inverse = [t + dot_nn(t, f) for t, f in zip(inverse, fourth)]
    width = 16
    while width <= size:
        fresh = same(width) & jnp.logical_not(same(width // 2))
        left = [dot_nn(t, jnp.where(fresh, a, 0.0)) for t, a in zip(inverse, lowers)]
        inverse = [t + dot_nn(l, t) for t, l in zip(inverse, left)]
        width *= 2
    return inverse


def rounded(values):
    return values.astype(jnp.bfloat16).astype(jnp.float32)


def sigmoid(values):
    return 1.0 / (1.0 + jnp.exp(-values))


def unit_scale(pre):
    return lax.rsqrt(jnp.sum(pre * pre, axis=1, keepdims=True) + 1e-6)


def mean_scale(values):
    return lax.rsqrt(jnp.mean(values * values, axis=1, keepdims=True) + 1e-5)


def delta_forward(
    lanes, heads, group, proj_ref, taps_ref, gain_ref, low_ref, off_ref, rem_ref,
    zed_ref, mixed_ref, sums_ref, s_ref, t_ref, mk_ref, mv_ref, u_ref,
    state, last, unit,
):
    size = lanes * 8
    rows = group * 8
    wide = heads * HD
    scale = HD ** (-0.5)

    @pl.when(pl.program_id(0) == 0)
    def _():
        state[...] = jnp.zeros_like(state)
        last[...] = jnp.zeros_like(last)

    top = lax.broadcasted_iota(jnp.int32, (rows, HD), 0) == 0
    for kind in range(KINDS):
        for h in range(heads):
            cols = pl.ds(kind * wide + h * HD, HD)
            signal = [rounded(proj_ref[s, :, cols]) for s in range(lanes)]
            moved = {}
            for back in range(1, TAPS):
                lane = lanes - back
                edge = last[kind * heads + h, back, 0:1]
                moved[lane] = jnp.where(top, edge, pltpu.roll(signal[lane], 1, 0))
            for back in range(1, TAPS):
                last[kind * heads + h, back, 0:1] = signal[lanes - back][rows - 1 : rows]
            for s in range(lanes):
                off = off_ref[s]
                total = signal[s] * taps_ref[kind * TAPS : kind * TAPS + 1, h * HD : (h + 1) * HD]
                for hop in range(1, TAPS):
                    earlier = signal[s - hop] if s >= hop else moved[lanes + s - hop]
                    tap = taps_ref[kind * TAPS + hop : kind * TAPS + hop + 1, h * HD : (h + 1) * HD]
                    total = total + jnp.where(off >= hop, earlier, 0.0) * tap
                sums_ref[s, :, cols] = total
                pre = total * sigmoid(total)
                if kind < 2:
                    pre = pre * unit_scale(pre)
                unit[s, :, cols] = pre

    row_t = time_of((size, size), 0, lanes)
    col_t = time_of((size, size), 1, lanes)
    local_t = time_of((size, HD), 0, lanes).astype(jnp.float32)
    pairs = [(g, h) for g in range(group) for h in range(heads)]

    def span(g):
        return pl.ds(g * 8, 8)

    def flat(ref, g, first, count=HD):
        return ref[:, span(g), first : first + count].reshape(size, count)

    gates = {}
    for g in range(group):
        logits = flat(proj_ref, g, 4 * wide)
        strength = sigmoid(rounded(logits))
        for h in range(heads):
            gates[g, h] = jnp.broadcast_to(strength[:, h : h + 1], (size, HD))
    keys = {p: flat(unit, p[0], wide + p[1] * HD) for p in pairs}
    kbs = {p: gates[p] * keys[p] for p in pairs}
    lows = {g: low_ref[g].astype(jnp.float32) for g in range(group)}
    lowers = [
        -jnp.where(row_t == col_t, 0.0, lows[p[0]]) * dot_nt(kbs[p], keys[p]) for p in pairs
    ]
    inverses = dict(zip(pairs, lower_inverses(lowers, lanes)))
    mks = {p: dot_nn(inverses[p], kbs[p]) for p in pairs}
    mvs = {
        p: dot_nn(inverses[p], gates[p] * flat(unit, p[0], 2 * wide + p[1] * HD))
        for p in pairs
    }
    queries = {p: flat(unit, p[0], p[1] * HD) for p in pairs}
    scores = {p: lows[p[0]] * dot_nt(queries[p], keys[p]) for p in pairs}
    for g, h in pairs:
        t_ref[g, h] = inverses[g, h].astype(t_ref.dtype)
        mk_ref[g, h] = mks[g, h].astype(mk_ref.dtype)
        mv_ref[g, h] = mvs[g, h].astype(mv_ref.dtype)
    for g in range(group):
        carry = jnp.where(flat(off_ref, g, 0) > local_t, 1.0, 0.0)
        keep = jnp.where(flat(rem_ref, g, 0) + local_t >= size, 1.0, 0.0)
        for h in range(heads):
            p = (g, h)
            held = state[h]
            s_ref[g, h] = held.astype(s_ref.dtype)
            u = mvs[p] - carry * dot_nn(mks[p], held)
            u_ref[g, h] = u.astype(u_ref.dtype)
            state[h] = (carry[0:1] * keep[0:1]) * held + dot_tn(keys[p], keep * u)
            out = (carry * dot_nn(queries[p], held) + dot_nn(scores[p], u)) * scale
            mixed = rounded(out)
            gate = flat(proj_ref, g, 3 * wide + h * HD)
            zed = mixed * mean_scale(mixed) * gain_ref[...] * (gate * sigmoid(gate))
            mixed_ref[:, span(g), h * HD : (h + 1) * HD] = mixed.reshape(lanes, 8, HD).astype(
                mixed_ref.dtype
            )
            zed_ref[:, span(g), h * HD : (h + 1) * HD] = zed.reshape(lanes, 8, HD).astype(
                zed_ref.dtype
            )


def delta_backward(
    lanes, heads, group, proj_ref, sums_ref, mixed_ref, dzed_ref, taps_ref, gain_ref,
    low_ref, off_ref, rem_ref, s_ref, t_ref, mk_ref, mv_ref, u_ref,
    dproj_ref, gtaps_ref, ghead_ref,
    state, edge, edge_off, errs, taps_sum, head_sum,
):
    size = lanes * 8
    rows = group * 8
    wide = heads * HD
    scale = HD ** (-0.5)

    @pl.when(pl.program_id(0) == 0)
    def _():
        state[...] = jnp.zeros_like(state)
        edge[...] = jnp.zeros_like(edge)
        edge_off[...] = jnp.zeros_like(edge_off)
        taps_sum[...] = jnp.zeros_like(taps_sum)
        head_sum[...] = jnp.zeros_like(head_sum)

    row_t = time_of((size, size), 0, lanes)
    col_t = time_of((size, size), 1, lanes)
    local_t = time_of((size, HD), 0, lanes).astype(jnp.float32)
    lane_id = lax.broadcasted_iota(jnp.int32, (size, HD), 1)
    pairs = [(g, h) for g in range(group) for h in range(heads)]

    def span(g):
        return pl.ds(g * 8, 8)

    def flat(ref, g, first, count=HD):
        return ref[:, span(g), first : first + count].reshape(size, count)

    def put(ref, g, first, value):
        ref[:, span(g), first : first + HD] = value.reshape(lanes, 8, HD).astype(ref.dtype)

    gain = gain_ref[...]
    d_out, q, k, v, beta = {}, {}, {}, {}, {}
    pre, scales, slopes = {}, {}, {}
    head_total = jnp.zeros((size, HD), jnp.float32)
    strengths = {}
    carries, keeps, lows = {}, {}, {}
    for g in range(group):
        carries[g] = jnp.where(flat(off_ref, g, 0) > local_t, 1.0, 0.0)
        keeps[g] = jnp.where(flat(rem_ref, g, 0) + local_t >= size, 1.0, 0.0)
        lows[g] = low_ref[g].astype(jnp.float32)
        strengths[g] = sigmoid(rounded(flat(proj_ref, g, 4 * wide)))
    for g, h in pairs:
        p = (g, h)
        mixed = flat(mixed_ref, g, h * HD).astype(jnp.float32)
        gate = flat(proj_ref, g, 3 * wide + h * HD)
        dzed = flat(dzed_ref, g, h * HD)
        s = sigmoid(gate)
        r = mean_scale(mixed)
        through = dzed * (gate * s)
        head_total = head_total + through * mixed * r
        inner = jnp.mean(mixed * gain * through, axis=1, keepdims=True)
        d_mixed = rounded(r * gain * through - mixed * (r * r * r) * inner)
        put(dproj_ref, g, 3 * wide + h * HD, dzed * (mixed * r * gain) * (s * (1.0 + gate * (1.0 - s))))
        d_out[p] = d_mixed * scale
        for kind, store in ((0, q), (1, k), (2, v)):
            total = flat(sums_ref, g, kind * wide + h * HD)
            s = sigmoid(total)
            value = total * s
            slopes[kind, g, h] = s * (1.0 + total * (1.0 - s))
            if kind < 2:
                pre[kind, g, h] = value
                scales[kind, g, h] = unit_scale(value)
                value = value * scales[kind, g, h]
            store[p] = value
        beta[p] = jnp.broadcast_to(strengths[g][:, h : h + 1], (size, HD))
    head_sum[...] += head_total

    scores = {p: lows[p[0]] * dot_nt(q[p], k[p]) for p in pairs}
    du = {p: dot_tn(scores[p], d_out[p]) for p in pairs}
    ds = {p: lows[p[0]] * dot_nt(d_out[p], u_ref[p[0], p[1]]) for p in pairs}
    cdo = {p: carries[p[0]] * d_out[p] for p in pairs}
    dq = {p: dot_nt(cdo[p], s_ref[p[0], p[1]]) + dot_nn(ds[p], k[p]) for p in pairs}
    dk = {p: dot_tn(ds[p], q[p]) for p in pairs}
    lift = {p: dot_tn(q[p], cdo[p]) for p in pairs}
    later = {}
    for g in reversed(range(group)):
        for h in range(heads):
            p = (g, h)
            later[p] = state[h]
            du[p] = du[p] + keeps[g] * dot_nn(k[p], later[p])
            mk = carries[g] * mk_ref[g, h].astype(jnp.float32)
            state[h] = (carries[g][0:1] * keeps[g][0:1]) * later[p] + lift[p] - dot_tn(mk, du[p])
    for p in pairs:
        dk[p] = dk[p] + dot_nt(keeps[p[0]] * u_ref[p[0], p[1]].astype(jnp.float32), later[p])
    dmk = {p: -carries[p[0]] * dot_nt(du[p], s_ref[p[0], p[1]]) for p in pairs}
    xx = {p: dot_tn(t_ref[p[0], p[1]], dmk[p]) for p in pairs}
    yy = {p: dot_tn(t_ref[p[0], p[1]], du[p]) for p in pairs}
    da = {
        p: jnp.where(row_t == col_t, 0.0, lows[p[0]])
        * (dot_nt(xx[p], mk_ref[p[0], p[1]]) + dot_nt(yy[p], mv_ref[p[0], p[1]]))
        for p in pairs
    }
    dkb = {p: xx[p] - dot_nn(da[p], k[p]) for p in pairs}
    dk = {p: dk[p] - dot_tn(da[p], beta[p] * k[p]) + beta[p] * dkb[p] for p in pairs}
    for g in range(group):
        d_logits = jnp.zeros((size, HD), jnp.float32)
        for h in range(heads):
            p = (g, h)
            db = jnp.sum(dkb[p] * k[p] + yy[p] * v[p], axis=1, keepdims=True)
            d_logits = d_logits + jnp.where(lane_id == h, db * beta[p] * (1.0 - beta[p]), 0.0)
            for kind, grad in ((0, dq[p]), (1, dk[p])):
                r, raw = scales[kind, g, h], pre[kind, g, h]
                inner = jnp.sum(raw * grad, axis=1, keepdims=True)
                err = (r * grad - raw * (r * r * r) * inner) * slopes[kind, g, h]
                put(errs, g, kind * wide + h * HD, err)
            put(errs, g, 2 * wide + h * HD, beta[p] * yy[p] * slopes[2, g, h])
        put(dproj_ref, g, 4 * wide, d_logits)

    bottom = lax.broadcasted_iota(jnp.int32, (rows, HD), 0) == rows - 1
    for kind in range(KINDS):
        for h in range(heads):
            at = kind * wide + h * HD
            cols = pl.ds(at, HD)
            err = [errs[s, :, cols] for s in range(lanes)]
            taps = [
                taps_ref[kind * TAPS + hop : kind * TAPS + hop + 1, h * HD : (h + 1) * HD]
                for hop in range(TAPS)
            ]
            sums = [jnp.zeros((rows, HD), jnp.float32) for _ in range(TAPS)]
            live = {}
            for hop in range(1, TAPS):
                for s in range(lanes):
                    live[hop, s] = jnp.where(off_ref[s] >= hop, err[s], 0.0)
            for hop in range(1, TAPS):
                for s in range(hop):
                    row = jnp.where(edge_off[s, 0:1] >= hop, edge[kind * heads + h, s, 0:1], 0.0)
                    live[hop, lanes + s] = jnp.where(
                        bottom, row, pltpu.roll(live[hop, s], rows - 1, 0)
                    )
            for s in range(lanes):
                signal = rounded(proj_ref[s, :, cols])
                total = err[s] * taps[0]
                sums[0] = sums[0] + err[s] * signal
                for hop in range(1, TAPS):
                    total = total + live[hop, s + hop] * taps[hop]
                    sums[hop] = sums[hop] + live[hop, s + hop] * signal
                dproj_ref[s, :, cols] = total.astype(dproj_ref.dtype)
            for s in range(TAPS - 1):
                edge[kind * heads + h, s, 0:1] = err[s][0:1]
            for hop in range(TAPS):
                folded = sums[hop].reshape(group, 8, HD)
                taps_sum[kind * TAPS + hop, :, h * HD : (h + 1) * HD] += jnp.sum(folded, axis=0)
    for s in range(TAPS - 1):
        edge_off[s, 0:1] = off_ref[s][0:1]

    @pl.when(pl.program_id(0) == pl.num_programs(0) - 1)
    def _():
        gtaps_ref[...] = jnp.sum(taps_sum[...], axis=1)
        ghead_ref[...] = jnp.sum(head_sum[...], axis=0, keepdims=True)


def mixer_specs(lanes, heads, group, flip):
    size = lanes * 8
    at = (lambda i: flip - 1 - i) if flip else (lambda i: i)

    def token(width):
        return pl.BlockSpec((lanes, 8 * group, width), lambda i: (0, at(i), 0))

    def saved(first, second):
        return pl.BlockSpec((group, heads, first, second), lambda i: (at(i), 0, 0, 0))

    square = pl.BlockSpec((group, size, size), lambda i: (at(i), 0, 0))
    return token, saved, square


def fixed(shape):
    return pl.BlockSpec(shape, lambda i: (0,) * len(shape))


def saved_shapes(lanes, heads, blocks):
    size = lanes * 8
    kind = jnp.bfloat16
    return [
        jax.ShapeDtypeStruct((blocks, heads, HD, HD), kind),
        jax.ShapeDtypeStruct((blocks, heads, size, size), kind),
        jax.ShapeDtypeStruct((blocks, heads, size, HD), kind),
        jax.ShapeDtypeStruct((blocks, heads, size, HD), kind),
        jax.ShapeDtypeStruct((blocks, heads, size, HD), kind),
    ]


def mixer_forward(proj, taps, gain, low, off, rem, heads, group=4):
    lanes, tokens, width = proj.shape
    blocks, wide = tokens // 8, heads * HD
    size = lanes * 8
    token, saved, square = mixer_specs(lanes, heads, group, 0)
    return pl.pallas_call(
        functools.partial(delta_forward, lanes, heads, group),
        grid=(blocks // group,),
        in_specs=[token(width), fixed(taps.shape), fixed(gain.shape), square, token(HD), token(HD)],
        out_specs=[
            token(wide), token(wide), token(KINDS * wide),
            saved(HD, HD), saved(size, size), saved(size, HD), saved(size, HD), saved(size, HD),
        ],
        out_shape=[
            jax.ShapeDtypeStruct((lanes, tokens, wide), jnp.bfloat16),
            jax.ShapeDtypeStruct((lanes, tokens, wide), jnp.bfloat16),
            jax.ShapeDtypeStruct((lanes, tokens, KINDS * wide), jnp.float32),
        ] + saved_shapes(lanes, heads, blocks),
        scratch_shapes=[
            pltpu.VMEM((heads, HD, HD), jnp.float32),
            pltpu.VMEM((KINDS * heads, TAPS, 8, HD), jnp.float32),
            pltpu.VMEM((lanes, 8 * group, KINDS * wide), jnp.float32),
        ],
        compiler_params=pltpu.CompilerParams(vmem_limit_bytes=48 * 1024 * 1024),
    )(proj, taps, gain, low, off, rem)


def mixer_backward(
    proj, sums, mixed, dzed, taps, gain, low, off, rem, saves, heads, group=4
):
    lanes, tokens, width = proj.shape
    blocks, wide = tokens // 8, heads * HD
    size = lanes * 8
    token, saved, square = mixer_specs(lanes, heads, group, blocks // group)
    return pl.pallas_call(
        functools.partial(delta_backward, lanes, heads, group),
        grid=(blocks // group,),
        in_specs=[
            token(width), token(KINDS * wide), token(wide), token(wide),
            fixed(taps.shape), fixed(gain.shape), square, token(HD), token(HD),
            saved(HD, HD), saved(size, size), saved(size, HD), saved(size, HD), saved(size, HD),
        ],
        out_specs=[token(width), fixed(taps.shape), fixed(gain.shape)],
        out_shape=[
            jax.ShapeDtypeStruct((lanes, tokens, width), jnp.bfloat16),
            jax.ShapeDtypeStruct(taps.shape, jnp.float32),
            jax.ShapeDtypeStruct(gain.shape, jnp.float32),
        ],
        scratch_shapes=[
            pltpu.VMEM((heads, HD, HD), jnp.float32),
            pltpu.VMEM((KINDS * heads, TAPS, 8, HD), jnp.float32),
            pltpu.VMEM((TAPS, 8, HD), jnp.float32),
            pltpu.VMEM((lanes, 8 * group, KINDS * wide), jnp.float32),
            pltpu.VMEM((taps.shape[0], 8, wide), jnp.float32),
            pltpu.VMEM((size, HD), jnp.float32),
        ],
        compiler_params=pltpu.CompilerParams(vmem_limit_bytes=48 * 1024 * 1024),
    )(proj, sums, mixed, dzed, taps, gain, low, off, rem, *saves)


def segment_masks(lengths_grid, order_row, lanes, tokens):
    slots = order_row.shape[0]
    flat = lengths_grid.reshape(slots)
    first = lax.broadcasted_iota(jnp.int32, (slots, slots), 0)
    second = lax.broadcasted_iota(jnp.int32, (slots, slots), 1)
    run_len = jnp.sum(jnp.where(order_row[:, None] == second, flat[None, :], 0), axis=1)
    ends = jnp.sum(jnp.where(first >= second, run_len[None, :], 0), axis=1)
    starts = ends - run_len
    size = lanes * 8
    blocks = tokens // 8
    lane = lax.broadcasted_iota(jnp.int32, (lanes, tokens), 0)
    step = lax.broadcasted_iota(jnp.int32, (lanes, tokens), 1)
    place = step * lanes + lane
    inside = (starts[:, None, None] <= place[None]) & (place[None] < ends[:, None, None])
    start_at = jnp.sum(jnp.where(inside, starts[:, None, None], 0), axis=0)
    end_at = jnp.sum(jnp.where(inside, ends[:, None, None], 0), axis=0)

    def blocked(values):
        return values.reshape(lanes, blocks, 8).transpose(1, 0, 2).reshape(blocks, size)

    start_b, place_b = blocked(start_at), blocked(place)
    low = (start_b[:, :, None] == start_b[:, None, :]) & (place_b[:, :, None] >= place_b[:, None, :])

    def spread(values):
        return jnp.broadcast_to(values.astype(jnp.float32)[:, :, None], (lanes, tokens, HD))

    return low.astype(jnp.bfloat16), spread(place - start_at), spread(end_at - place)


def project(left_side, right_side):
    return jnp.dot(left_side, right_side, preferred_element_type=jnp.float32)


def times_t(left_side, right_side):
    return lax.dot_general(
        left_side, right_side, (((1,), (1,)), ((), ())), preferred_element_type=jnp.float32
    )


def contract_rows(left_side, right_side):
    return lax.dot_general(
        left_side, right_side, (((0,), (0,)), ((), ())), preferred_element_type=jnp.float32
    )


def rms(values, gain, eps):
    return values * lax.rsqrt(jnp.mean(values * values, axis=-1, keepdims=True) + eps) * gain


def rms_back(values, gain, eps, grad):
    r = lax.rsqrt(jnp.mean(values * values, axis=-1, keepdims=True) + eps)
    inner = jnp.mean(values * gain * grad, axis=-1, keepdims=True)
    return r * gain * grad - values * (r * r * r) * inner, grad * values * r


def column_windows(columns, shards):
    own = columns // shards
    tiles = columns // HD
    width = 1
    while any(min(s * own // HD, tiles - width) * HD + width * HD < (s + 1) * own for s in range(shards)):
        width += 1

    def first(s):
        if isinstance(s, int):
            return min(s * own // HD, tiles - width) * HD
        return jnp.minimum(lax.div(s * own, HD), tiles - width) * HD

    return first, width * HD


def place_windows(kinds, shards, columns, window, first, own, in_ref, *out_refs):
    for kind, out_ref in zip(range(kinds), out_refs):
        for tile in range(columns // HD):
            total = None
            for s in range(shards):
                low = max(tile * HD, s * own)
                high = min((tile + 1) * HD, (s + 1) * own)
                if low < high:
                    at = kind * window + tile * HD - first(s)
                    term = in_ref[0, s, :, at : at + HD].astype(jnp.float32)
                    total = term if total is None else total + term
            out_ref[:, tile * HD : (tile + 1) * HD] = total


def widen(collected, kinds, columns, window, first):
    replicas, shards, part, wide = collected.shape
    return pl.pallas_call(
        functools.partial(place_windows, kinds, shards, columns, window, first, columns // shards),
        grid=(replicas,),
        in_specs=[pl.BlockSpec((1, shards, part, wide), lambda i: (i, 0, 0, 0))],
        out_specs=[pl.BlockSpec((part, columns), lambda i: (i, 0))] * kinds,
        out_shape=[jax.ShapeDtypeStruct((replicas * part, columns), jnp.float32)] * kinds,
        compiler_params=pltpu.CompilerParams(vmem_limit_bytes=48 * 1024 * 1024),
    )(collected)


def body(
    layer_input,
    out_cotangent,
    seq_lengths,
    seq_order,
    w_query,
    w_key,
    w_value,
    w_beta,
    w_outgate,
    w_output,
    conv_query,
    conv_key,
    conv_value,
    attn_gain,
    head_gain,
    mlp_gain,
    w_gate,
    w_up,
    w_down,
):
    bf16, f32 = jnp.bfloat16, jnp.float32
    shards = lax.axis_size("shard")
    shard = lax.axis_index("shard")
    both, group = ("shard", "replica"), ("shard",)
    rows, width = layer_input.shape
    tokens = shards * rows
    weight_rows = w_query.shape[0]
    own = w_output.shape[0]
    heads = own // HD
    hidden_own = w_down.shape[0]
    ffn = w_gate.shape[1]
    ffn_first, ffn_window = column_windows(ffn, shards)
    col_first, col_window = column_windows(width, shards)
    shift = shard * hidden_own - ffn_first(shard)

    total_heads = w_beta.shape[1]
    head_part = jnp.pad(head_gain, (0, weight_rows - head_gain.shape[0]))
    little = jnp.concatenate([w_beta, jnp.stack([attn_gain, mlp_gain, head_part], axis=1)], axis=1)
    little = jnp.pad(little, ((0, 0), (0, HD - little.shape[1])))
    attn_weights, all_source, little = exchange(
        [
            Spread((w_query, w_key, w_value, w_outgate), col_window, col_first, -0.5, 12.0),
            Gather("shard", layer_input, 4),
            Gather("shard", little, 1, 0.0, 20.0),
        ],
        both,
        0,
    )
    mlp_weights, dy = exchange(
        [
            Spread((w_gate, w_up), ffn_window, ffn_first, -0.5, 16.0),
            Gather("shard", out_cotangent, 4),
        ],
        both,
        1,
    )
    dy = dy.reshape(tokens, width)
    mlp_weights = mlp_weights.reshape(width, 2 * ffn_window)
    full_attn_gain = little[:, :, total_heads].reshape(width).astype(f32)
    full_mlp_gain = little[:, :, total_heads + 1].reshape(width).astype(f32)
    head_row = little[:, : head_gain.shape[0], total_heads + 2].reshape(1, HD).astype(f32)
    beta = lax.dynamic_slice_in_dim(little.reshape(width, HD), shard * heads, heads, axis=1)
    attn_weights = jnp.concatenate(
        [attn_weights.reshape(width, 4 * own), jnp.pad(beta, ((0, 0), (0, HD - heads)))], axis=1
    )
    low, off, rem = segment_masks(seq_lengths[0], seq_order[0], shards, rows)

    source = layer_input.astype(f32)
    all_source = all_source.reshape(tokens, width).astype(f32)
    normed = rms(all_source, full_attn_gain, 1e-6).astype(bf16)
    projected = project(normed, attn_weights).reshape(shards, rows, -1)
    taps = jnp.concatenate([conv_query, conv_key, conv_value], axis=0).astype(f32)
    zed, mixed, sums, *saves = mixer_forward(projected, taps, head_row, low, off, rem, heads)
    zed = zed.reshape(tokens, own)
    (hidden,) = exchange([Scatter("shard", project(zed, w_output).astype(bf16), 4)], group, 2)
    hidden = source + hidden

    (mlp_in,) = exchange(
        [Gather("shard", rms(hidden, full_mlp_gain, 1e-6).astype(bf16), 4)], group, 3
    )
    mlp_in = mlp_in.reshape(tokens, width)
    w_down = lax.dynamic_update_slice(jnp.zeros((ffn_window, width), bf16), w_down, (shift, 0))
    lin = project(mlp_in, mlp_weights)
    gate_lin, up_lin = lin[:, :ffn_window], lin[:, ffn_window:]
    s = jax.nn.sigmoid(gate_lin)
    product = (gate_lin * s * up_lin).astype(bf16)
    d_product = times_t(dy, w_down)
    d_gate = (d_product * up_lin * s * (1.0 + gate_lin * (1.0 - s))).astype(bf16)
    d_up = (d_product * gate_lin * s).astype(bf16)
    d_lin = jnp.concatenate([d_gate, d_up], axis=1)
    g_down = contract_rows(product, dy).astype(bf16)
    g_lin = contract_rows(mlp_in, d_lin).astype(bf16)
    d_mlp_in, g_lin, g_down = exchange(
        [
            Scatter("shard", times_t(d_lin, mlp_weights).astype(bf16), 4),
            Collect(g_lin, 0.5, 13.0),
            Total(g_down, 0.7, 13.0),
        ],
        both,
        4,
    )
    d_hidden_norm, g_mlp_rows = rms_back(hidden, full_mlp_gain, 1e-6, d_mlp_in)
    d_hidden = out_cotangent.astype(f32) + d_hidden_norm

    (d_attn,) = exchange([Gather("shard", d_hidden.astype(bf16), 4)], group, 5)
    d_attn = d_attn.reshape(tokens, width)
    g_output = contract_rows(zed, d_attn).astype(bf16)
    out_terms, g_output = exchange(
        [Scatter("shard", project(product, w_down).astype(bf16), 4), Total(g_output, 0.5, 10.0)],
        both,
        6,
    )
    d_zed = times_t(d_attn, w_output).reshape(shards, rows, own)
    d_proj, g_taps, g_head = mixer_backward(
        projected, sums, mixed, d_zed, taps, head_row, low, off, rem, saves, heads
    )
    d_proj = d_proj.reshape(tokens, -1)
    g_proj = contract_rows(normed, d_proj).astype(bf16)
    d_normed, g_proj = exchange(
        [Scatter("shard", times_t(d_proj, attn_weights).astype(bf16), 4), Collect(g_proj, 0.5, 10.0)],
        both,
        7,
    )
    d_source, g_attn_rows = rms_back(source, full_attn_gain, 1e-6, d_normed)

    def dealt(values):
        return values.reshape(shards, -1)

    small = jnp.concatenate(
        [dealt(jnp.sum(g_attn_rows, axis=0)), dealt(jnp.sum(g_mlp_rows, axis=0)), dealt(g_head)], axis=1
    )
    small = jnp.pad(small, ((0, 0), (0, -small.shape[1] % HD)))
    small = jnp.broadcast_to(small[:, None, :], (shards, 8, small.shape[1]))
    small, g_taps = exchange(
        [Small(small, jnp.pad(g_taps, ((0, 16 - g_taps.shape[0]), (0, 0))))], both, 8
    )
    g_query, g_key, g_value, g_outgate = widen(g_proj, 4, width, col_window, col_first)
    g_gate, g_up = widen(g_lin, 2, ffn, ffn_window, ffn_first)
    g_beta = g_proj[..., 4 * own : 4 * own + heads].transpose(0, 2, 1, 3)
    g_down = lax.dynamic_slice_in_dim(g_down.reshape(-1, width), shift, hidden_own)
    gains = width // shards
    return (
        (hidden + out_terms).astype(bf16),
        (d_hidden + d_source).astype(bf16),
        g_query,
        g_key,
        g_value,
        g_beta.reshape(weight_rows, total_heads).astype(f32),
        g_outgate,
        g_output.reshape(own, width).astype(f32),
        g_taps[:TAPS],
        g_taps[TAPS : 2 * TAPS],
        g_taps[2 * TAPS : 3 * TAPS],
        small[0, :gains],
        small[0, 2 * gains : 2 * gains + head_gain.shape[0]],
        small[0, gains : 2 * gains],
        g_gate,
        g_up,
        g_down.astype(f32),
    )


def solution(mesh):
    tokens = P(("replica", "shard"), None)
    whole, columns, vector = P("shard", None), P(None, "shard"), P("shard")
    in_specs = (tokens, tokens, P("replica", None, None), P("replica", None)) + (whole,) * 6
    in_specs += (columns,) * 3 + (vector,) * 3 + (whole,) * 3
    out_specs = (tokens, tokens) + (whole,) * 6 + (columns,) * 3 + (vector,) * 3 + (whole,) * 3
    return jax.shard_map(body, mesh=mesh, in_specs=in_specs, out_specs=out_specs, check_vma=False)
```

```python
import functools

import jax
import jax.numpy as jnp
from jax import lax
from jax.experimental import pallas as pl
from jax.experimental.pallas import tpu as pltpu
from jax.sharding import PartitionSpec as P

MESH = pl.DeviceIdType.MESH
ANY = pl.BlockSpec(memory_space=pl.ANY)
VMEM = pl.BlockSpec(memory_space=pltpu.VMEM)
DMA = pltpu.SemaphoreType.DMA
UP, DOWN, RIGHT, LEFT = range(4)


def grid_of(axis):
    count = lax.axis_size(axis)
    if axis == "replica":
        across = 2 if count % 2 == 0 else 1
        return count // across, across
    depth = 4 if count % 4 == 0 else count
    return depth, count // depth


class Lines:
    def __init__(self, axis):
        self.axis = axis
        self.Z, self.X = grid_of(axis)
        self.count = self.Z * self.X
        self.me = lax.axis_index(axis)
        self.z, self.x = lax.div(self.me, self.X), lax.rem(self.me, self.X)
        z, x, X = self.z, self.x, self.X
        self.targets = ((z + 1) * X + x, (z - 1) * X + x, z * X + x + 1, z * X + x - 1)
        self.exists = (z < self.Z - 1, z > 0, x < X - 1, x > 0)

    def to(self, way):
        return {self.axis: self.targets[way]}

    def other(self, k):
        return lax.rem(self.me + k, self.count)

    def slot(self, zz, xx):
        return zz * self.X + xx


class Turned(Lines):
    def __init__(self, line):
        self.axis, self.count, self.me = line.axis, line.count, line.me
        self.Z, self.X, self.z, self.x = line.X, line.Z, line.x, line.z
        self.targets = line.targets[2:] + line.targets[:2]
        self.exists = line.exists[2:] + line.exists[:2]

    def slot(self, zz, xx):
        return xx * self.Z + zz


class Column(Lines):
    def __init__(self, line):
        self.axis, self.count, self.me = line.axis, line.Z, line.z
        self.Z, self.X, self.z, self.x = line.Z, 1, line.z, jnp.int32(0)
        self.targets = line.targets
        self.exists = line.exists[:2] + (jnp.bool_(False),) * 2

    def slot(self, zz, xx):
        return zz


def greet(lines, everyone):
    barrier = pltpu.get_barrier_semaphore()
    count = jnp.int32(0)
    for line in lines:
        if line.axis in everyone:
            for k in range(1, line.count):
                pl.semaphore_signal(
                    barrier, inc=1, device_id={line.axis: line.other(k)}, device_id_type=MESH
                )
            count = count + (line.count - 1)
            continue
        for way in range(4):

            @pl.when(line.exists[way])
            def _(line=line, way=way):
                pl.semaphore_signal(barrier, inc=1, device_id=line.to(way), device_id_type=MESH)

            count = count + jnp.where(line.exists[way], 1, 0)
    pl.semaphore_wait(barrier, count)


def remote(src, dst, send_sem, recv_sem, device):
    return pltpu.make_async_remote_copy(
        src_ref=src,
        dst_ref=dst,
        send_sem=send_sem,
        recv_sem=recv_sem,
        device_id=device,
        device_id_type=MESH,
    )


def in_place(view, sem):
    return pltpu.make_async_copy(view, view, sem)


def gather_sems(axis, chunks):
    Z, X = grid_of(axis)
    return [DMA((4, Z * X, chunks)), DMA((Z * X, chunks))]


def gather_steps(line, chunks, view, source, ready, sems, start, pace):
    send_sem, recv_sem = sems
    Z, X, z, x, me = line.Z, line.X, line.z, line.x, line.me
    exists = line.exists

    def copy(way, origin, c, src=None):
        spot = view(origin, c)
        return remote(
            spot if src is None else src,
            spot,
            send_sem.at[way, origin, c],
            recv_sem.at[origin, c],
            line.to(way),
        )

    def first(c):
        ready(c)
        for way in range(4):

            @pl.when(exists[way])
            def _(way=way):
                copy(way, me, c, source(c)).start()

    def hop(d, c):
        for way, here in ((UP, z - d >= 0), (DOWN, z + d < Z)):

            @pl.when(here)
            def _(way=way):
                origin = line.slot(z - d if way == UP else z + d, x)
                copy(way, origin, c).wait_recv()
                for onward in (way, RIGHT, LEFT):

                    @pl.when(exists[onward])
                    def _(onward=onward):
                        copy(onward, origin, c).start()

    def across(e, level, c):
        for way, here in ((RIGHT, x - e >= 0), (LEFT, x + e < X)):

            @pl.when(here)
            def _(way=way):
                origin = line.slot(level, x - e if way == RIGHT else x + e)
                copy(way, origin, c).wait_recv()
                if X > 2:

                    @pl.when(exists[way])
                    def _():
                        copy(way, origin, c).start()

    def finish():
        for c in range(chunks):
            for zz in range(Z):
                for way, here in ((UP, zz <= z), (DOWN, zz >= z)):

                    @pl.when(exists[way] & here)
                    def _(way=way, zz=zz, c=c):
                        copy(way, line.slot(zz, x), c).wait_send()

                for xx in range(X):
                    for way, here in ((RIGHT, xx <= x), (LEFT, xx >= x)):

                        @pl.when(exists[way] & here)
                        def _(way=way, zz=zz, xx=xx, c=c):
                            copy(way, line.slot(zz, xx), c).wait_send()

    steps = []
    for c in range(chunks):
        steps.append((start + pace * c / chunks, functools.partial(first, c)))
    for d in range(1, Z):
        for c in range(chunks):
            steps.append((start + pace * (d - 1 + (c + 1) / chunks), functools.partial(hop, d, c)))
    for e in range(1, X):
        for dz in range(Z):
            level = lax.rem(z + dz, Z)
            for c in range(chunks):
                when = start + pace * (Z + e + (dz * chunks + c) / (Z * chunks))
                steps.append((when, functools.partial(across, e, level, c)))
    steps.append((start + pace * (Z + X + 1), finish))
    return steps


def scatter_slots(dims):
    Z, X = dims
    if X == 1:
        return Z, 1
    if X == 2:
        return Z, Z
    return Z * X, Z * (X + 1)


def scatter_scratch(dims, chunks, rows, width, kind):
    Z, X = dims
    held, across = scatter_slots(dims)
    return [
        pltpu.VMEM((held, chunks, rows, width), kind),
        pltpu.VMEM((across, chunks, rows, width), kind),
        pltpu.VMEM((Z + 1, chunks, rows, width), kind),
        DMA((held,)),
        DMA((Z * X, chunks)),
        DMA((across, chunks)),
        DMA((Z, chunks)),
        DMA((Z + 1, chunks)),
    ]


STEP = 16


def stride(rows):
    return max(n for n in (16, 32, 64) if rows % n == 0 and n <= BIG)


BIG = 64


def scatter_steps(line, chunks, block, piece, scratch, store, done, start, pace):
    mine, from_x, from_z, load_sem, xs_sem, xr_sem, zs_sem, zr_sem = scratch
    Z, X, z, x = line.Z, line.X, line.z, line.x
    exists = line.exists
    rows = mine.shape[2]
    step = stride(rows)

    def spot(zz, xx):
        return zz if X <= 2 else zz * X + xx

    def load(zz, xx):
        at = spot(zz, xx)
        return pltpu.make_async_copy(block(line.slot(zz, xx)), mine.at[at], load_sem.at[at])

    def x_landing(zz, xx, right, receiver):
        if X <= 2:
            return zz
        return zz * (X + 1) + (xx if right else jnp.where(xx == receiver, X, xx))

    def x_copy(right, zz, xx, c):
        landing = x_landing(zz, xx, right, x + 1 if right else x - 1)
        src = piece(line.slot(zz, xx), c) if X <= 2 else mine.at[spot(zz, xx), c]
        return remote(
            src,
            from_x.at[landing, c],
            xs_sem.at[zz * X + xx, c],
            xr_sem.at[landing, c],
            line.to(RIGHT if right else LEFT),
        )

    def z_copy(up, zz, c):
        landing = zz if up else jnp.where(zz == z - 1, Z, zz)
        return remote(
            mine.at[spot(zz, x), c],
            from_z.at[landing, c],
            zs_sem.at[zz, c],
            zr_sem.at[landing, c],
            line.to(UP if up else DOWN),
        )

    def wait_in(buffer, sem, at, c):
        in_place(buffer.at[at, c], sem.at[at, c]).wait()

    def add_in(at, buffer, landing, c):
        def body(i, carry):
            part = pl.ds(pl.multiple_of(i * step, step), step)
            mine[at, c, part] = (
                mine[at, c, part].astype(jnp.float32) + buffer[landing, c, part].astype(jnp.float32)
            ).astype(mine.dtype)
            return carry

        lax.fori_loop(0, rows // step, body, 0)

    def x_line(zz):
        for k in range(X - 1):
            for right, xx, here in ((True, X - 1 - k, X - 1 - k > x), (False, k, k < x)):

                @pl.when(here)
                def _(right=right, xx=xx):
                    if X > 2:
                        load(zz, xx).wait()
                    for c in range(chunks):
                        if X > 2:

                            @pl.when(exists[LEFT if right else RIGHT])
                            def _(c=c):
                                landing = x_landing(zz, xx, right, jnp.int32(-1))
                                wait_in(from_x, xr_sem, landing, c)
                                add_in(spot(zz, xx), from_x, landing, c)

                        x_copy(right, zz, xx, c).start()

    def x_join(zz, c):
        at = spot(zz, x)
        if X == 2:
            wait_in(from_x, xr_sem, zz, c)
            add_in(at, from_x, zz, c)
        elif X > 2:
            for right in (True, False):

                @pl.when(exists[LEFT if right else RIGHT])
                def _(right=right):
                    landing = zz * (X + 1) + (x if right else X)
                    wait_in(from_x, xr_sem, landing, c)
                    add_in(at, from_x, landing, c)

    def ways(k):
        return ((True, Z - 1 - k, Z - 1 - k > z), (False, k, k < z))

    def begin():
        for zz in range(Z):
            for xx in range(X):
                if X > 2:
                    load(zz, xx).start()
            if X <= 2:
                load(zz, x).start()
        for k in range(Z - 1):
            for up, zz, here in ways(k):

                @pl.when(here)
                def _(zz=zz):
                    x_line(zz)

        x_line(z)

    def pass_on(k, c):
        for up, zz, here in ways(k):

            @pl.when(here)
            def _(up=up, zz=zz):
                if c == 0:
                    load(zz, x).wait()
                x_join(zz, c)

                @pl.when(exists[DOWN if up else UP])
                def _():
                    wait_in(from_z, zr_sem, zz, c)
                    add_in(spot(zz, x), from_z, zz, c)

                z_copy(up, zz, c).start()

    def settle(c):
        if c == 0:
            load(z, x).wait()
        x_join(z, c)

        @pl.when(exists[DOWN])
        def _():
            wait_in(from_z, zr_sem, z, c)

        @pl.when(exists[UP])
        def _():
            wait_in(from_z, zr_sem, Z, c)

        def body(i, carry):
            part = pl.ds(pl.multiple_of(i * step, step), step)
            total = mine[spot(z, x), c, part].astype(jnp.float32)
            below = from_z[z, c, part].astype(jnp.float32)
            above = from_z[Z, c, part].astype(jnp.float32)
            total = total + jnp.where(z > 0, below, 0.0)
            total = total + jnp.where(z < Z - 1, above, 0.0)
            store(c, part, total)
            return carry

        lax.fori_loop(0, rows // step, body, 0)
        done(c)

    def finish():
        for zz in range(Z):
            for c in range(chunks):
                for xx in range(X):

                    @pl.when(xx != x)
                    def _(zz=zz, xx=xx, c=c):
                        x_copy(True, zz, xx, c).wait_send()

                @pl.when(zz != z)
                def _(zz=zz, c=c):
                    z_copy(True, zz, c).wait_send()

    steps = [(start, begin)]
    for k in range(Z - 1):
        for c in range(chunks):
            steps.append(
                (start + pace * (k + (c + 1) / chunks), functools.partial(pass_on, k, c))
            )
    for c in range(chunks):
        steps.append((start + pace * (Z - 1 + (c + 1) / chunks), functools.partial(settle, c)))
    steps.append((start + pace * (Z + 2), finish))
    return steps


class Gather:
    def __init__(self, axis, block, chunks, start=0.0, pace=21.0, beside=False, turned=False):
        self.axis, self.chunks, self.start, self.pace = axis, chunks, start, pace
        self.beside, self.turned = beside, turned
        self.inputs = [block]
        self.everyone = ()
        count = lax.axis_size(axis)
        rows, width = block.shape
        shape = (rows, count * width) if beside else (count, rows, width)
        self.outputs = [(ANY, jax.ShapeDtypeStruct(shape, block.dtype))]
        self.scratch = [DMA] + gather_sems(axis, chunks - turned)
        if turned:
            self.scratch += gather_sems(axis, 1)

    def steps(self, lines, ins, outs, scratch):
        line, (x_ref,), (out_ref,) = lines[self.axis], ins, outs
        own_sem, *sems = scratch
        rows, width = x_ref.shape[0] // self.chunks, x_ref.shape[1]

        def view(origin, part):
            if self.beside:
                return out_ref.at[part, pl.ds(pl.multiple_of(origin * width, HD), width)]
            return out_ref.at[origin, part]

        own = pltpu.make_async_copy(x_ref, view(line.me, pl.ds(0, x_ref.shape[0])), own_sem)

        def part_steps(line, first, count, sems, start):
            def part(c):
                return pl.ds((first + c) * rows, rows)

            return gather_steps(
                line,
                count,
                lambda origin, c: view(origin, part(c)),
                lambda c: x_ref.at[part(c)],
                lambda c: None,
                sems,
                start,
                self.pace,
            )

        straight = self.chunks - self.turned
        steps = part_steps(line, 0, straight, sems[:2], self.start)
        if self.turned:
            steps += part_steps(Turned(line), straight, 1, sems[2:], self.start + 0.9 * self.pace)
        return [(self.start, own.start)] + steps + [(steps[-1][0], own.wait)]


class Scatter:
    def __init__(self, axis, terms, chunks, start=0.0, pace=21.0, turned=False, column=False):
        self.axis, self.chunks, self.start, self.pace = axis, chunks, start, pace
        self.turned, self.column = turned, column
        dims = grid_of(axis)
        if column:
            dims = (dims[0], 1)
        count = dims[0] * dims[1]
        rows, width = terms.shape[0] // count // chunks, terms.shape[1]
        self.inputs = [terms.reshape(count, chunks, rows, width)]
        self.everyone = ()
        self.outputs = [(VMEM, jax.ShapeDtypeStruct((chunks * rows, width), jnp.float32))]
        self.scratch = scatter_scratch(dims, chunks - turned, rows, width, terms.dtype)
        self.half = len(self.scratch)
        if turned:
            self.scratch += scatter_scratch(dims[::-1], 1, rows, width, terms.dtype)

    def steps(self, lines, ins, outs, scratch):
        (p_ref,), (out_ref,) = ins, outs
        rows = p_ref.shape[2]

        def part_steps(line, first, count, scratch, start):
            def store(c, part, total):
                at = pl.multiple_of((first + c) * rows + part.start, STEP)
                out_ref[pl.ds(at, part.size)] = total

            return scatter_steps(
                line,
                count,
                lambda slot: p_ref.at[slot, pl.ds(first, count)],
                lambda slot, c: p_ref.at[slot, first + c],
                scratch,
                store,
                lambda c: None,
                start,
                self.pace,
            )

        line, straight = lines[self.axis], self.chunks - self.turned
        if self.column:
            line = Column(line)
        steps = part_steps(line, 0, straight, scratch[: self.half], self.start)
        if self.turned:
            steps += part_steps(Turned(line), straight, 1, scratch[self.half :], self.start + 0.01)
        return steps


class Spread:
    def __init__(self, weights, window, first, start=0.0, pace=6.0):
        self.inputs = list(weights)
        self.window, self.first, self.start, self.pace = window, first, start, pace
        self.everyone = ("shard",)
        shards, replicas = lax.axis_size("shard"), lax.axis_size("replica")
        self.part = weights[0].shape[0] // replicas
        wide = len(weights) * window
        shape = (shards, replicas, self.part, wide)
        self.outputs = [(ANY, jax.ShapeDtypeStruct(shape, weights[0].dtype))]
        self.scratch = [
            DMA((len(weights),)),
            DMA((len(weights), shards)),
            DMA((len(weights), shards)),
        ] + gather_sems("replica", shards)

    def steps(self, lines, ins, outs, scratch):
        own_sem, deal_send, deal_recv, *sems = scratch
        (out_ref,) = outs
        group, copies = lines["shard"], lines["replica"]
        rows = pl.ds(pl.multiple_of(copies.me * self.part, self.part), self.part)
        kinds = range(len(ins))

        def source(kind, target):
            return ins[kind].at[rows, pl.ds(pl.multiple_of(self.first(target), 128), self.window)]

        def landing(kind, origin):
            return out_ref.at[origin, copies.me, :, pl.ds(kind * self.window, self.window)]

        def own(kind):
            return pltpu.make_async_copy(
                source(kind, group.me), landing(kind, group.me), own_sem.at[kind]
            )

        def deal(kind, k):
            target = group.other(k)
            return remote(
                source(kind, target),
                landing(kind, group.me),
                deal_send.at[kind, k],
                deal_recv.at[kind, group.me],
                {"shard": target},
            )

        def begin():
            for k in range(1, group.count):
                for kind in kinds:
                    deal(kind, k).start()
            for kind in kinds:
                own(kind).start()

        def ready(c):
            @pl.when(c == group.me)
            def _():
                for kind in kinds:
                    own(kind).wait()

            @pl.when(c != group.me)
            def _():
                for kind in kinds:
                    in_place(landing(kind, c), deal_recv.at[kind, c]).wait()

        def finish():
            for k in range(1, group.count):
                for kind in kinds:
                    deal(kind, k).wait_send()

        steps = gather_steps(
            copies,
            group.count,
            lambda origin, c: out_ref.at[c, origin],
            lambda c: out_ref.at[c, copies.me],
            ready,
            sems,
            self.start + 2 * self.pace,
            self.pace,
        )
        return [(self.start, begin)] + steps + [(steps[-1][0], finish)]


class Trade:
    def __init__(self, block, start=0.0, pace=6.0):
        self.inputs = [block]
        self.start, self.pace = start, pace
        self.everyone = ()
        shards, part, width = block.shape
        shape = (shards, lax.axis_size("replica"), part, width)
        self.outputs = [(ANY, jax.ShapeDtypeStruct(shape, block.dtype))]
        self.scratch = [DMA] + gather_sems("replica", shards)

    def steps(self, lines, ins, outs, scratch):
        own_sem, *sems = scratch
        (x_ref,), (out_ref,) = ins, outs
        copies = lines["replica"]
        own = pltpu.make_async_copy(x_ref, out_ref.at[:, copies.me], own_sem)
        steps = gather_steps(
            copies,
            x_ref.shape[0],
            lambda origin, c: out_ref.at[c, origin],
            lambda c: x_ref.at[c],
            lambda c: None,
            sems,
            self.start,
            self.pace,
        )
        return [(self.start, own.start)] + steps + [(steps[-1][0], own.wait)]


class Sum:
    def __init__(self, terms, start=0.0, pace=6.0):
        shards, replicas = lax.axis_size("shard"), lax.axis_size("replica")
        part, wide = terms.shape[0] // shards // replicas, terms.shape[1]
        self.inputs = [terms.reshape(shards, replicas, part, wide)]
        self.start, self.pace = start, pace
        self.everyone = ()
        self.outputs = [(VMEM, jax.ShapeDtypeStruct((shards, part, wide), terms.dtype))]
        self.scratch = scatter_scratch(grid_of("replica"), shards, part, wide, terms.dtype)

    def steps(self, lines, ins, outs, scratch):
        (p_ref,), (out_ref,) = ins, outs

        def store(c, part, total):
            out_ref[c, part] = total.astype(out_ref.dtype)

        return scatter_steps(
            lines["replica"],
            out_ref.shape[0],
            lambda slot: p_ref.at[:, slot],
            lambda slot, c: p_ref.at[c, slot],
            scratch,
            store,
            lambda c: None,
            self.start,
            self.pace,
        )


class Deliver:
    def __init__(self, sums, start=0.0, again=30.0, pace=24.0):
        self.inputs = [sums]
        self.start, self.again, self.pace = start, again, pace
        self.everyone = ("shard",)
        shards, replicas = lax.axis_size("shard"), lax.axis_size("replica")
        self.outputs = [(ANY, jax.ShapeDtypeStruct((replicas,) + sums.shape, sums.dtype))]
        self.scratch = [DMA, DMA((shards,)), DMA((shards,))] + gather_sems("replica", shards)

    def steps(self, lines, ins, outs, scratch):
        own_sem, send_sem, recv_sem, *sems = scratch
        (x_ref,), (out_ref,) = ins, outs
        group, copies = lines["shard"], lines["replica"]
        own = pltpu.make_async_copy(
            x_ref.at[group.me], out_ref.at[copies.me, group.me], own_sem
        )

        def deal(k):
            target = group.other(k)
            return remote(
                x_ref.at[target],
                out_ref.at[copies.me, group.me],
                send_sem.at[k],
                recv_sem.at[group.me],
                {"shard": target},
            )

        def begin():
            own.start()
            for k in range(1, group.count):
                deal(k).start()

        def ready(c):
            @pl.when(c == group.me)
            def _():
                own.wait()

            @pl.when(c != group.me)
            def _():
                in_place(out_ref.at[copies.me, c], recv_sem.at[c]).wait()

        def finish():
            for k in range(1, group.count):
                deal(k).wait_send()

        steps = gather_steps(
            copies,
            group.count,
            lambda origin, c: out_ref.at[origin, c],
            lambda c: out_ref.at[copies.me, c],
            ready,
            sems,
            self.again,
            self.pace,
        )
        return [(self.start, begin)] + steps + [(steps[-1][0], finish)]


class Total:
    def __init__(self, terms, start=0.0, pace=6.0):
        replicas = lax.axis_size("replica")
        share, wide = terms.shape[0] // replicas, terms.shape[1]
        chunks = max(n for n in (1, 2, 3, 4) if share % (n * STEP) == 0)
        rows = share // chunks
        self.inputs = [terms.reshape(replicas, chunks, rows, wide)]
        self.start, self.pace, self.chunks = start, pace, chunks
        self.everyone = ()
        kind = terms.dtype
        self.outputs = [(ANY, jax.ShapeDtypeStruct((replicas, chunks, rows, wide), kind))]
        self.scratch = [pltpu.VMEM((chunks, rows, wide), kind), DMA((chunks,))]
        self.scratch += gather_sems("replica", chunks)
        self.scratch += scatter_scratch(grid_of("replica"), chunks, rows, wide, kind)

    def steps(self, lines, ins, outs, scratch):
        (p_ref,), (out_ref,) = ins, outs
        total_ref, own_sem = scratch[:2]
        copies = lines["replica"]

        def own(c):
            return pltpu.make_async_copy(
                total_ref.at[c], out_ref.at[copies.me, c], own_sem.at[c]
            )

        def store(c, part, total):
            total_ref[c, part] = total.astype(total_ref.dtype)

        def finish():
            for c in range(self.chunks):
                own(c).wait()

        summing = scatter_steps(
            copies,
            self.chunks,
            lambda slot: p_ref.at[slot],
            lambda slot, c: p_ref.at[slot, c],
            scratch[4:],
            store,
            lambda c: own(c).start(),
            self.start,
            self.pace,
        )
        sharing = gather_steps(
            copies,
            self.chunks,
            lambda origin, c: out_ref.at[origin, c],
            lambda c: total_ref.at[c],
            lambda c: None,
            scratch[2:4],
            self.start + self.pace * (copies.Z + 2),
            self.pace,
        )
        return summing + sharing + [(sharing[-1][0], finish)]


class Small:
    def __init__(self, dealt, shared, start=0.0):
        shards, replicas = lax.axis_size("shard"), lax.axis_size("replica")
        self.inputs = [dealt, shared]
        self.start = start
        self.everyone = ("shard", "replica")
        one = dealt.shape[1:]
        self.outputs = [
            (VMEM, jax.ShapeDtypeStruct(one, jnp.float32)),
            (VMEM, jax.ShapeDtypeStruct(shared.shape, jnp.float32)),
        ]
        self.scratch = [
            pltpu.VMEM((shards,) + one, jnp.float32),
            pltpu.VMEM((replicas,) + one, jnp.float32),
            pltpu.VMEM((replicas,) + shared.shape, jnp.float32),
            DMA((shards,)), DMA((shards,)),
            DMA((2, replicas)), DMA((2, replicas)), DMA((2,)),
        ]

    def steps(self, lines, ins, outs, scratch):
        dealt, shared = ins
        out_one, out_rows = outs
        got, got_one, got_rows, send, recv, send2, recv2, own = scratch
        group, copies = lines["shard"], lines["replica"]

        def deal(k):
            target = group.other(k)
            return remote(
                dealt.at[target], got.at[group.me], send.at[k], recv.at[group.me], {"shard": target}
            )

        def share(which, k):
            buffer = (got_one, got_rows)[which]
            return remote(
                buffer.at[copies.me] if which == 0 else shared,
                buffer.at[copies.me],
                send2.at[which, k],
                recv2.at[which, copies.me],
                {"replica": copies.other(k)},
            )

        def keep():
            return pltpu.make_async_copy(dealt.at[group.me], got.at[group.me], own.at[0])

        def keep_rows():
            return pltpu.make_async_copy(shared, got_rows.at[copies.me], own.at[1])

        def begin():
            keep().start()
            keep_rows().start()
            for k in range(1, group.count):
                deal(k).start()
            for k in range(1, copies.count):
                share(1, k).start()

        def middle():
            keep().wait()
            for k in range(1, group.count):
                origin = group.other(k)
                in_place(got.at[origin], recv.at[origin]).wait()
            total = got[0]
            for s in range(1, group.count):
                total = total + got[s]
            got_one[copies.me] = total
            for k in range(1, copies.count):
                share(0, k).start()

        def end():
            keep_rows().wait()
            for k in range(1, copies.count):
                origin = copies.other(k)
                in_place(got_one.at[origin], recv2.at[0, origin]).wait()
                in_place(got_rows.at[origin], recv2.at[1, origin]).wait()
            one, rows = got_one[0], got_rows[0]
            for r in range(1, copies.count):
                one, rows = one + got_one[r], rows + got_rows[r]
            out_one[...] = one
            out_rows[...] = rows
            for k in range(1, group.count):
                deal(k).wait_send()
            for k in range(1, copies.count):
                share(0, k).wait_send()
                share(1, k).wait_send()

        return [(-0.5, begin), (self.start, middle), (self.start + 40.0, end)]


def layout_of(tasks):
    inputs, outputs, scratch, spans = [], [], [], []
    for task in tasks:
        spans.append((len(inputs), len(outputs), len(scratch)))
        inputs += task.inputs
        outputs += task.outputs
        scratch += task.scratch
    return inputs, outputs, scratch, spans


def task_steps(tasks, spans, axes, ins, outs, scratch):
    lines = {axis: Lines(axis) for axis in axes}
    everyone = {axis for task in tasks for axis in task.everyone}
    steps = []
    for task, (i, o, s) in zip(tasks, spans):
        steps += task.steps(
            lines,
            ins[i : i + len(task.inputs)],
            outs[o : o + len(task.outputs)],
            scratch[s : s + len(task.scratch)],
        )
    steps.sort(key=lambda step: step[0])
    return [(-1.0, lambda: greet(list(lines.values()), everyone))] + steps


def exchange(tasks, axes, ident):
    inputs, outputs, scratch, spans = layout_of(tasks)

    def kernel(*refs):
        ins = refs[: len(inputs)]
        outs = refs[len(inputs) : len(inputs) + len(outputs)]
        rest = refs[len(inputs) + len(outputs) :]
        for _, step in task_steps(tasks, spans, axes, ins, outs, rest):
            step()

    return pl.pallas_call(
        kernel,
        in_specs=[ANY] * len(inputs),
        out_specs=[spec for spec, _ in outputs],
        out_shape=[shape for _, shape in outputs],
        scratch_shapes=scratch,
        compiler_params=pltpu.CompilerParams(
            collective_id=ident, has_side_effects=True, vmem_limit_bytes=60 * 1024 * 1024
        ),
    )(*inputs)


HD = 128
TAPS = 4
KINDS = 3


def dot_nn(a, b):
    return lax.dot_general(
        a.astype(jnp.bfloat16),
        b.astype(jnp.bfloat16),
        (((1,), (0,)), ((), ())),
        preferred_element_type=jnp.float32,
    )


def dot_nt(a, b):
    return lax.dot_general(
        a.astype(jnp.bfloat16),
        b.astype(jnp.bfloat16),
        (((1,), (1,)), ((), ())),
        preferred_element_type=jnp.float32,
    )


def dot_tn(a, b):
    return lax.dot_general(
        a.astype(jnp.bfloat16),
        b.astype(jnp.bfloat16),
        (((0,), (0,)), ((), ())),
        preferred_element_type=jnp.float32,
    )


def time_of(shape, dim, lanes):
    index = lax.broadcasted_iota(jnp.int32, shape, dim)
    return lax.rem(index, 8) * lanes + lax.div(index, 8)


def lower_inverses(lowers, lanes):
    size = lowers[0].shape[0]
    row_t = time_of((size, size), 0, lanes)
    col_t = time_of((size, size), 1, lanes)
    eye = jnp.where(row_t == col_t, 1.0, 0.0)

    def same(width):
        return lax.div(row_t, width) == lax.div(col_t, width)

    first = [jnp.where(same(8), a, 0.0) for a in lowers]
    second = [dot_nn(f, f) for f in first]
    inverse = [eye + f + s + dot_nn(f, s) for f, s in zip(first, second)]
    fourth = [dot_nn(s, s) for s in second]
    inverse = [t + dot_nn(t, f) for t, f in zip(inverse, fourth)]
    width = 16
    while width <= size:
        fresh = same(width) & jnp.logical_not(same(width // 2))
        left = [dot_nn(t, jnp.where(fresh, a, 0.0)) for t, a in zip(inverse, lowers)]
        inverse = [t + dot_nn(l, t) for t, l in zip(inverse, left)]
        width *= 2
    return inverse


def rounded(values):
    return values.astype(jnp.bfloat16).astype(jnp.float32)


def sigmoid(values):
    return 1.0 / (1.0 + jnp.exp(-values))


def unit_scale(pre):
    return lax.rsqrt(jnp.sum(pre * pre, axis=1, keepdims=True) + 1e-6)


def mean_scale(values):
    return lax.rsqrt(jnp.mean(values * values, axis=1, keepdims=True) + 1e-5)


def delta_forward(
    lanes, heads, group, proj_ref, taps_ref, gain_ref, low_ref, off_ref, rem_ref,
    zed_ref, mixed_ref, sums_ref, s_ref, t_ref, mk_ref, mv_ref, u_ref,
    state, last, unit,
):
    size = lanes * 8
    rows = group * 8
    wide = heads * HD
    scale = HD ** (-0.5)

    @pl.when(pl.program_id(0) == 0)
    def _():
        state[...] = jnp.zeros_like(state)
        last[...] = jnp.zeros_like(last)

    top = lax.broadcasted_iota(jnp.int32, (rows, HD), 0) == 0
    for kind in range(KINDS):
        for h in range(heads):
            cols = pl.ds(kind * wide + h * HD, HD)
            signal = [rounded(proj_ref[s, :, cols]) for s in range(lanes)]
            moved = {}
            for back in range(1, TAPS):
                lane = lanes - back
                edge = last[kind * heads + h, back, 0:1]
                moved[lane] = jnp.where(top, edge, pltpu.roll(signal[lane], 1, 0))
            for back in range(1, TAPS):
                last[kind * heads + h, back, 0:1] = signal[lanes - back][rows - 1 : rows]
            for s in range(lanes):
                off = off_ref[s]
                total = signal[s] * taps_ref[kind * TAPS : kind * TAPS + 1, h * HD : (h + 1) * HD]
                for hop in range(1, TAPS):
                    earlier = signal[s - hop] if s >= hop else moved[lanes + s - hop]
                    tap = taps_ref[kind * TAPS + hop : kind * TAPS + hop + 1, h * HD : (h + 1) * HD]
                    total = total + jnp.where(off >= hop, earlier, 0.0) * tap
                sums_ref[s, :, cols] = total
                pre = total * sigmoid(total)
                if kind < 2:
                    pre = pre * unit_scale(pre)
                unit[s, :, cols] = pre

    row_t = time_of((size, size), 0, lanes)
    col_t = time_of((size, size), 1, lanes)
    local_t = time_of((size, HD), 0, lanes).astype(jnp.float32)
    pairs = [(g, h) for g in range(group) for h in range(heads)]

    def span(g):
        return pl.ds(g * 8, 8)

    def flat(ref, g, first, count=HD):
        return ref[:, span(g), first : first + count].reshape(size, count)

    gates = {}
    for g in range(group):
        logits = flat(proj_ref, g, 4 * wide)
        strength = sigmoid(rounded(logits))
        for h in range(heads):
            gates[g, h] = jnp.broadcast_to(strength[:, h : h + 1], (size, HD))
    keys = {p: flat(unit, p[0], wide + p[1] * HD) for p in pairs}
    kbs = {p: gates[p] * keys[p] for p in pairs}
    lows = {g: low_ref[g].astype(jnp.float32) for g in range(group)}
    lowers = [
        -jnp.where(row_t == col_t, 0.0, lows[p[0]]) * dot_nt(kbs[p], keys[p]) for p in pairs
    ]
    inverses = dict(zip(pairs, lower_inverses(lowers, lanes)))
    mks = {p: dot_nn(inverses[p], kbs[p]) for p in pairs}
    mvs = {
        p: dot_nn(inverses[p], gates[p] * flat(unit, p[0], 2 * wide + p[1] * HD))
        for p in pairs
    }
    queries = {p: flat(unit, p[0], p[1] * HD) for p in pairs}
    scores = {p: lows[p[0]] * dot_nt(queries[p], keys[p]) for p in pairs}
    for g, h in pairs:
        t_ref[g, h] = inverses[g, h].astype(t_ref.dtype)
        mk_ref[g, h] = mks[g, h].astype(mk_ref.dtype)
        mv_ref[g, h] = mvs[g, h].astype(mv_ref.dtype)
    for g in range(group):
        carry = jnp.where(flat(off_ref, g, 0) > local_t, 1.0, 0.0)
        keep = jnp.where(flat(rem_ref, g, 0) + local_t >= size, 1.0, 0.0)
        for h in range(heads):
            p = (g, h)
            held = state[h]
            s_ref[g, h] = held.astype(s_ref.dtype)
            u = mvs[p] - carry * dot_nn(mks[p], held)
            u_ref[g, h] = u.astype(u_ref.dtype)
            state[h] = (carry[0:1] * keep[0:1]) * held + dot_tn(keys[p], keep * u)
            out = (carry * dot_nn(queries[p], held) + dot_nn(scores[p], u)) * scale
            mixed = rounded(out)
            gate = flat(proj_ref, g, 3 * wide + h * HD)
            zed = mixed * mean_scale(mixed) * gain_ref[...] * (gate * sigmoid(gate))
            mixed_ref[:, span(g), h * HD : (h + 1) * HD] = mixed.reshape(lanes, 8, HD).astype(
                mixed_ref.dtype
            )
            zed_ref[:, span(g), h * HD : (h + 1) * HD] = zed.reshape(lanes, 8, HD).astype(
                zed_ref.dtype
            )


def delta_backward(
    lanes, heads, group, proj_ref, sums_ref, mixed_ref, dzed_ref, taps_ref, gain_ref,
    low_ref, off_ref, rem_ref, s_ref, t_ref, mk_ref, mv_ref, u_ref,
    dproj_ref, gtaps_ref, ghead_ref,
    state, edge, edge_off, errs, taps_sum, head_sum,
):
    size = lanes * 8
    rows = group * 8
    wide = heads * HD
    scale = HD ** (-0.5)

    @pl.when(pl.program_id(0) == 0)
    def _():
        state[...] = jnp.zeros_like(state)
        edge[...] = jnp.zeros_like(edge)
        edge_off[...] = jnp.zeros_like(edge_off)
        taps_sum[...] = jnp.zeros_like(taps_sum)
        head_sum[...] = jnp.zeros_like(head_sum)

    row_t = time_of((size, size), 0, lanes)
    col_t = time_of((size, size), 1, lanes)
    local_t = time_of((size, HD), 0, lanes).astype(jnp.float32)
    lane_id = lax.broadcasted_iota(jnp.int32, (size, HD), 1)
    pairs = [(g, h) for g in range(group) for h in range(heads)]

    def span(g):
        return pl.ds(g * 8, 8)

    def flat(ref, g, first, count=HD):
        return ref[:, span(g), first : first + count].reshape(size, count)

    def put(ref, g, first, value):
        ref[:, span(g), first : first + HD] = value.reshape(lanes, 8, HD).astype(ref.dtype)

    gain = gain_ref[...]
    d_out, q, k, v, beta = {}, {}, {}, {}, {}
    pre, scales, slopes = {}, {}, {}
    head_total = jnp.zeros((size, HD), jnp.float32)
    strengths = {}
    carries, keeps, lows = {}, {}, {}
    for g in range(group):
        carries[g] = jnp.where(flat(off_ref, g, 0) > local_t, 1.0, 0.0)
        keeps[g] = jnp.where(flat(rem_ref, g, 0) + local_t >= size, 1.0, 0.0)
        lows[g] = low_ref[g].astype(jnp.float32)
        strengths[g] = sigmoid(rounded(flat(proj_ref, g, 4 * wide)))
    for g, h in pairs:
        p = (g, h)
        mixed = flat(mixed_ref, g, h * HD).astype(jnp.float32)
        gate = flat(proj_ref, g, 3 * wide + h * HD)
        dzed = flat(dzed_ref, g, h * HD)
        s = sigmoid(gate)
        r = mean_scale(mixed)
        through = dzed * (gate * s)
        head_total = head_total + through * mixed * r
        inner = jnp.mean(mixed * gain * through, axis=1, keepdims=True)
        d_mixed = rounded(r * gain * through - mixed * (r * r * r) * inner)
        put(dproj_ref, g, 3 * wide + h * HD, dzed * (mixed * r * gain) * (s * (1.0 + gate * (1.0 - s))))
        d_out[p] = d_mixed * scale
        for kind, store in ((0, q), (1, k), (2, v)):
            total = flat(sums_ref, g, kind * wide + h * HD)
            s = sigmoid(total)
            value = total * s
            slopes[kind, g, h] = s * (1.0 + total * (1.0 - s))
            if kind < 2:
                pre[kind, g, h] = value
                scales[kind, g, h] = unit_scale(value)
                value = value * scales[kind, g, h]
            store[p] = value
        beta[p] = jnp.broadcast_to(strengths[g][:, h : h + 1], (size, HD))
    head_sum[...] += head_total

    scores = {p: lows[p[0]] * dot_nt(q[p], k[p]) for p in pairs}
    du = {p: dot_tn(scores[p], d_out[p]) for p in pairs}
    ds = {p: lows[p[0]] * dot_nt(d_out[p], u_ref[p[0], p[1]]) for p in pairs}
    cdo = {p: carries[p[0]] * d_out[p] for p in pairs}
    dq = {p: dot_nt(cdo[p], s_ref[p[0], p[1]]) + dot_nn(ds[p], k[p]) for p in pairs}
    dk = {p: dot_tn(ds[p], q[p]) for p in pairs}
    lift = {p: dot_tn(q[p], cdo[p]) for p in pairs}
    later = {}
    for g in reversed(range(group)):
        for h in range(heads):
            p = (g, h)
            later[p] = state[h]
            du[p] = du[p] + keeps[g] * dot_nn(k[p], later[p])
            mk = carries[g] * mk_ref[g, h].astype(jnp.float32)
            state[h] = (carries[g][0:1] * keeps[g][0:1]) * later[p] + lift[p] - dot_tn(mk, du[p])
    for p in pairs:
        dk[p] = dk[p] + dot_nt(keeps[p[0]] * u_ref[p[0], p[1]].astype(jnp.float32), later[p])
    dmk = {p: -carries[p[0]] * dot_nt(du[p], s_ref[p[0], p[1]]) for p in pairs}
    xx = {p: dot_tn(t_ref[p[0], p[1]], dmk[p]) for p in pairs}
    yy = {p: dot_tn(t_ref[p[0], p[1]], du[p]) for p in pairs}
    da = {
        p: jnp.where(row_t == col_t, 0.0, lows[p[0]])
        * (dot_nt(xx[p], mk_ref[p[0], p[1]]) + dot_nt(yy[p], mv_ref[p[0], p[1]]))
        for p in pairs
    }
    dkb = {p: xx[p] - dot_nn(da[p], k[p]) for p in pairs}
    dk = {p: dk[p] - dot_tn(da[p], beta[p] * k[p]) + beta[p] * dkb[p] for p in pairs}
    for g in range(group):
        d_logits = jnp.zeros((size, HD), jnp.float32)
        for h in range(heads):
            p = (g, h)
            db = jnp.sum(dkb[p] * k[p] + yy[p] * v[p], axis=1, keepdims=True)
            d_logits = d_logits + jnp.where(lane_id == h, db * beta[p] * (1.0 - beta[p]), 0.0)
            for kind, grad in ((0, dq[p]), (1, dk[p])):
                r, raw = scales[kind, g, h], pre[kind, g, h]
                inner = jnp.sum(raw * grad, axis=1, keepdims=True)
                err = (r * grad - raw * (r * r * r) * inner) * slopes[kind, g, h]
                put(errs, g, kind * wide + h * HD, err)
            put(errs, g, 2 * wide + h * HD, beta[p] * yy[p] * slopes[2, g, h])
        put(dproj_ref, g, 4 * wide, d_logits)

    bottom = lax.broadcasted_iota(jnp.int32, (rows, HD), 0) == rows - 1
    for kind in range(KINDS):
        for h in range(heads):
            at = kind * wide + h * HD
            cols = pl.ds(at, HD)
            err = [errs[s, :, cols] for s in range(lanes)]
            taps = [
                taps_ref[kind * TAPS + hop : kind * TAPS + hop + 1, h * HD : (h + 1) * HD]
                for hop in range(TAPS)
            ]
            sums = [jnp.zeros((rows, HD), jnp.float32) for _ in range(TAPS)]
            live = {}
            for hop in range(1, TAPS):
                for s in range(lanes):
                    live[hop, s] = jnp.where(off_ref[s] >= hop, err[s], 0.0)
            for hop in range(1, TAPS):
                for s in range(hop):
                    row = jnp.where(edge_off[s, 0:1] >= hop, edge[kind * heads + h, s, 0:1], 0.0)
                    live[hop, lanes + s] = jnp.where(
                        bottom, row, pltpu.roll(live[hop, s], rows - 1, 0)
                    )
            for s in range(lanes):
                signal = rounded(proj_ref[s, :, cols])
                total = err[s] * taps[0]
                sums[0] = sums[0] + err[s] * signal
                for hop in range(1, TAPS):
                    total = total + live[hop, s + hop] * taps[hop]
                    sums[hop] = sums[hop] + live[hop, s + hop] * signal
                dproj_ref[s, :, cols] = total.astype(dproj_ref.dtype)
            for s in range(TAPS - 1):
                edge[kind * heads + h, s, 0:1] = err[s][0:1]
            for hop in range(TAPS):
                folded = sums[hop].reshape(group, 8, HD)
                taps_sum[kind * TAPS + hop, :, h * HD : (h + 1) * HD] += jnp.sum(folded, axis=0)
    for s in range(TAPS - 1):
        edge_off[s, 0:1] = off_ref[s][0:1]

    @pl.when(pl.program_id(0) == pl.num_programs(0) - 1)
    def _():
        gtaps_ref[...] = jnp.sum(taps_sum[...], axis=1)
        ghead_ref[...] = jnp.sum(head_sum[...], axis=0, keepdims=True)


def mixer_specs(lanes, heads, group, flip):
    size = lanes * 8
    at = (lambda i: flip - 1 - i) if flip else (lambda i: i)

    def token(width):
        return pl.BlockSpec((lanes, 8 * group, width), lambda i: (0, at(i), 0))

    def saved(first, second):
        return pl.BlockSpec((group, heads, first, second), lambda i: (at(i), 0, 0, 0))

    square = pl.BlockSpec((group, size, size), lambda i: (at(i), 0, 0))
    return token, saved, square


def fixed(shape):
    return pl.BlockSpec(shape, lambda i: (0,) * len(shape))


def saved_shapes(lanes, heads, blocks):
    size = lanes * 8
    kind = jnp.bfloat16
    return [
        jax.ShapeDtypeStruct((blocks, heads, HD, HD), kind),
        jax.ShapeDtypeStruct((blocks, heads, size, size), kind),
        jax.ShapeDtypeStruct((blocks, heads, size, HD), kind),
        jax.ShapeDtypeStruct((blocks, heads, size, HD), kind),
        jax.ShapeDtypeStruct((blocks, heads, size, HD), kind),
    ]


def mixer_forward(proj, taps, gain, low, off, rem, heads, group=4):
    lanes, tokens, width = proj.shape
    blocks, wide = tokens // 8, heads * HD
    size = lanes * 8
    token, saved, square = mixer_specs(lanes, heads, group, 0)
    return pl.pallas_call(
        functools.partial(delta_forward, lanes, heads, group),
        grid=(blocks // group,),
        in_specs=[token(width), fixed(taps.shape), fixed(gain.shape), square, token(HD), token(HD)],
        out_specs=[
            token(wide), token(wide), token(KINDS * wide),
            saved(HD, HD), saved(size, size), saved(size, HD), saved(size, HD), saved(size, HD),
        ],
        out_shape=[
            jax.ShapeDtypeStruct((lanes, tokens, wide), jnp.bfloat16),
            jax.ShapeDtypeStruct((lanes, tokens, wide), jnp.bfloat16),
            jax.ShapeDtypeStruct((lanes, tokens, KINDS * wide), jnp.float32),
        ] + saved_shapes(lanes, heads, blocks),
        scratch_shapes=[
            pltpu.VMEM((heads, HD, HD), jnp.float32),
            pltpu.VMEM((KINDS * heads, TAPS, 8, HD), jnp.float32),
            pltpu.VMEM((lanes, 8 * group, KINDS * wide), jnp.float32),
        ],
        compiler_params=pltpu.CompilerParams(vmem_limit_bytes=48 * 1024 * 1024),
        cost_estimate=pl.CostEstimate(flops=35 * 10**9, bytes_accessed=40 * 10**6, transcendentals=0),
    )(proj, taps, gain, low, off, rem)


def mixer_backward(
    proj, sums, mixed, dzed, taps, gain, low, off, rem, saves, heads, group=4
):
    lanes, tokens, width = proj.shape
    blocks, wide = tokens // 8, heads * HD
    size = lanes * 8
    token, saved, square = mixer_specs(lanes, heads, group, blocks // group)
    return pl.pallas_call(
        functools.partial(delta_backward, lanes, heads, group),
        grid=(blocks // group,),
        in_specs=[
            token(width), token(KINDS * wide), token(wide), token(wide),
            fixed(taps.shape), fixed(gain.shape), square, token(HD), token(HD),
            saved(HD, HD), saved(size, size), saved(size, HD), saved(size, HD), saved(size, HD),
        ],
        out_specs=[token(width), fixed(taps.shape), fixed(gain.shape)],
        out_shape=[
            jax.ShapeDtypeStruct((lanes, tokens, width), jnp.bfloat16),
            jax.ShapeDtypeStruct(taps.shape, jnp.float32),
            jax.ShapeDtypeStruct(gain.shape, jnp.float32),
        ],
        scratch_shapes=[
            pltpu.VMEM((heads, HD, HD), jnp.float32),
            pltpu.VMEM((KINDS * heads, TAPS, 8, HD), jnp.float32),
            pltpu.VMEM((TAPS, 8, HD), jnp.float32),
            pltpu.VMEM((lanes, 8 * group, KINDS * wide), jnp.float32),
            pltpu.VMEM((taps.shape[0], 8, wide), jnp.float32),
            pltpu.VMEM((size, HD), jnp.float32),
        ],
        compiler_params=pltpu.CompilerParams(vmem_limit_bytes=48 * 1024 * 1024),
        cost_estimate=pl.CostEstimate(flops=35 * 10**9, bytes_accessed=40 * 10**6, transcendentals=0),
    )(proj, sums, mixed, dzed, taps, gain, low, off, rem, *saves)


def segment_masks(lengths_grid, order_row, lanes, tokens):
    slots = order_row.shape[0]
    flat = lengths_grid.reshape(slots)
    first = lax.broadcasted_iota(jnp.int32, (slots, slots), 0)
    second = lax.broadcasted_iota(jnp.int32, (slots, slots), 1)
    run_len = jnp.sum(jnp.where(order_row[:, None] == second, flat[None, :], 0), axis=1)
    ends = jnp.sum(jnp.where(first >= second, run_len[None, :], 0), axis=1)
    starts = ends - run_len
    size = lanes * 8
    blocks = tokens // 8
    lane = lax.broadcasted_iota(jnp.int32, (lanes, tokens), 0)
    step = lax.broadcasted_iota(jnp.int32, (lanes, tokens), 1)
    place = step * lanes + lane
    inside = (starts[:, None, None] <= place[None]) & (place[None] < ends[:, None, None])
    start_at = jnp.sum(jnp.where(inside, starts[:, None, None], 0), axis=0)
    end_at = jnp.sum(jnp.where(inside, ends[:, None, None], 0), axis=0)

    def blocked(values):
        return values.reshape(lanes, blocks, 8).transpose(1, 0, 2).reshape(blocks, size)

    start_b, place_b = blocked(start_at), blocked(place)
    low = (start_b[:, :, None] == start_b[:, None, :]) & (place_b[:, :, None] >= place_b[:, None, :])

    def spread(values):
        return jnp.broadcast_to(values.astype(jnp.float32)[:, :, None], (lanes, tokens, HD))

    return low.astype(jnp.bfloat16), spread(place - start_at), spread(end_at - place)


def project(left_side, right_side):
    return jnp.dot(left_side, right_side, preferred_element_type=jnp.float32)


def times_t(left_side, right_side):
    return lax.dot_general(
        left_side, right_side, (((1,), (1,)), ((), ())), preferred_element_type=jnp.float32
    )


def contract_rows(left_side, right_side):
    return lax.dot_general(
        left_side, right_side, (((0,), (0,)), ((), ())), preferred_element_type=jnp.float32
    )


def rms(values, gain, eps):
    return values * lax.rsqrt(jnp.mean(values * values, axis=-1, keepdims=True) + eps) * gain


def rms_back(values, gain, eps, grad):
    r = lax.rsqrt(jnp.mean(values * values, axis=-1, keepdims=True) + eps)
    inner = jnp.mean(values * gain * grad, axis=-1, keepdims=True)
    return r * gain * grad - values * (r * r * r) * inner, grad * values * r


def deal(stacked):
    return lax.all_to_all(stacked, "shard", split_axis=0, concat_axis=0, tiled=True)


def cross(blocks):
    shards = lax.axis_size("shard")
    return lax.ppermute(blocks, "shard", [(s, s ^ 1) for s in range(shards)])


def column_windows(columns, shards):
    own = columns // shards
    tiles = columns // HD
    width = 1
    while any(min(s * own // HD, tiles - width) * HD + width * HD < (s + 1) * own for s in range(shards)):
        width += 1

    def first(s):
        if isinstance(s, int):
            return min(s * own // HD, tiles - width) * HD
        return jnp.minimum(lax.div(s * own, HD), tiles - width) * HD

    return first, width * HD


def place_windows(kinds, shards, columns, window, first, own, in_ref, *out_refs):
    for kind, out_ref in zip(range(kinds), out_refs):
        for tile in range(columns // HD):
            total = None
            for s in range(shards):
                low = max(tile * HD, s * own)
                high = min((tile + 1) * HD, (s + 1) * own)
                if low < high:
                    at = kind * window + tile * HD - first(s)
                    term = in_ref[0, s, :, at : at + HD].astype(jnp.float32)
                    total = term if total is None else total + term
            out_ref[:, tile * HD : (tile + 1) * HD] = total


def widen(collected, kinds, columns, window, first):
    replicas, shards, part, wide = collected.shape
    return pl.pallas_call(
        functools.partial(place_windows, kinds, shards, columns, window, first, columns // shards),
        grid=(replicas,),
        in_specs=[pl.BlockSpec((1, shards, part, wide), lambda i: (i, 0, 0, 0))],
        out_specs=[pl.BlockSpec((part, columns), lambda i: (i, 0))] * kinds,
        out_shape=[jax.ShapeDtypeStruct((replicas * part, columns), jnp.float32)] * kinds,
        compiler_params=pltpu.CompilerParams(vmem_limit_bytes=48 * 1024 * 1024),
    )(collected)


def body(
    layer_input,
    out_cotangent,
    seq_lengths,
    seq_order,
    w_query,
    w_key,
    w_value,
    w_beta,
    w_outgate,
    w_output,
    conv_query,
    conv_key,
    conv_value,
    attn_gain,
    head_gain,
    mlp_gain,
    w_gate,
    w_up,
    w_down,
):
    bf16, f32 = jnp.bfloat16, jnp.float32
    shards = lax.axis_size("shard")
    shard = lax.axis_index("shard")
    both, group = ("shard", "replica"), ("shard",)
    rows, width = layer_input.shape
    tokens = shards * rows
    weight_rows = w_query.shape[0]
    own = w_output.shape[0]
    heads = own // HD
    hidden_own = w_down.shape[0]
    ffn = w_gate.shape[1]
    ffn_first, ffn_window = column_windows(ffn, shards)
    col_first, col_window = column_windows(width, shards)
    shift = shard * hidden_own - ffn_first(shard)

    total_heads = w_beta.shape[1]
    head_part = jnp.pad(head_gain, (0, weight_rows - head_gain.shape[0]))
    little = jnp.concatenate([w_beta, jnp.stack([attn_gain, mlp_gain, head_part], axis=1)], axis=1)
    little = jnp.pad(little, ((0, 0), (0, HD - little.shape[1])))
    attn_weights, all_source, little = exchange(
        [
            Spread((w_query, w_key, w_value, w_outgate), col_window, col_first, -0.5, 12.0),
            Gather("shard", layer_input, 8, turned=True),
            Gather("shard", little, 1, 0.0, 20.0),
        ],
        both,
        0,
    )
    full_attn_gain = little[:, :, total_heads].reshape(width).astype(f32)
    full_mlp_gain = little[:, :, total_heads + 1].reshape(width).astype(f32)
    head_row = little[:, : head_gain.shape[0], total_heads + 2].reshape(1, HD).astype(f32)
    beta = lax.dynamic_slice_in_dim(little.reshape(width, HD), shard * heads, heads, axis=1)
    attn_weights = jnp.concatenate(
        [attn_weights.reshape(width, 4 * own), jnp.pad(beta, ((0, 0), (0, HD - heads)))], axis=1
    )
    replicas = lax.axis_size("replica")
    part = weight_rows // replicas
    at = lax.axis_index("replica") * part
    windows = [
        lax.slice_in_dim(w, ffn_first(s), ffn_first(s) + ffn_window, axis=1)
        for s in range(shards)
        for w in (
            lax.dynamic_slice_in_dim(w_gate, at, part),
            lax.dynamic_slice_in_dim(w_up, at, part),
        )
    ]
    mlp_weights = jnp.stack(
        [jnp.concatenate(windows[2 * s : 2 * s + 2], axis=1) for s in range(shards)]
    )
    full_output = jnp.broadcast_to(
        lax.dynamic_slice_in_dim(w_output, at, part)[None], (shards, part, width)
    )
    later_weights = jnp.concatenate([mlp_weights, full_output], axis=2)
    later_weights, all_source = lax.optimization_barrier((later_weights, all_source))
    later_weights = deal(later_weights)
    mlp_weights = later_weights[..., : 2 * ffn_window]
    full_output = later_weights[..., 2 * ffn_window :]
    low, off, rem = segment_masks(seq_lengths[0], seq_order[0], shards, rows)

    source = layer_input.astype(f32)
    all_source = all_source.reshape(tokens, width).astype(f32)
    normed = rms(all_source, full_attn_gain, 1e-6).astype(bf16)
    projected = project(normed, attn_weights).reshape(shards, rows, -1)
    taps = jnp.concatenate([conv_query, conv_key, conv_value], axis=0).astype(f32)
    zed, mixed, sums, *saves = mixer_forward(projected, taps, head_row, low, off, rem, heads)
    all_zed, mlp_weights, full_output, dy = exchange(
        [
            Gather("shard", zed.reshape(tokens, own), 8, 0.0, 21.0, True, True),
            Trade(mlp_weights, 0.2, 31.0),
            Trade(full_output, 0.1, 42.0),
            Gather("shard", out_cotangent, 8, 80.0, 21.0, turned=True),
        ],
        both,
        2,
    )
    zed = zed.reshape(tokens, own)
    mlp_weights = mlp_weights.reshape(width, 2 * ffn_window)
    dy = dy.reshape(tokens, width)
    all_hidden = all_source + project(all_zed, full_output.reshape(width, width))
    mlp_in = rms(all_hidden, full_mlp_gain, 1e-6).astype(bf16)
    hidden = lax.dynamic_slice_in_dim(all_hidden, shard * rows, rows)
    w_down = lax.dynamic_update_slice(jnp.zeros((ffn_window, width), bf16), w_down, (shift, 0))
    lin = project(mlp_in, mlp_weights)
    gate_lin, up_lin = lin[:, :ffn_window], lin[:, ffn_window:]
    s = jax.nn.sigmoid(gate_lin)
    product = (gate_lin * s * up_lin).astype(bf16)
    d_product = times_t(dy, w_down)
    d_gate = (d_product * up_lin * s * (1.0 + gate_lin * (1.0 - s))).astype(bf16)
    d_up = (d_product * gate_lin * s).astype(bf16)
    d_lin = jnp.concatenate([d_gate, d_up], axis=1)
    g_down = contract_rows(product, dy).astype(bf16)
    g_lin = contract_rows(mlp_in, d_lin).astype(bf16)
    d_mlp_in, g_lin, g_down = exchange(
        [
            Scatter("shard", times_t(d_lin, mlp_weights).astype(bf16), 4),
            Sum(g_lin, 0.5, 20.0),
            Total(g_down, 0.7, 16.0),
        ],
        both,
        4,
    )
    d_hidden_norm, g_mlp_rows = rms_back(hidden, full_mlp_gain, 1e-6, d_mlp_in)
    d_hidden = out_cotangent.astype(f32) + d_hidden_norm

    (d_attn,) = exchange(
        [Gather("shard", d_hidden.astype(bf16), 8, turned=True)], group, 5
    )
    g_lin, d_attn = lax.optimization_barrier((g_lin, d_attn))
    g_lin = deal(g_lin)
    d_attn = d_attn.reshape(tokens, width)
    g_output = contract_rows(zed, d_attn).astype(bf16)
    d_zed = times_t(d_attn, w_output).reshape(shards, rows, own)
    d_proj, g_taps, g_head = mixer_backward(
        projected, sums, mixed, d_zed, taps, head_row, low, off, rem, saves, heads
    )
    d_proj = d_proj.reshape(tokens, -1)
    g_proj = contract_rows(normed, d_proj).astype(bf16)
    d_normed, g_proj, g_output, g_lin = exchange(
        [
            Scatter("shard", times_t(d_proj, attn_weights).astype(bf16), 4),
            Sum(g_proj, 0.5, 16.0),
            Total(g_output, 0.7, 14.0),
            Gather("replica", g_lin.reshape(-1, 2 * ffn_window), 4, 0.3, 31.0),
        ],
        both,
        6,
    )
    d_source, g_attn_rows = rms_back(source, full_attn_gain, 1e-6, d_normed)

    def dealt(values):
        return values.reshape(shards, -1)

    small = jnp.concatenate(
        [dealt(jnp.sum(g_attn_rows, axis=0)), dealt(jnp.sum(g_mlp_rows, axis=0)), dealt(g_head)], axis=1
    )
    small = jnp.pad(small, ((0, 0), (0, -small.shape[1] % HD)))
    small = jnp.broadcast_to(small[:, None, :], (shards, 8, small.shape[1]))
    out_terms, g_proj, small, g_taps = exchange(
        [
            Scatter("shard", project(product, w_down).astype(bf16), 4),
            Deliver(g_proj, -0.4, 30.0, 24.0),
            Small(small, jnp.pad(g_taps, ((0, 16 - g_taps.shape[0]), (0, 0))), 50.0),
        ],
        both,
        7,
    )
    g_lin = g_lin.reshape(replicas, shards, -1, 2 * ffn_window)
    g_query, g_key, g_value, g_outgate = widen(g_proj, 4, width, col_window, col_first)
    g_gate, g_up = widen(g_lin, 2, ffn, ffn_window, ffn_first)
    g_beta = g_proj[..., 4 * own : 4 * own + heads].transpose(0, 2, 1, 3)
    g_down = lax.dynamic_slice_in_dim(g_down.reshape(-1, width), shift, hidden_own)
    gains = width // shards
    return (
        (hidden + out_terms).astype(bf16),
        (d_hidden + d_source).astype(bf16),
        g_query,
        g_key,
        g_value,
        g_beta.reshape(weight_rows, total_heads).astype(f32),
        g_outgate,
        g_output.reshape(own, width).astype(f32),
        g_taps[:TAPS],
        g_taps[TAPS : 2 * TAPS],
        g_taps[2 * TAPS : 3 * TAPS],
        small[0, :gains],
        small[0, 2 * gains : 2 * gains + head_gain.shape[0]],
        small[0, gains : 2 * gains],
        g_gate,
        g_up,
        g_down.astype(f32),
    )


def solution(mesh):
    tokens = P(("replica", "shard"), None)
    whole, columns, vector = P("shard", None), P(None, "shard"), P("shard")
    in_specs = (tokens, tokens, P("replica", None, None), P("replica", None)) + (whole,) * 6
    in_specs += (columns,) * 3 + (vector,) * 3 + (whole,) * 3
    out_specs = (tokens, tokens) + (whole,) * 6 + (columns,) * 3 + (vector,) * 3 + (whole,) * 3
    return jax.shard_map(body, mesh=mesh, in_specs=in_specs, out_specs=out_specs, check_vma=False)
```

```python
import functools

import jax
import jax.numpy as jnp
from jax import lax
from jax.experimental import pallas as pl
from jax.experimental.pallas import tpu as pltpu
from jax.sharding import PartitionSpec as P

MESH = pl.DeviceIdType.MESH
ANY = pl.BlockSpec(memory_space=pl.ANY)
VMEM = pl.BlockSpec(memory_space=pltpu.VMEM)
DMA = pltpu.SemaphoreType.DMA
UP, DOWN, RIGHT, LEFT = range(4)


def grid_of(axis):
    count = lax.axis_size(axis)
    if axis == "replica":
        across = 2 if count % 2 == 0 else 1
        return count // across, across
    depth = 4 if count % 4 == 0 else count
    return depth, count // depth


class Lines:
    def __init__(self, axis):
        self.axis = axis
        self.Z, self.X = grid_of(axis)
        self.count = self.Z * self.X
        self.me = lax.axis_index(axis)
        self.z, self.x = lax.div(self.me, self.X), lax.rem(self.me, self.X)
        z, x, X = self.z, self.x, self.X
        self.targets = ((z + 1) * X + x, (z - 1) * X + x, z * X + x + 1, z * X + x - 1)
        self.exists = (z < self.Z - 1, z > 0, x < X - 1, x > 0)

    def to(self, way):
        return {self.axis: self.targets[way]}

    def other(self, k):
        return lax.rem(self.me + k, self.count)

    def slot(self, zz, xx):
        return zz * self.X + xx


class Turned(Lines):
    def __init__(self, line):
        self.axis, self.count, self.me = line.axis, line.count, line.me
        self.Z, self.X, self.z, self.x = line.X, line.Z, line.x, line.z
        self.targets = line.targets[2:] + line.targets[:2]
        self.exists = line.exists[2:] + line.exists[:2]

    def slot(self, zz, xx):
        return xx * self.Z + zz


class Column(Lines):
    def __init__(self, line):
        self.axis, self.count, self.me = line.axis, line.Z, line.z
        self.Z, self.X, self.z, self.x = line.Z, 1, line.z, jnp.int32(0)
        self.targets = line.targets
        self.exists = line.exists[:2] + (jnp.bool_(False),) * 2

    def slot(self, zz, xx):
        return zz


def greet(lines, everyone):
    barrier = pltpu.get_barrier_semaphore()
    count = jnp.int32(0)
    for line in lines:
        if line.axis in everyone:
            for k in range(1, line.count):
                pl.semaphore_signal(
                    barrier, inc=1, device_id={line.axis: line.other(k)}, device_id_type=MESH
                )
            count = count + (line.count - 1)
            continue
        for way in range(4):

            @pl.when(line.exists[way])
            def _(line=line, way=way):
                pl.semaphore_signal(barrier, inc=1, device_id=line.to(way), device_id_type=MESH)

            count = count + jnp.where(line.exists[way], 1, 0)
    pl.semaphore_wait(barrier, count)


def remote(src, dst, send_sem, recv_sem, device):
    return pltpu.make_async_remote_copy(
        src_ref=src,
        dst_ref=dst,
        send_sem=send_sem,
        recv_sem=recv_sem,
        device_id=device,
        device_id_type=MESH,
    )


def in_place(view, sem):
    return pltpu.make_async_copy(view, view, sem)


def staged(src, dst, held, sems):
    load = pltpu.make_async_copy(src, held, sems.at[0])
    save = pltpu.make_async_copy(held, dst, sems.at[1])

    def turn():
        load.wait()
        save.start()

    return load.start, turn, save.wait


def gather_sems(axis, chunks):
    Z, X = grid_of(axis)
    return [DMA((4, Z * X, chunks)), DMA((Z * X, chunks))]


def gather_steps(line, chunks, view, source, ready, sems, start, pace):
    send_sem, recv_sem = sems
    Z, X, z, x, me = line.Z, line.X, line.z, line.x, line.me
    exists = line.exists

    def copy(way, origin, c, src=None):
        spot = view(origin, c)
        return remote(
            spot if src is None else src,
            spot,
            send_sem.at[way, origin, c],
            recv_sem.at[origin, c],
            line.to(way),
        )

    def first(c):
        ready(c)
        for way in range(4):

            @pl.when(exists[way])
            def _(way=way):
                copy(way, me, c, source(c)).start()

    def hop(d, c):
        for way, here in ((UP, z - d >= 0), (DOWN, z + d < Z)):

            @pl.when(here)
            def _(way=way):
                origin = line.slot(z - d if way == UP else z + d, x)
                copy(way, origin, c).wait_recv()
                for onward in (way, RIGHT, LEFT):

                    @pl.when(exists[onward])
                    def _(onward=onward):
                        copy(onward, origin, c).start()

    def across(e, level, c):
        for way, here in ((RIGHT, x - e >= 0), (LEFT, x + e < X)):

            @pl.when(here)
            def _(way=way):
                origin = line.slot(level, x - e if way == RIGHT else x + e)
                copy(way, origin, c).wait_recv()
                if X > 2:

                    @pl.when(exists[way])
                    def _():
                        copy(way, origin, c).start()

    def finish():
        for c in range(chunks):
            for zz in range(Z):
                for way, here in ((UP, zz <= z), (DOWN, zz >= z)):

                    @pl.when(exists[way] & here)
                    def _(way=way, zz=zz, c=c):
                        copy(way, line.slot(zz, x), c).wait_send()

                for xx in range(X):
                    for way, here in ((RIGHT, xx <= x), (LEFT, xx >= x)):

                        @pl.when(exists[way] & here)
                        def _(way=way, zz=zz, xx=xx, c=c):
                            copy(way, line.slot(zz, xx), c).wait_send()

    steps = []
    for c in range(chunks):
        steps.append((start + pace * c / chunks, functools.partial(first, c)))
    for d in range(1, Z):
        for c in range(chunks):
            steps.append((start + pace * (d - 1 + (c + 1) / chunks), functools.partial(hop, d, c)))
    for e in range(1, X):
        for dz in range(Z):
            level = lax.rem(z + dz, Z)
            for c in range(chunks):
                when = start + pace * (Z + e + (dz * chunks + c) / (Z * chunks))
                steps.append((when, functools.partial(across, e, level, c)))
    steps.append((start + pace * (Z + X + 1), finish))
    return steps


def scatter_slots(dims):
    Z, X = dims
    if X == 1:
        return Z, 1
    if X == 2:
        return Z, Z
    return Z * X, Z * (X + 1)


def scatter_scratch(dims, chunks, rows, width, kind):
    Z, X = dims
    held, across = scatter_slots(dims)
    return [
        pltpu.VMEM((held, chunks, rows, width), kind),
        pltpu.VMEM((across, chunks, rows, width), kind),
        pltpu.VMEM((Z + 1, chunks, rows, width), kind),
        DMA((held,)),
        DMA((Z * X, chunks)),
        DMA((across, chunks)),
        DMA((Z, chunks)),
        DMA((Z + 1, chunks)),
    ]


STEP = 16


def stride(rows):
    return max(n for n in (16, 32, 64) if rows % n == 0 and n <= BIG)


BIG = 64


def scatter_steps(line, chunks, block, piece, scratch, store, done, start, pace):
    mine, from_x, from_z, load_sem, xs_sem, xr_sem, zs_sem, zr_sem = scratch
    Z, X, z, x = line.Z, line.X, line.z, line.x
    exists = line.exists
    rows = mine.shape[2]
    step = stride(rows)

    def spot(zz, xx):
        return zz if X <= 2 else zz * X + xx

    def load(zz, xx):
        at = spot(zz, xx)
        return pltpu.make_async_copy(block(line.slot(zz, xx)), mine.at[at], load_sem.at[at])

    def x_landing(zz, xx, right, receiver):
        if X <= 2:
            return zz
        return zz * (X + 1) + (xx if right else jnp.where(xx == receiver, X, xx))

    def x_copy(right, zz, xx, c):
        landing = x_landing(zz, xx, right, x + 1 if right else x - 1)
        src = piece(line.slot(zz, xx), c) if X <= 2 else mine.at[spot(zz, xx), c]
        return remote(
            src,
            from_x.at[landing, c],
            xs_sem.at[zz * X + xx, c],
            xr_sem.at[landing, c],
            line.to(RIGHT if right else LEFT),
        )

    def z_copy(up, zz, c):
        landing = zz if up else jnp.where(zz == z - 1, Z, zz)
        return remote(
            mine.at[spot(zz, x), c],
            from_z.at[landing, c],
            zs_sem.at[zz, c],
            zr_sem.at[landing, c],
            line.to(UP if up else DOWN),
        )

    def wait_in(buffer, sem, at, c):
        in_place(buffer.at[at, c], sem.at[at, c]).wait()

    def add_in(at, buffer, landing, c):
        def body(i, carry):
            part = pl.ds(pl.multiple_of(i * step, step), step)
            mine[at, c, part] = (
                mine[at, c, part].astype(jnp.float32) + buffer[landing, c, part].astype(jnp.float32)
            ).astype(mine.dtype)
            return carry

        lax.fori_loop(0, rows // step, body, 0)

    def x_line(zz):
        for k in range(X - 1):
            for right, xx, here in ((True, X - 1 - k, X - 1 - k > x), (False, k, k < x)):

                @pl.when(here)
                def _(right=right, xx=xx):
                    if X > 2:
                        load(zz, xx).wait()
                    for c in range(chunks):
                        if X > 2:

                            @pl.when(exists[LEFT if right else RIGHT])
                            def _(c=c):
                                landing = x_landing(zz, xx, right, jnp.int32(-1))
                                wait_in(from_x, xr_sem, landing, c)
                                add_in(spot(zz, xx), from_x, landing, c)

                        x_copy(right, zz, xx, c).start()

    def x_join(zz, c):
        at = spot(zz, x)
        if X == 2:
            wait_in(from_x, xr_sem, zz, c)
            add_in(at, from_x, zz, c)
        elif X > 2:
            for right in (True, False):

                @pl.when(exists[LEFT if right else RIGHT])
                def _(right=right):
                    landing = zz * (X + 1) + (x if right else X)
                    wait_in(from_x, xr_sem, landing, c)
                    add_in(at, from_x, landing, c)

    def ways(k):
        return ((True, Z - 1 - k, Z - 1 - k > z), (False, k, k < z))

    def begin():
        for zz in range(Z):
            for xx in range(X):
                if X > 2:
                    load(zz, xx).start()
            if X <= 2:
                load(zz, x).start()
        for k in range(Z - 1):
            for up, zz, here in ways(k):

                @pl.when(here)
                def _(zz=zz):
                    x_line(zz)

        x_line(z)

    def pass_on(k, c):
        for up, zz, here in ways(k):

            @pl.when(here)
            def _(up=up, zz=zz):
                if c == 0:
                    load(zz, x).wait()
                x_join(zz, c)

                @pl.when(exists[DOWN if up else UP])
                def _():
                    wait_in(from_z, zr_sem, zz, c)
                    add_in(spot(zz, x), from_z, zz, c)

                z_copy(up, zz, c).start()

    def settle(c):
        if c == 0:
            load(z, x).wait()
        x_join(z, c)

        @pl.when(exists[DOWN])
        def _():
            wait_in(from_z, zr_sem, z, c)

        @pl.when(exists[UP])
        def _():
            wait_in(from_z, zr_sem, Z, c)

        def body(i, carry):
            part = pl.ds(pl.multiple_of(i * step, step), step)
            total = mine[spot(z, x), c, part].astype(jnp.float32)
            below = from_z[z, c, part].astype(jnp.float32)
            above = from_z[Z, c, part].astype(jnp.float32)
            total = total + jnp.where(z > 0, below, 0.0)
            total = total + jnp.where(z < Z - 1, above, 0.0)
            store(c, part, total)
            return carry

        lax.fori_loop(0, rows // step, body, 0)
        done(c)

    def finish():
        for zz in range(Z):
            for c in range(chunks):
                for xx in range(X):

                    @pl.when(xx != x)
                    def _(zz=zz, xx=xx, c=c):
                        x_copy(True, zz, xx, c).wait_send()

                @pl.when(zz != z)
                def _(zz=zz, c=c):
                    z_copy(True, zz, c).wait_send()

    steps = [(start, begin)]
    for k in range(Z - 1):
        for c in range(chunks):
            steps.append(
                (start + pace * (k + (c + 1) / chunks), functools.partial(pass_on, k, c))
            )
    for c in range(chunks):
        steps.append((start + pace * (Z - 1 + (c + 1) / chunks), functools.partial(settle, c)))
    steps.append((start + pace * (Z + 2), finish))
    return steps


class Gather:
    def __init__(self, axis, block, chunks, start=0.0, pace=21.0, beside=False, turned=False):
        self.axis, self.chunks, self.start, self.pace = axis, chunks, start, pace
        self.beside, self.turned = beside, turned
        self.inputs = [block]
        self.everyone = ()
        count = lax.axis_size(axis)
        rows, width = block.shape
        shape = (rows, count * width) if beside else (count, rows, width)
        self.outputs = [(ANY, jax.ShapeDtypeStruct(shape, block.dtype))]
        self.scratch = [pltpu.VMEM(block.shape, block.dtype), DMA((2,))]
        self.scratch += gather_sems(axis, chunks - turned)
        if turned:
            self.scratch += gather_sems(axis, 1)

    def steps(self, lines, ins, outs, scratch):
        line, (x_ref,), (out_ref,) = lines[self.axis], ins, outs
        held, own_sems, *sems = scratch
        rows, width = x_ref.shape[0] // self.chunks, x_ref.shape[1]

        def view(origin, part):
            if self.beside:
                return out_ref.at[part, pl.ds(pl.multiple_of(origin * width, HD), width)]
            return out_ref.at[origin, part]

        begin, turn, end = staged(x_ref, view(line.me, pl.ds(0, x_ref.shape[0])), held, own_sems)

        def part_steps(line, first, count, sems, start):
            def part(c):
                return pl.ds((first + c) * rows, rows)

            return gather_steps(
                line,
                count,
                lambda origin, c: view(origin, part(c)),
                lambda c: x_ref.at[part(c)],
                lambda c: None,
                sems,
                start,
                self.pace,
            )

        straight = self.chunks - self.turned
        steps = part_steps(line, 0, straight, sems[:2], self.start)
        if self.turned:
            steps += part_steps(Turned(line), straight, 1, sems[2:], self.start + 0.9 * self.pace)
        return [(self.start, begin), (self.start + 0.95 * self.pace, turn)] + steps + [(steps[-1][0], end)]


class Scatter:
    def __init__(self, axis, terms, chunks, start=0.0, pace=21.0, turned=False, column=False):
        self.axis, self.chunks, self.start, self.pace = axis, chunks, start, pace
        self.turned, self.column = turned, column
        dims = grid_of(axis)
        if column:
            dims = (dims[0], 1)
        count = dims[0] * dims[1]
        rows, width = terms.shape[0] // count // chunks, terms.shape[1]
        self.inputs = [terms.reshape(count, chunks, rows, width)]
        self.everyone = ()
        self.outputs = [(VMEM, jax.ShapeDtypeStruct((chunks * rows, width), jnp.float32))]
        self.scratch = scatter_scratch(dims, chunks - turned, rows, width, terms.dtype)
        self.half = len(self.scratch)
        if turned:
            self.scratch += scatter_scratch(dims[::-1], 1, rows, width, terms.dtype)

    def steps(self, lines, ins, outs, scratch):
        (p_ref,), (out_ref,) = ins, outs
        rows = p_ref.shape[2]

        def part_steps(line, first, count, scratch, start):
            def store(c, part, total):
                at = pl.multiple_of((first + c) * rows + part.start, STEP)
                out_ref[pl.ds(at, part.size)] = total

            return scatter_steps(
                line,
                count,
                lambda slot: p_ref.at[slot, pl.ds(first, count)],
                lambda slot, c: p_ref.at[slot, first + c],
                scratch,
                store,
                lambda c: None,
                start,
                self.pace,
            )

        line, straight = lines[self.axis], self.chunks - self.turned
        if self.column:
            line = Column(line)
        steps = part_steps(line, 0, straight, scratch[: self.half], self.start)
        if self.turned:
            steps += part_steps(Turned(line), straight, 1, scratch[self.half :], self.start + 0.01)
        return steps


class Spread:
    def __init__(self, weights, window, first, start=0.0, pace=6.0):
        self.inputs = list(weights)
        self.window, self.first, self.start, self.pace = window, first, start, pace
        self.everyone = ("shard",)
        shards, replicas = lax.axis_size("shard"), lax.axis_size("replica")
        self.part = weights[0].shape[0] // replicas
        wide = len(weights) * window
        shape = (shards, replicas, self.part, wide)
        self.outputs = [(ANY, jax.ShapeDtypeStruct(shape, weights[0].dtype))]
        self.scratch = [
            DMA((len(weights),)),
            DMA((len(weights), shards)),
            DMA((len(weights), shards)),
        ] + gather_sems("replica", shards)

    def steps(self, lines, ins, outs, scratch):
        own_sem, deal_send, deal_recv, *sems = scratch
        (out_ref,) = outs
        group, copies = lines["shard"], lines["replica"]
        rows = pl.ds(pl.multiple_of(copies.me * self.part, self.part), self.part)
        kinds = range(len(ins))

        def source(kind, target):
            return ins[kind].at[rows, pl.ds(pl.multiple_of(self.first(target), 128), self.window)]

        def landing(kind, origin):
            return out_ref.at[origin, copies.me, :, pl.ds(kind * self.window, self.window)]

        def own(kind):
            return pltpu.make_async_copy(
                source(kind, group.me), landing(kind, group.me), own_sem.at[kind]
            )

        def deal(kind, k):
            target = group.other(k)
            return remote(
                source(kind, target),
                landing(kind, group.me),
                deal_send.at[kind, k],
                deal_recv.at[kind, group.me],
                {"shard": target},
            )

        def begin():
            for k in range(1, group.count):
                for kind in kinds:
                    deal(kind, k).start()
            for kind in kinds:
                own(kind).start()

        def ready(c):
            @pl.when(c == group.me)
            def _():
                for kind in kinds:
                    own(kind).wait()

            @pl.when(c != group.me)
            def _():
                for kind in kinds:
                    in_place(landing(kind, c), deal_recv.at[kind, c]).wait()

        def finish():
            for k in range(1, group.count):
                for kind in kinds:
                    deal(kind, k).wait_send()

        steps = gather_steps(
            copies,
            group.count,
            lambda origin, c: out_ref.at[c, origin],
            lambda c: out_ref.at[c, copies.me],
            ready,
            sems,
            self.start + 2 * self.pace,
            self.pace,
        )
        return [(self.start, begin)] + steps + [(steps[-1][0], finish)]


class Trade:
    def __init__(self, block, start=0.0, pace=6.0):
        self.inputs = [block]
        self.start, self.pace = start, pace
        self.everyone = ()
        shards, part, width = block.shape
        shape = (shards, lax.axis_size("replica"), part, width)
        self.outputs = [(ANY, jax.ShapeDtypeStruct(shape, block.dtype))]
        self.scratch = [pltpu.VMEM(block.shape, block.dtype), DMA((2,))]
        self.scratch += gather_sems("replica", shards)

    def steps(self, lines, ins, outs, scratch):
        held, own_sems, *sems = scratch
        (x_ref,), (out_ref,) = ins, outs
        copies = lines["replica"]
        begin, turn, end = staged(x_ref, out_ref.at[:, copies.me], held, own_sems)
        steps = gather_steps(
            copies,
            x_ref.shape[0],
            lambda origin, c: out_ref.at[c, origin],
            lambda c: x_ref.at[c],
            lambda c: None,
            sems,
            self.start,
            self.pace,
        )
        return [(self.start, begin), (self.start + 0.95 * self.pace, turn)] + steps + [(steps[-1][0], end)]


class Sum:
    def __init__(self, terms, start=0.0, pace=6.0):
        shards, replicas = lax.axis_size("shard"), lax.axis_size("replica")
        part, wide = terms.shape[0] // shards // replicas, terms.shape[1]
        self.inputs = [terms.reshape(shards, replicas, part, wide)]
        self.start, self.pace = start, pace
        self.everyone = ()
        self.outputs = [(VMEM, jax.ShapeDtypeStruct((shards, part, wide), terms.dtype))]
        self.scratch = scatter_scratch(grid_of("replica"), shards, part, wide, terms.dtype)

    def steps(self, lines, ins, outs, scratch):
        (p_ref,), (out_ref,) = ins, outs

        def store(c, part, total):
            out_ref[c, part] = total.astype(out_ref.dtype)

        return scatter_steps(
            lines["replica"],
            out_ref.shape[0],
            lambda slot: p_ref.at[:, slot],
            lambda slot, c: p_ref.at[c, slot],
            scratch,
            store,
            lambda c: None,
            self.start,
            self.pace,
        )


class Deliver:
    def __init__(self, sums, start=0.0, again=30.0, pace=24.0):
        self.inputs = [sums]
        self.start, self.again, self.pace = start, again, pace
        self.everyone = ("shard",)
        shards, replicas = lax.axis_size("shard"), lax.axis_size("replica")
        self.outputs = [(ANY, jax.ShapeDtypeStruct((replicas,) + sums.shape, sums.dtype))]
        self.scratch = [DMA, DMA((shards,)), DMA((shards,))] + gather_sems("replica", shards)

    def steps(self, lines, ins, outs, scratch):
        own_sem, send_sem, recv_sem, *sems = scratch
        (x_ref,), (out_ref,) = ins, outs
        group, copies = lines["shard"], lines["replica"]
        own = pltpu.make_async_copy(
            x_ref.at[group.me], out_ref.at[copies.me, group.me], own_sem
        )

        def deal(k):
            target = group.other(k)
            return remote(
                x_ref.at[target],
                out_ref.at[copies.me, group.me],
                send_sem.at[k],
                recv_sem.at[group.me],
                {"shard": target},
            )

        def begin():
            own.start()
            for k in range(1, group.count):
                deal(k).start()

        def ready(c):
            @pl.when(c == group.me)
            def _():
                own.wait()

            @pl.when(c != group.me)
            def _():
                in_place(out_ref.at[copies.me, c], recv_sem.at[c]).wait()

        def finish():
            for k in range(1, group.count):
                deal(k).wait_send()

        steps = gather_steps(
            copies,
            group.count,
            lambda origin, c: out_ref.at[origin, c],
            lambda c: out_ref.at[copies.me, c],
            ready,
            sems,
            self.again,
            self.pace,
        )
        return [(self.start, begin)] + steps + [(steps[-1][0], finish)]


class Total:
    def __init__(self, terms, start=0.0, pace=6.0):
        replicas = lax.axis_size("replica")
        share, wide = terms.shape[0] // replicas, terms.shape[1]
        chunks = max(n for n in (1, 2, 3, 4) if share % (n * STEP) == 0)
        rows = share // chunks
        self.inputs = [terms.reshape(replicas, chunks, rows, wide)]
        self.start, self.pace, self.chunks = start, pace, chunks
        self.everyone = ()
        kind = terms.dtype
        self.outputs = [(ANY, jax.ShapeDtypeStruct((replicas, chunks, rows, wide), kind))]
        self.scratch = [pltpu.VMEM((chunks, rows, wide), kind), DMA((chunks,))]
        self.scratch += gather_sems("replica", chunks)
        self.scratch += scatter_scratch(grid_of("replica"), chunks, rows, wide, kind)

    def steps(self, lines, ins, outs, scratch):
        (p_ref,), (out_ref,) = ins, outs
        total_ref, own_sem = scratch[:2]
        copies = lines["replica"]

        def own(c):
            return pltpu.make_async_copy(
                total_ref.at[c], out_ref.at[copies.me, c], own_sem.at[c]
            )

        def store(c, part, total):
            total_ref[c, part] = total.astype(total_ref.dtype)

        def finish():
            for c in range(self.chunks):
                own(c).wait()

        summing = scatter_steps(
            copies,
            self.chunks,
            lambda slot: p_ref.at[slot],
            lambda slot, c: p_ref.at[slot, c],
            scratch[4:],
            store,
            lambda c: own(c).start(),
            self.start,
            self.pace,
        )
        sharing = gather_steps(
            copies,
            self.chunks,
            lambda origin, c: out_ref.at[origin, c],
            lambda c: total_ref.at[c],
            lambda c: None,
            scratch[2:4],
            self.start + self.pace * (copies.Z + 2),
            self.pace,
        )
        return summing + sharing + [(sharing[-1][0], finish)]


class Small:
    def __init__(self, dealt, shared, start=0.0):
        shards, replicas = lax.axis_size("shard"), lax.axis_size("replica")
        self.inputs = [dealt, shared]
        self.start = start
        self.everyone = ("shard", "replica")
        one = dealt.shape[1:]
        self.outputs = [
            (VMEM, jax.ShapeDtypeStruct(one, jnp.float32)),
            (VMEM, jax.ShapeDtypeStruct(shared.shape, jnp.float32)),
        ]
        self.scratch = [
            pltpu.VMEM((shards,) + one, jnp.float32),
            pltpu.VMEM((replicas,) + one, jnp.float32),
            pltpu.VMEM((replicas,) + shared.shape, jnp.float32),
            DMA((shards,)), DMA((shards,)),
            DMA((2, replicas)), DMA((2, replicas)), DMA((2,)),
        ]

    def steps(self, lines, ins, outs, scratch):
        dealt, shared = ins
        out_one, out_rows = outs
        got, got_one, got_rows, send, recv, send2, recv2, own = scratch
        group, copies = lines["shard"], lines["replica"]

        def deal(k):
            target = group.other(k)
            return remote(
                dealt.at[target], got.at[group.me], send.at[k], recv.at[group.me], {"shard": target}
            )

        def share(which, k):
            buffer = (got_one, got_rows)[which]
            return remote(
                buffer.at[copies.me] if which == 0 else shared,
                buffer.at[copies.me],
                send2.at[which, k],
                recv2.at[which, copies.me],
                {"replica": copies.other(k)},
            )

        def keep():
            return pltpu.make_async_copy(dealt.at[group.me], got.at[group.me], own.at[0])

        def keep_rows():
            return pltpu.make_async_copy(shared, got_rows.at[copies.me], own.at[1])

        def begin():
            keep().start()
            keep_rows().start()
            for k in range(1, group.count):
                deal(k).start()
            for k in range(1, copies.count):
                share(1, k).start()

        def middle():
            keep().wait()
            for k in range(1, group.count):
                origin = group.other(k)
                in_place(got.at[origin], recv.at[origin]).wait()
            total = got[0]
            for s in range(1, group.count):
                total = total + got[s]
            got_one[copies.me] = total
            for k in range(1, copies.count):
                share(0, k).start()

        def end():
            keep_rows().wait()
            for k in range(1, copies.count):
                origin = copies.other(k)
                in_place(got_one.at[origin], recv2.at[0, origin]).wait()
                in_place(got_rows.at[origin], recv2.at[1, origin]).wait()
            one, rows = got_one[0], got_rows[0]
            for r in range(1, copies.count):
                one, rows = one + got_one[r], rows + got_rows[r]
            out_one[...] = one
            out_rows[...] = rows
            for k in range(1, group.count):
                deal(k).wait_send()
            for k in range(1, copies.count):
                share(0, k).wait_send()
                share(1, k).wait_send()

        return [(-0.5, begin), (self.start, middle), (self.start + 40.0, end)]


def layout_of(tasks):
    inputs, outputs, scratch, spans = [], [], [], []
    for task in tasks:
        spans.append((len(inputs), len(outputs), len(scratch)))
        inputs += task.inputs
        outputs += task.outputs
        scratch += task.scratch
    return inputs, outputs, scratch, spans


def task_steps(tasks, spans, axes, ins, outs, scratch):
    lines = {axis: Lines(axis) for axis in axes}
    everyone = {axis for task in tasks for axis in task.everyone}
    steps = []
    for task, (i, o, s) in zip(tasks, spans):
        steps += task.steps(
            lines,
            ins[i : i + len(task.inputs)],
            outs[o : o + len(task.outputs)],
            scratch[s : s + len(task.scratch)],
        )
    steps.sort(key=lambda step: step[0])
    return [(-1.0, lambda: greet(list(lines.values()), everyone))] + steps


def exchange(tasks, axes, ident):
    inputs, outputs, scratch, spans = layout_of(tasks)

    def kernel(*refs):
        ins = refs[: len(inputs)]
        outs = refs[len(inputs) : len(inputs) + len(outputs)]
        rest = refs[len(inputs) + len(outputs) :]
        for _, step in task_steps(tasks, spans, axes, ins, outs, rest):
            step()

    return pl.pallas_call(
        kernel,
        in_specs=[ANY] * len(inputs),
        out_specs=[spec for spec, _ in outputs],
        out_shape=[shape for _, shape in outputs],
        scratch_shapes=scratch,
        compiler_params=pltpu.CompilerParams(
            collective_id=ident, has_side_effects=True, vmem_limit_bytes=60 * 1024 * 1024
        ),
    )(*inputs)


HD = 128
TAPS = 4
KINDS = 3


def dot_nn(a, b):
    return lax.dot_general(
        a.astype(jnp.bfloat16),
        b.astype(jnp.bfloat16),
        (((1,), (0,)), ((), ())),
        preferred_element_type=jnp.float32,
    )


def dot_nt(a, b):
    return lax.dot_general(
        a.astype(jnp.bfloat16),
        b.astype(jnp.bfloat16),
        (((1,), (1,)), ((), ())),
        preferred_element_type=jnp.float32,
    )


def dot_tn(a, b):
    return lax.dot_general(
        a.astype(jnp.bfloat16),
        b.astype(jnp.bfloat16),
        (((0,), (0,)), ((), ())),
        preferred_element_type=jnp.float32,
    )


def time_of(shape, dim, lanes):
    index = lax.broadcasted_iota(jnp.int32, shape, dim)
    return lax.rem(index, 8) * lanes + lax.div(index, 8)


def lower_inverses(lowers, lanes):
    size = lowers[0].shape[0]
    row_t = time_of((size, size), 0, lanes)
    col_t = time_of((size, size), 1, lanes)
    eye = jnp.where(row_t == col_t, 1.0, 0.0)

    def same(width):
        return lax.div(row_t, width) == lax.div(col_t, width)

    first = [jnp.where(same(8), a, 0.0) for a in lowers]
    second = [dot_nn(f, f) for f in first]
    inverse = [eye + f + s + dot_nn(f, s) for f, s in zip(first, second)]
    fourth = [dot_nn(s, s) for s in second]
    inverse = [t + dot_nn(t, f) for t, f in zip(inverse, fourth)]
    width = 16
    while width <= size:
        fresh = same(width) & jnp.logical_not(same(width // 2))
        left = [dot_nn(t, jnp.where(fresh, a, 0.0)) for t, a in zip(inverse, lowers)]
        inverse = [t + dot_nn(l, t) for t, l in zip(inverse, left)]
        width *= 2
    return inverse


def rounded(values):
    return values.astype(jnp.bfloat16).astype(jnp.float32)


def sigmoid(values):
    return 1.0 / (1.0 + jnp.exp(-values))


def unit_scale(pre):
    return lax.rsqrt(jnp.sum(pre * pre, axis=1, keepdims=True) + 1e-6)


def mean_scale(values):
    return lax.rsqrt(jnp.mean(values * values, axis=1, keepdims=True) + 1e-5)


def delta_forward(
    lanes, heads, group, proj_ref, taps_ref, gain_ref, low_ref, off_ref, rem_ref,
    zed_ref, mixed_ref, sums_ref, s_ref, t_ref, mk_ref, mv_ref, u_ref,
    state, last, unit,
):
    size = lanes * 8
    rows = group * 8
    wide = heads * HD
    scale = HD ** (-0.5)

    @pl.when(pl.program_id(0) == 0)
    def _():
        state[...] = jnp.zeros_like(state)
        last[...] = jnp.zeros_like(last)

    top = lax.broadcasted_iota(jnp.int32, (rows, HD), 0) == 0
    for kind in range(KINDS):
        for h in range(heads):
            cols = pl.ds(kind * wide + h * HD, HD)
            signal = [rounded(proj_ref[s, :, cols]) for s in range(lanes)]
            moved = {}
            for back in range(1, TAPS):
                lane = lanes - back
                edge = last[kind * heads + h, back, 0:1]
                moved[lane] = jnp.where(top, edge, pltpu.roll(signal[lane], 1, 0))
            for back in range(1, TAPS):
                last[kind * heads + h, back, 0:1] = signal[lanes - back][rows - 1 : rows]
            for s in range(lanes):
                off = off_ref[s]
                total = signal[s] * taps_ref[kind * TAPS : kind * TAPS + 1, h * HD : (h + 1) * HD]
                for hop in range(1, TAPS):
                    earlier = signal[s - hop] if s >= hop else moved[lanes + s - hop]
                    tap = taps_ref[kind * TAPS + hop : kind * TAPS + hop + 1, h * HD : (h + 1) * HD]
                    total = total + jnp.where(off >= hop, earlier, 0.0) * tap
                sums_ref[s, :, cols] = total
                pre = total * sigmoid(total)
                if kind < 2:
                    pre = pre * unit_scale(pre)
                unit[s, :, cols] = pre

    row_t = time_of((size, size), 0, lanes)
    col_t = time_of((size, size), 1, lanes)
    local_t = time_of((size, HD), 0, lanes).astype(jnp.float32)
    pairs = [(g, h) for g in range(group) for h in range(heads)]

    def span(g):
        return pl.ds(g * 8, 8)

    def flat(ref, g, first, count=HD):
        return ref[:, span(g), first : first + count].reshape(size, count)

    gates = {}
    for g in range(group):
        logits = flat(proj_ref, g, 4 * wide)
        strength = sigmoid(rounded(logits))
        for h in range(heads):
            gates[g, h] = jnp.broadcast_to(strength[:, h : h + 1], (size, HD))
    keys = {p: flat(unit, p[0], wide + p[1] * HD) for p in pairs}
    kbs = {p: gates[p] * keys[p] for p in pairs}
    lows = {g: low_ref[g].astype(jnp.float32) for g in range(group)}
    lowers = [
        -jnp.where(row_t == col_t, 0.0, lows[p[0]]) * dot_nt(kbs[p], keys[p]) for p in pairs
    ]
    inverses = dict(zip(pairs, lower_inverses(lowers, lanes)))
    mks = {p: dot_nn(inverses[p], kbs[p]) for p in pairs}
    mvs = {
        p: dot_nn(inverses[p], gates[p] * flat(unit, p[0], 2 * wide + p[1] * HD))
        for p in pairs
    }
    queries = {p: flat(unit, p[0], p[1] * HD) for p in pairs}
    scores = {p: lows[p[0]] * dot_nt(queries[p], keys[p]) for p in pairs}
    for g, h in pairs:
        t_ref[g, h] = inverses[g, h].astype(t_ref.dtype)
        mk_ref[g, h] = mks[g, h].astype(mk_ref.dtype)
        mv_ref[g, h] = mvs[g, h].astype(mv_ref.dtype)
    for g in range(group):
        carry = jnp.where(flat(off_ref, g, 0) > local_t, 1.0, 0.0)
        keep = jnp.where(flat(rem_ref, g, 0) + local_t >= size, 1.0, 0.0)
        for h in range(heads):
            p = (g, h)
            held = state[h]
            s_ref[g, h] = held.astype(s_ref.dtype)
            u = mvs[p] - carry * dot_nn(mks[p], held)
            u_ref[g, h] = u.astype(u_ref.dtype)
            state[h] = (carry[0:1] * keep[0:1]) * held + dot_tn(keys[p], keep * u)
            out = (carry * dot_nn(queries[p], held) + dot_nn(scores[p], u)) * scale
            mixed = rounded(out)
            gate = flat(proj_ref, g, 3 * wide + h * HD)
            zed = mixed * mean_scale(mixed) * gain_ref[...] * (gate * sigmoid(gate))
            mixed_ref[:, span(g), h * HD : (h + 1) * HD] = mixed.reshape(lanes, 8, HD).astype(
                mixed_ref.dtype
            )
            zed_ref[:, span(g), h * HD : (h + 1) * HD] = zed.reshape(lanes, 8, HD).astype(
                zed_ref.dtype
            )


def delta_backward(
    lanes, heads, group, proj_ref, sums_ref, mixed_ref, dzed_ref, taps_ref, gain_ref,
    low_ref, off_ref, rem_ref, s_ref, t_ref, mk_ref, mv_ref, u_ref,
    dproj_ref, gtaps_ref, ghead_ref,
    state, edge, edge_off, errs, taps_sum, head_sum,
):
    size = lanes * 8
    rows = group * 8
    wide = heads * HD
    scale = HD ** (-0.5)

    @pl.when(pl.program_id(0) == 0)
    def _():
        state[...] = jnp.zeros_like(state)
        edge[...] = jnp.zeros_like(edge)
        edge_off[...] = jnp.zeros_like(edge_off)
        taps_sum[...] = jnp.zeros_like(taps_sum)
        head_sum[...] = jnp.zeros_like(head_sum)

    row_t = time_of((size, size), 0, lanes)
    col_t = time_of((size, size), 1, lanes)
    local_t = time_of((size, HD), 0, lanes).astype(jnp.float32)
    lane_id = lax.broadcasted_iota(jnp.int32, (size, HD), 1)
    pairs = [(g, h) for g in range(group) for h in range(heads)]

    def span(g):
        return pl.ds(g * 8, 8)

    def flat(ref, g, first, count=HD):
        return ref[:, span(g), first : first + count].reshape(size, count)

    def put(ref, g, first, value):
        ref[:, span(g), first : first + HD] = value.reshape(lanes, 8, HD).astype(ref.dtype)

    gain = gain_ref[...]
    d_out, q, k, v, beta = {}, {}, {}, {}, {}
    pre, scales, slopes = {}, {}, {}
    head_total = jnp.zeros((size, HD), jnp.float32)
    strengths = {}
    carries, keeps, lows = {}, {}, {}
    for g in range(group):
        carries[g] = jnp.where(flat(off_ref, g, 0) > local_t, 1.0, 0.0)
        keeps[g] = jnp.where(flat(rem_ref, g, 0) + local_t >= size, 1.0, 0.0)
        lows[g] = low_ref[g].astype(jnp.float32)
        strengths[g] = sigmoid(rounded(flat(proj_ref, g, 4 * wide)))
    for g, h in pairs:
        p = (g, h)
        mixed = flat(mixed_ref, g, h * HD).astype(jnp.float32)
        gate = flat(proj_ref, g, 3 * wide + h * HD)
        dzed = flat(dzed_ref, g, h * HD)
        s = sigmoid(gate)
        r = mean_scale(mixed)
        through = dzed * (gate * s)
        head_total = head_total + through * mixed * r
        inner = jnp.mean(mixed * gain * through, axis=1, keepdims=True)
        d_mixed = rounded(r * gain * through - mixed * (r * r * r) * inner)
        put(dproj_ref, g, 3 * wide + h * HD, dzed * (mixed * r * gain) * (s * (1.0 + gate * (1.0 - s))))
        d_out[p] = d_mixed * scale
        for kind, store in ((0, q), (1, k), (2, v)):
            total = flat(sums_ref, g, kind * wide + h * HD)
            s = sigmoid(total)
            value = total * s
            slopes[kind, g, h] = s * (1.0 + total * (1.0 - s))
            if kind < 2:
                pre[kind, g, h] = value
                scales[kind, g, h] = unit_scale(value)
                value = value * scales[kind, g, h]
            store[p] = value
        beta[p] = jnp.broadcast_to(strengths[g][:, h : h + 1], (size, HD))
    head_sum[...] += head_total

    scores = {p: lows[p[0]] * dot_nt(q[p], k[p]) for p in pairs}
    du = {p: dot_tn(scores[p], d_out[p]) for p in pairs}
    ds = {p: lows[p[0]] * dot_nt(d_out[p], u_ref[p[0], p[1]]) for p in pairs}
    cdo = {p: carries[p[0]] * d_out[p] for p in pairs}
    dq = {p: dot_nt(cdo[p], s_ref[p[0], p[1]]) + dot_nn(ds[p], k[p]) for p in pairs}
    dk = {p: dot_tn(ds[p], q[p]) for p in pairs}
    lift = {p: dot_tn(q[p], cdo[p]) for p in pairs}
    later = {}
    for g in reversed(range(group)):
        for h in range(heads):
            p = (g, h)
            later[p] = state[h]
            du[p] = du[p] + keeps[g] * dot_nn(k[p], later[p])
            mk = carries[g] * mk_ref[g, h].astype(jnp.float32)
            state[h] = (carries[g][0:1] * keeps[g][0:1]) * later[p] + lift[p] - dot_tn(mk, du[p])
    for p in pairs:
        dk[p] = dk[p] + dot_nt(keeps[p[0]] * u_ref[p[0], p[1]].astype(jnp.float32), later[p])
    dmk = {p: -carries[p[0]] * dot_nt(du[p], s_ref[p[0], p[1]]) for p in pairs}
    xx = {p: dot_tn(t_ref[p[0], p[1]], dmk[p]) for p in pairs}
    yy = {p: dot_tn(t_ref[p[0], p[1]], du[p]) for p in pairs}
    da = {
        p: jnp.where(row_t == col_t, 0.0, lows[p[0]])
        * (dot_nt(xx[p], mk_ref[p[0], p[1]]) + dot_nt(yy[p], mv_ref[p[0], p[1]]))
        for p in pairs
    }
    dkb = {p: xx[p] - dot_nn(da[p], k[p]) for p in pairs}
    dk = {p: dk[p] - dot_tn(da[p], beta[p] * k[p]) + beta[p] * dkb[p] for p in pairs}
    for g in range(group):
        d_logits = jnp.zeros((size, HD), jnp.float32)
        for h in range(heads):
            p = (g, h)
            db = jnp.sum(dkb[p] * k[p] + yy[p] * v[p], axis=1, keepdims=True)
            d_logits = d_logits + jnp.where(lane_id == h, db * beta[p] * (1.0 - beta[p]), 0.0)
            for kind, grad in ((0, dq[p]), (1, dk[p])):
                r, raw = scales[kind, g, h], pre[kind, g, h]
                inner = jnp.sum(raw * grad, axis=1, keepdims=True)
                err = (r * grad - raw * (r * r * r) * inner) * slopes[kind, g, h]
                put(errs, g, kind * wide + h * HD, err)
            put(errs, g, 2 * wide + h * HD, beta[p] * yy[p] * slopes[2, g, h])
        put(dproj_ref, g, 4 * wide, d_logits)

    bottom = lax.broadcasted_iota(jnp.int32, (rows, HD), 0) == rows - 1
    for kind in range(KINDS):
        for h in range(heads):
            at = kind * wide + h * HD
            cols = pl.ds(at, HD)
            err = [errs[s, :, cols] for s in range(lanes)]
            taps = [
                taps_ref[kind * TAPS + hop : kind * TAPS + hop + 1, h * HD : (h + 1) * HD]
                for hop in range(TAPS)
            ]
            sums = [jnp.zeros((rows, HD), jnp.float32) for _ in range(TAPS)]
            live = {}
            for hop in range(1, TAPS):
                for s in range(lanes):
                    live[hop, s] = jnp.where(off_ref[s] >= hop, err[s], 0.0)
            for hop in range(1, TAPS):
                for s in range(hop):
                    row = jnp.where(edge_off[s, 0:1] >= hop, edge[kind * heads + h, s, 0:1], 0.0)
                    live[hop, lanes + s] = jnp.where(
                        bottom, row, pltpu.roll(live[hop, s], rows - 1, 0)
                    )
            for s in range(lanes):
                signal = rounded(proj_ref[s, :, cols])
                total = err[s] * taps[0]
                sums[0] = sums[0] + err[s] * signal
                for hop in range(1, TAPS):
                    total = total + live[hop, s + hop] * taps[hop]
                    sums[hop] = sums[hop] + live[hop, s + hop] * signal
                dproj_ref[s, :, cols] = total.astype(dproj_ref.dtype)
            for s in range(TAPS - 1):
                edge[kind * heads + h, s, 0:1] = err[s][0:1]
            for hop in range(TAPS):
                folded = sums[hop].reshape(group, 8, HD)
                taps_sum[kind * TAPS + hop, :, h * HD : (h + 1) * HD] += jnp.sum(folded, axis=0)
    for s in range(TAPS - 1):
        edge_off[s, 0:1] = off_ref[s][0:1]

    @pl.when(pl.program_id(0) == pl.num_programs(0) - 1)
    def _():
        gtaps_ref[...] = jnp.sum(taps_sum[...], axis=1)
        ghead_ref[...] = jnp.sum(head_sum[...], axis=0, keepdims=True)


def mixer_specs(lanes, heads, group, flip):
    size = lanes * 8
    at = (lambda i: flip - 1 - i) if flip else (lambda i: i)

    def token(width):
        return pl.BlockSpec((lanes, 8 * group, width), lambda i: (0, at(i), 0))

    def saved(first, second):
        return pl.BlockSpec((group, heads, first, second), lambda i: (at(i), 0, 0, 0))

    square = pl.BlockSpec((group, size, size), lambda i: (at(i), 0, 0))
    return token, saved, square


def fixed(shape):
    return pl.BlockSpec(shape, lambda i: (0,) * len(shape))


def saved_shapes(lanes, heads, blocks):
    size = lanes * 8
    kind = jnp.bfloat16
    return [
        jax.ShapeDtypeStruct((blocks, heads, HD, HD), kind),
        jax.ShapeDtypeStruct((blocks, heads, size, size), kind),
        jax.ShapeDtypeStruct((blocks, heads, size, HD), kind),
        jax.ShapeDtypeStruct((blocks, heads, size, HD), kind),
        jax.ShapeDtypeStruct((blocks, heads, size, HD), kind),
    ]


def mixer_forward(proj, taps, gain, low, off, rem, heads, group=4):
    lanes, tokens, width = proj.shape
    blocks, wide = tokens // 8, heads * HD
    size = lanes * 8
    token, saved, square = mixer_specs(lanes, heads, group, 0)
    return pl.pallas_call(
        functools.partial(delta_forward, lanes, heads, group),
        grid=(blocks // group,),
        in_specs=[token(width), fixed(taps.shape), fixed(gain.shape), square, token(HD), token(HD)],
        out_specs=[
            token(wide), token(wide), token(KINDS * wide),
            saved(HD, HD), saved(size, size), saved(size, HD), saved(size, HD), saved(size, HD),
        ],
        out_shape=[
            jax.ShapeDtypeStruct((lanes, tokens, wide), jnp.bfloat16),
            jax.ShapeDtypeStruct((lanes, tokens, wide), jnp.bfloat16),
            jax.ShapeDtypeStruct((lanes, tokens, KINDS * wide), jnp.float32),
        ] + saved_shapes(lanes, heads, blocks),
        scratch_shapes=[
            pltpu.VMEM((heads, HD, HD), jnp.float32),
            pltpu.VMEM((KINDS * heads, TAPS, 8, HD), jnp.float32),
            pltpu.VMEM((lanes, 8 * group, KINDS * wide), jnp.float32),
        ],
        compiler_params=pltpu.CompilerParams(vmem_limit_bytes=48 * 1024 * 1024),
        cost_estimate=pl.CostEstimate(flops=35 * 10**9, bytes_accessed=40 * 10**6, transcendentals=0),
    )(proj, taps, gain, low, off, rem)


def mixer_backward(
    proj, sums, mixed, dzed, taps, gain, low, off, rem, saves, heads, group=4
):
    lanes, tokens, width = proj.shape
    blocks, wide = tokens // 8, heads * HD
    size = lanes * 8
    token, saved, square = mixer_specs(lanes, heads, group, blocks // group)
    return pl.pallas_call(
        functools.partial(delta_backward, lanes, heads, group),
        grid=(blocks // group,),
        in_specs=[
            token(width), token(KINDS * wide), token(wide), token(wide),
            fixed(taps.shape), fixed(gain.shape), square, token(HD), token(HD),
            saved(HD, HD), saved(size, size), saved(size, HD), saved(size, HD), saved(size, HD),
        ],
        out_specs=[token(width), fixed(taps.shape), fixed(gain.shape)],
        out_shape=[
            jax.ShapeDtypeStruct((lanes, tokens, width), jnp.bfloat16),
            jax.ShapeDtypeStruct(taps.shape, jnp.float32),
            jax.ShapeDtypeStruct(gain.shape, jnp.float32),
        ],
        scratch_shapes=[
            pltpu.VMEM((heads, HD, HD), jnp.float32),
            pltpu.VMEM((KINDS * heads, TAPS, 8, HD), jnp.float32),
            pltpu.VMEM((TAPS, 8, HD), jnp.float32),
            pltpu.VMEM((lanes, 8 * group, KINDS * wide), jnp.float32),
            pltpu.VMEM((taps.shape[0], 8, wide), jnp.float32),
            pltpu.VMEM((size, HD), jnp.float32),
        ],
        compiler_params=pltpu.CompilerParams(vmem_limit_bytes=48 * 1024 * 1024),
        cost_estimate=pl.CostEstimate(flops=35 * 10**9, bytes_accessed=40 * 10**6, transcendentals=0),
    )(proj, sums, mixed, dzed, taps, gain, low, off, rem, *saves)


def segment_masks(lengths_grid, order_row, lanes, tokens):
    slots = order_row.shape[0]
    flat = lengths_grid.reshape(slots)
    first = lax.broadcasted_iota(jnp.int32, (slots, slots), 0)
    second = lax.broadcasted_iota(jnp.int32, (slots, slots), 1)
    run_len = jnp.sum(jnp.where(order_row[:, None] == second, flat[None, :], 0), axis=1)
    ends = jnp.sum(jnp.where(first >= second, run_len[None, :], 0), axis=1)
    starts = ends - run_len
    size = lanes * 8
    blocks = tokens // 8
    lane = lax.broadcasted_iota(jnp.int32, (lanes, tokens), 0)
    step = lax.broadcasted_iota(jnp.int32, (lanes, tokens), 1)
    place = step * lanes + lane
    inside = (starts[:, None, None] <= place[None]) & (place[None] < ends[:, None, None])
    start_at = jnp.sum(jnp.where(inside, starts[:, None, None], 0), axis=0)
    end_at = jnp.sum(jnp.where(inside, ends[:, None, None], 0), axis=0)

    def blocked(values):
        return values.reshape(lanes, blocks, 8).transpose(1, 0, 2).reshape(blocks, size)

    start_b, place_b = blocked(start_at), blocked(place)
    low = (start_b[:, :, None] == start_b[:, None, :]) & (place_b[:, :, None] >= place_b[:, None, :])

    def spread(values):
        return jnp.broadcast_to(values.astype(jnp.float32)[:, :, None], (lanes, tokens, HD))

    return low.astype(jnp.bfloat16), spread(place - start_at), spread(end_at - place)


def exchange_beside(tasks, axes, ident, compute, grid, pace, operands, results, scratch, flops):
    inputs, outputs, own_scratch, spans = layout_of(tasks)
    counts = (len(inputs), len(operands), len(outputs), len(results), len(own_scratch), len(scratch))

    def kernel(*refs):
        groups, at = [], 0
        for count in counts:
            groups.append(refs[at : at + count])
            at += count
        task_ins, ins, task_outs, outs, task_scratch, rest = groups
        steps = task_steps(tasks, spans, axes, task_ins, task_outs, task_scratch)
        due = [min(max(int(when // pace), 0), grid) for when, _ in steps]
        for i in range(grid):
            if i in due:

                @pl.when(pl.program_id(0) == i)
                def _(i=i):
                    for turn, (_, step) in zip(due, steps):
                        if turn == i:
                            step()

        compute(*ins, *outs, *rest)

        @pl.when(pl.program_id(0) == grid - 1)
        def _():
            for turn, (_, step) in zip(due, steps):
                if turn == grid:
                    step()

    return pl.pallas_call(
        kernel,
        grid=(grid,),
        in_specs=[ANY] * len(inputs) + [spec for _, spec in operands],
        out_specs=[spec for spec, _ in outputs] + [spec for spec, _ in results],
        out_shape=[shape for _, shape in outputs] + [shape for _, shape in results],
        scratch_shapes=own_scratch + list(scratch),
        compiler_params=pltpu.CompilerParams(
            collective_id=ident, has_side_effects=True, vmem_limit_bytes=60 * 1024 * 1024
        ),
        cost_estimate=pl.CostEstimate(flops=flops, bytes_accessed=60 * 10**6, transcendentals=0),
    )(*inputs, *[array for array, _ in operands])


def feed_forward(
    rows, window, zed_ref, source_ref, wo_ref, wi_ref, wd_ref, gain_ref,
    hidden_ref, in_ref, product_ref, slopes_ref, out_ref, held,
):
    width = source_ref.shape[1]
    wide = 512
    squares = jnp.zeros((rows, 1), jnp.float32)
    for n in range(0, width, wide):
        cols = slice(n, n + wide)
        part = source_ref[:, cols].astype(jnp.float32) + dot_nn(zed_ref[...], wo_ref[:, cols])
        held[:, cols] = part
        squares = squares + jnp.sum(part * part, axis=1, keepdims=True)
    scale = lax.rsqrt(squares / width + 1e-6)
    for n in range(0, width, wide):
        cols = slice(n, n + wide)
        in_ref[:, cols] = (held[:, cols] * scale * gain_ref[:, cols]).astype(in_ref.dtype)

    @pl.when(pl.program_id(0) == lax.axis_index("shard"))
    def _():
        hidden_ref[...] = held[...]

    wide = 256
    for n in range(0, window, wide):
        cols = slice(n, n + wide)
        ups = slice(window + n, window + n + wide)
        gate = dot_nn(in_ref[...], wi_ref[:, cols])
        up = dot_nn(in_ref[...], wi_ref[:, ups])
        s = sigmoid(gate)
        silu = gate * s
        product_ref[:, cols] = (silu * up).astype(product_ref.dtype)
        slopes_ref[:, cols] = (up * s * (1.0 + gate * (1.0 - s))).astype(slopes_ref.dtype)
        slopes_ref[:, ups] = silu.astype(slopes_ref.dtype)
    wide = 512
    for n in range(0, width, wide):
        cols = slice(n, n + wide)
        out_ref[:, cols] = dot_nn(product_ref[...], wd_ref[:, cols]).astype(out_ref.dtype)


def feed_backward(window, dy_ref, slopes_ref, wi_ref, wd_ref, dlin_ref, dterm_ref):
    width = dy_ref.shape[1]
    wide = 256
    for n in range(0, window, wide):
        cols = slice(n, n + wide)
        ups = slice(window + n, window + n + wide)
        d_product = dot_nt(dy_ref[...], wd_ref[cols])
        for part in (cols, ups):
            slope = slopes_ref[:, part].astype(jnp.float32)
            dlin_ref[:, part] = (d_product * slope).astype(dlin_ref.dtype)
    wide = 512
    for n in range(0, width, wide):
        cols = slice(n, n + wide)
        dterm_ref[:, cols] = dot_nt(dlin_ref[...], wi_ref[cols]).astype(dterm_ref.dtype)


def whole(array):
    return pl.BlockSpec(array.shape, lambda i: (0, 0), pipeline_mode=pl.Buffered(1))


def run_feed_forward(tasks, axes, ident, zed, source, w_output, w_in, w_down, gain, rows):
    tokens, width = source.shape
    window = w_down.shape[0]

    def token(columns):
        return pl.BlockSpec((rows, columns), lambda i: (i, 0))

    results = [(fixed((rows, width)), jax.ShapeDtypeStruct((rows, width), jnp.float32))]
    for columns in (width, window, 2 * window, width):
        results.append((token(columns), jax.ShapeDtypeStruct((tokens, columns), zed.dtype)))
    return exchange_beside(
        tasks,
        axes,
        ident,
        functools.partial(feed_forward, rows, window),
        tokens // rows,
        6.0,
        [(zed, token(width)), (source, token(width))]
        + [(a, whole(a)) for a in (w_output, w_in, w_down, gain)],
        results,
        [pltpu.VMEM((rows, width), jnp.float32)],
        90 * 10**9,
    )


def run_feed_backward(dy, slopes, w_in, w_down, rows):
    tokens, width = dy.shape
    window = w_down.shape[0]

    def token(columns):
        return pl.BlockSpec((rows, columns), lambda i: (i, 0))

    columns = (2 * window, width)
    return pl.pallas_call(
        functools.partial(feed_backward, window),
        grid=(tokens // rows,),
        in_specs=[token(width), token(2 * window), whole(w_in), whole(w_down)],
        out_specs=[token(c) for c in columns],
        out_shape=[jax.ShapeDtypeStruct((tokens, c), dy.dtype) for c in columns],
        compiler_params=pltpu.CompilerParams(vmem_limit_bytes=60 * 1024 * 1024),
        cost_estimate=pl.CostEstimate(flops=30 * 10**9, bytes_accessed=40 * 10**6, transcendentals=0),
    )(dy, slopes, w_in, w_down)


def feed_gradients(in_ref, dlin_ref, product_ref, dy_ref, glin_ref, gdown_ref):
    glin_ref[...] = dot_tn(in_ref[...], dlin_ref[...]).astype(glin_ref.dtype)
    gdown_ref[...] = dot_tn(product_ref[...], dy_ref[...]).astype(gdown_ref.dtype)


def run_feed_gradients(tasks, axes, ident, mlp_in, d_lin, product, dy):
    tokens, width = mlp_in.shape
    window = product.shape[1]
    wide = 256
    if tokens > 2048:
        kind = mlp_in.dtype
        return (
            *exchange(tasks, axes, ident),
            contract_rows(mlp_in, d_lin).astype(kind),
            contract_rows(product, dy).astype(kind),
        )

    def columns(rows):
        return pl.BlockSpec((rows, wide), lambda i: (0, i))

    return exchange_beside(
        tasks,
        axes,
        ident,
        feed_gradients,
        width // wide,
        4.0,
        [
            (mlp_in, columns(tokens)),
            (d_lin, whole(d_lin)),
            (product, whole(product)),
            (dy, columns(tokens)),
        ],
        [
            (
                pl.BlockSpec((wide, 2 * window), lambda i: (i, 0)),
                jax.ShapeDtypeStruct((width, 2 * window), mlp_in.dtype),
            ),
            (columns(window), jax.ShapeDtypeStruct((window, width), mlp_in.dtype)),
        ],
        [],
        90 * 10**9,
    )


def project(left_side, right_side):
    return jnp.dot(left_side, right_side, preferred_element_type=jnp.float32)


def times_t(left_side, right_side):
    return lax.dot_general(
        left_side, right_side, (((1,), (1,)), ((), ())), preferred_element_type=jnp.float32
    )


def contract_rows(left_side, right_side):
    return lax.dot_general(
        left_side, right_side, (((0,), (0,)), ((), ())), preferred_element_type=jnp.float32
    )


def rms(values, gain, eps):
    return values * lax.rsqrt(jnp.mean(values * values, axis=-1, keepdims=True) + eps) * gain


def rms_back(values, gain, eps, grad):
    r = lax.rsqrt(jnp.mean(values * values, axis=-1, keepdims=True) + eps)
    inner = jnp.mean(values * gain * grad, axis=-1, keepdims=True)
    return r * gain * grad - values * (r * r * r) * inner, grad * values * r


def deal(stacked):
    return lax.all_to_all(stacked, "shard", split_axis=0, concat_axis=0, tiled=True)


def cross(blocks):
    shards = lax.axis_size("shard")
    return lax.ppermute(blocks, "shard", [(s, s ^ 1) for s in range(shards)])


def column_windows(columns, shards):
    own = columns // shards
    tiles = columns // HD
    width = 1
    while any(min(s * own // HD, tiles - width) * HD + width * HD < (s + 1) * own for s in range(shards)):
        width += 1

    def first(s):
        if isinstance(s, int):
            return min(s * own // HD, tiles - width) * HD
        return jnp.minimum(lax.div(s * own, HD), tiles - width) * HD

    return first, width * HD


def place_windows(kinds, shards, columns, window, first, own, in_ref, *out_refs):
    for kind, out_ref in zip(range(kinds), out_refs):
        for tile in range(columns // HD):
            total = None
            for s in range(shards):
                low = max(tile * HD, s * own)
                high = min((tile + 1) * HD, (s + 1) * own)
                if low < high:
                    at = kind * window + tile * HD - first(s)
                    term = in_ref[0, s, :, at : at + HD].astype(jnp.float32)
                    total = term if total is None else total + term
            out_ref[:, tile * HD : (tile + 1) * HD] = total


def widen(collected, kinds, columns, window, first):
    replicas, shards, part, wide = collected.shape
    return pl.pallas_call(
        functools.partial(place_windows, kinds, shards, columns, window, first, columns // shards),
        grid=(replicas,),
        in_specs=[pl.BlockSpec((1, shards, part, wide), lambda i: (i, 0, 0, 0))],
        out_specs=[pl.BlockSpec((part, columns), lambda i: (i, 0))] * kinds,
        out_shape=[jax.ShapeDtypeStruct((replicas * part, columns), jnp.float32)] * kinds,
        compiler_params=pltpu.CompilerParams(vmem_limit_bytes=48 * 1024 * 1024),
    )(collected)


def body(
    layer_input,
    out_cotangent,
    seq_lengths,
    seq_order,
    w_query,
    w_key,
    w_value,
    w_beta,
    w_outgate,
    w_output,
    conv_query,
    conv_key,
    conv_value,
    attn_gain,
    head_gain,
    mlp_gain,
    w_gate,
    w_up,
    w_down,
):
    bf16, f32 = jnp.bfloat16, jnp.float32
    shards = lax.axis_size("shard")
    shard = lax.axis_index("shard")
    both, group = ("shard", "replica"), ("shard",)
    rows, width = layer_input.shape
    tokens = shards * rows
    weight_rows = w_query.shape[0]
    own = w_output.shape[0]
    heads = own // HD
    hidden_own = w_down.shape[0]
    ffn = w_gate.shape[1]
    ffn_first, ffn_window = column_windows(ffn, shards)
    col_first, col_window = column_windows(width, shards)
    shift = shard * hidden_own - ffn_first(shard)

    total_heads = w_beta.shape[1]
    head_part = jnp.pad(head_gain, (0, weight_rows - head_gain.shape[0]))
    little = jnp.concatenate([w_beta, jnp.stack([attn_gain, mlp_gain, head_part], axis=1)], axis=1)
    little = jnp.pad(little, ((0, 0), (0, HD - little.shape[1])))
    attn_weights, all_source, little = exchange(
        [
            Spread((w_query, w_key, w_value, w_outgate), col_window, col_first, -0.5, 12.0),
            Gather("shard", layer_input, 8, turned=True),
            Gather("shard", little, 1, 0.0, 20.0),
        ],
        both,
        0,
    )
    full_attn_gain = little[:, :, total_heads].reshape(width).astype(f32)
    full_mlp_gain = little[:, :, total_heads + 1].reshape(width).astype(f32)
    head_row = little[:, : head_gain.shape[0], total_heads + 2].reshape(1, HD).astype(f32)
    beta = lax.dynamic_slice_in_dim(little.reshape(width, HD), shard * heads, heads, axis=1)
    attn_weights = jnp.concatenate(
        [attn_weights.reshape(width, 4 * own), jnp.pad(beta, ((0, 0), (0, HD - heads)))], axis=1
    )
    replicas = lax.axis_size("replica")
    part = weight_rows // replicas
    at = lax.axis_index("replica") * part
    windows = [
        lax.slice_in_dim(w, ffn_first(s), ffn_first(s) + ffn_window, axis=1)
        for s in range(shards)
        for w in (
            lax.dynamic_slice_in_dim(w_gate, at, part),
            lax.dynamic_slice_in_dim(w_up, at, part),
        )
    ]
    mlp_weights = jnp.stack(
        [jnp.concatenate(windows[2 * s : 2 * s + 2], axis=1) for s in range(shards)]
    )
    full_output = jnp.broadcast_to(
        lax.dynamic_slice_in_dim(w_output, at, part)[None], (shards, part, width)
    )
    later_weights = jnp.concatenate([mlp_weights, full_output], axis=2)
    later_weights, all_source = lax.optimization_barrier((later_weights, all_source))
    later_weights = deal(later_weights)
    mlp_weights = later_weights[..., : 2 * ffn_window]
    full_output = later_weights[..., 2 * ffn_window :]
    low, off, rem = segment_masks(seq_lengths[0], seq_order[0], shards, rows)

    source = layer_input.astype(f32)
    all_source = all_source.reshape(tokens, width)
    normed = rms(all_source.astype(f32), full_attn_gain, 1e-6).astype(bf16)
    projected = project(normed, attn_weights).reshape(shards, rows, -1)
    taps = jnp.concatenate([conv_query, conv_key, conv_value], axis=0).astype(f32)
    zed, mixed, sums, *saves = mixer_forward(projected, taps, head_row, low, off, rem, heads)
    all_zed, mlp_weights, full_output = exchange(
        [
            Gather("shard", zed.reshape(tokens, own), 8, 0.0, 21.0, True, True),
            Trade(mlp_weights, 0.2, 31.0),
            Trade(full_output, 0.1, 42.0),
        ],
        both,
        2,
    )
    zed = zed.reshape(tokens, own)
    mlp_weights = mlp_weights.reshape(width, 2 * ffn_window)
    w_down = lax.dynamic_update_slice(jnp.zeros((ffn_window, width), bf16), w_down, (shift, 0))
    dy, hidden, mlp_in, product, slopes, out_terms = run_feed_forward(
        [Gather("shard", out_cotangent, 8, turned=True)],
        group,
        3,
        all_zed,
        all_source,
        full_output.reshape(width, width),
        mlp_weights,
        w_down,
        full_mlp_gain[None, :],
        rows,
    )
    dy = dy.reshape(tokens, width)
    d_lin, d_terms = run_feed_backward(dy, slopes, mlp_weights, w_down, rows)
    d_mlp_in, g_lin, g_down = run_feed_gradients(
        [Scatter("shard", d_terms, 4)], group, 4, mlp_in, d_lin, product, dy
    )
    d_hidden_norm, g_mlp_rows = rms_back(hidden, full_mlp_gain, 1e-6, d_mlp_in)
    d_hidden = out_cotangent.astype(f32) + d_hidden_norm

    d_attn, g_lin, g_down = exchange(
        [
            Gather("shard", d_hidden.astype(bf16), 8, turned=True),
            Sum(g_lin, 0.5, 20.0),
            Total(g_down, 0.7, 16.0),
        ],
        both,
        5,
    )
    g_lin, d_attn = lax.optimization_barrier((g_lin, d_attn))
    g_lin = deal(g_lin)
    d_attn = d_attn.reshape(tokens, width)
    g_output = contract_rows(zed, d_attn).astype(bf16)
    d_zed = times_t(d_attn, w_output).reshape(shards, rows, own)
    d_proj, g_taps, g_head = mixer_backward(
        projected, sums, mixed, d_zed, taps, head_row, low, off, rem, saves, heads
    )
    d_proj = d_proj.reshape(tokens, -1)
    g_proj = contract_rows(normed, d_proj).astype(bf16)
    d_normed, g_proj, g_output, g_lin = exchange(
        [
            Scatter("shard", times_t(d_proj, attn_weights).astype(bf16), 4),
            Sum(g_proj, 0.5, 16.0),
            Total(g_output, 0.7, 14.0),
            Gather("replica", g_lin.reshape(-1, 2 * ffn_window), 4, 0.3, 31.0),
        ],
        both,
        6,
    )
    d_source, g_attn_rows = rms_back(source, full_attn_gain, 1e-6, d_normed)

    def dealt(values):
        return values.reshape(shards, -1)

    small = jnp.concatenate(
        [dealt(jnp.sum(g_attn_rows, axis=0)), dealt(jnp.sum(g_mlp_rows, axis=0)), dealt(g_head)], axis=1
    )
    small = jnp.pad(small, ((0, 0), (0, -small.shape[1] % HD)))
    small = jnp.broadcast_to(small[:, None, :], (shards, 8, small.shape[1]))
    out_terms, g_proj, small, g_taps = exchange(
        [
            Scatter("shard", out_terms, 4),
            Deliver(g_proj, -0.4, 30.0, 24.0),
            Small(small, jnp.pad(g_taps, ((0, 16 - g_taps.shape[0]), (0, 0))), 50.0),
        ],
        both,
        7,
    )
    g_lin = g_lin.reshape(replicas, shards, -1, 2 * ffn_window)
    g_query, g_key, g_value, g_outgate = widen(g_proj, 4, width, col_window, col_first)
    g_gate, g_up = widen(g_lin, 2, ffn, ffn_window, ffn_first)
    g_beta = g_proj[..., 4 * own : 4 * own + heads].transpose(0, 2, 1, 3)
    g_down = lax.dynamic_slice_in_dim(g_down.reshape(-1, width), shift, hidden_own)
    gains = width // shards
    return (
        (hidden + out_terms).astype(bf16),
        (d_hidden + d_source).astype(bf16),
        g_query,
        g_key,
        g_value,
        g_beta.reshape(weight_rows, total_heads).astype(f32),
        g_outgate,
        g_output.reshape(own, width).astype(f32),
        g_taps[:TAPS],
        g_taps[TAPS : 2 * TAPS],
        g_taps[2 * TAPS : 3 * TAPS],
        small[0, :gains],
        small[0, 2 * gains : 2 * gains + head_gain.shape[0]],
        small[0, gains : 2 * gains],
        g_gate,
        g_up,
        g_down.astype(f32),
    )


def solution(mesh):
    tokens = P(("replica", "shard"), None)
    whole, columns, vector = P("shard", None), P(None, "shard"), P("shard")
    in_specs = (tokens, tokens, P("replica", None, None), P("replica", None)) + (whole,) * 6
    in_specs += (columns,) * 3 + (vector,) * 3 + (whole,) * 3
    out_specs = (tokens, tokens) + (whole,) * 6 + (columns,) * 3 + (vector,) * 3 + (whole,) * 3
    return jax.shard_map(body, mesh=mesh, in_specs=in_specs, out_specs=out_specs, check_vma=False)
```

```python
import functools

import jax
import jax.numpy as jnp
from jax import lax
from jax.experimental import pallas as pl
from jax.experimental.pallas import tpu as pltpu
from jax.sharding import PartitionSpec as P

MESH = pl.DeviceIdType.MESH
ANY = pl.BlockSpec(memory_space=pl.ANY)
VMEM = pl.BlockSpec(memory_space=pltpu.VMEM)
DMA = pltpu.SemaphoreType.DMA
UP, DOWN, RIGHT, LEFT = range(4)


def grid_of(axis):
    count = lax.axis_size(axis)
    if axis == "replica":
        across = 2 if count % 2 == 0 else 1
        return count // across, across
    depth = 4 if count % 4 == 0 else count
    return depth, count // depth


class Lines:
    def __init__(self, axis):
        self.axis = axis
        self.Z, self.X = grid_of(axis)
        self.count = self.Z * self.X
        self.me = lax.axis_index(axis)
        self.z, self.x = lax.div(self.me, self.X), lax.rem(self.me, self.X)
        z, x, X = self.z, self.x, self.X
        self.targets = ((z + 1) * X + x, (z - 1) * X + x, z * X + x + 1, z * X + x - 1)
        self.exists = (z < self.Z - 1, z > 0, x < X - 1, x > 0)

    def to(self, way):
        return {self.axis: self.targets[way]}

    def other(self, k):
        return lax.rem(self.me + k, self.count)

    def slot(self, zz, xx):
        return zz * self.X + xx


class Turned(Lines):
    def __init__(self, line):
        self.axis, self.count, self.me = line.axis, line.count, line.me
        self.Z, self.X, self.z, self.x = line.X, line.Z, line.x, line.z
        self.targets = line.targets[2:] + line.targets[:2]
        self.exists = line.exists[2:] + line.exists[:2]

    def slot(self, zz, xx):
        return xx * self.Z + zz


class Column(Lines):
    def __init__(self, line):
        self.axis, self.count, self.me = line.axis, line.Z, line.z
        self.Z, self.X, self.z, self.x = line.Z, 1, line.z, jnp.int32(0)
        self.targets = line.targets
        self.exists = line.exists[:2] + (jnp.bool_(False),) * 2

    def slot(self, zz, xx):
        return zz


def greet(lines, everyone):
    barrier = pltpu.get_barrier_semaphore()
    count = jnp.int32(0)
    for line in lines:
        if line.axis in everyone:
            for k in range(1, line.count):
                pl.semaphore_signal(
                    barrier, inc=1, device_id={line.axis: line.other(k)}, device_id_type=MESH
                )
            count = count + (line.count - 1)
            continue
        for way in range(4):

            @pl.when(line.exists[way])
            def _(line=line, way=way):
                pl.semaphore_signal(barrier, inc=1, device_id=line.to(way), device_id_type=MESH)

            count = count + jnp.where(line.exists[way], 1, 0)
    pl.semaphore_wait(barrier, count)


def remote(src, dst, send_sem, recv_sem, device):
    return pltpu.make_async_remote_copy(
        src_ref=src,
        dst_ref=dst,
        send_sem=send_sem,
        recv_sem=recv_sem,
        device_id=device,
        device_id_type=MESH,
    )


def in_place(view, sem):
    return pltpu.make_async_copy(view, view, sem)


def staged(src, dst, held, sems):
    load = pltpu.make_async_copy(src, held, sems.at[0])
    save = pltpu.make_async_copy(held, dst, sems.at[1])

    def turn():
        load.wait()
        save.start()

    return load.start, turn, save.wait


def gather_sems(axis, chunks):
    Z, X = grid_of(axis)
    return [DMA((4, Z * X, chunks)), DMA((Z * X, chunks))]


def gather_steps(line, chunks, view, source, ready, sems, start, pace):
    send_sem, recv_sem = sems
    Z, X, z, x, me = line.Z, line.X, line.z, line.x, line.me
    exists = line.exists

    def copy(way, origin, c, src=None):
        spot = view(origin, c)
        return remote(
            spot if src is None else src,
            spot,
            send_sem.at[way, origin, c],
            recv_sem.at[origin, c],
            line.to(way),
        )

    def first(c):
        ready(c)
        for way in range(4):

            @pl.when(exists[way])
            def _(way=way):
                copy(way, me, c, source(c)).start()

    def hop(d, c):
        for way, here in ((UP, z - d >= 0), (DOWN, z + d < Z)):

            @pl.when(here)
            def _(way=way):
                origin = line.slot(z - d if way == UP else z + d, x)
                copy(way, origin, c).wait_recv()
                for onward in (way, RIGHT, LEFT):

                    @pl.when(exists[onward])
                    def _(onward=onward):
                        copy(onward, origin, c).start()

    def across(e, level, c):
        for way, here in ((RIGHT, x - e >= 0), (LEFT, x + e < X)):

            @pl.when(here)
            def _(way=way):
                origin = line.slot(level, x - e if way == RIGHT else x + e)
                copy(way, origin, c).wait_recv()
                if X > 2:

                    @pl.when(exists[way])
                    def _():
                        copy(way, origin, c).start()

    def finish():
        for c in range(chunks):
            for zz in range(Z):
                for way, here in ((UP, zz <= z), (DOWN, zz >= z)):

                    @pl.when(exists[way] & here)
                    def _(way=way, zz=zz, c=c):
                        copy(way, line.slot(zz, x), c).wait_send()

                for xx in range(X):
                    for way, here in ((RIGHT, xx <= x), (LEFT, xx >= x)):

                        @pl.when(exists[way] & here)
                        def _(way=way, zz=zz, xx=xx, c=c):
                            copy(way, line.slot(zz, xx), c).wait_send()

    steps = []
    for c in range(chunks):
        steps.append((start + pace * c / chunks, functools.partial(first, c)))
    for d in range(1, Z):
        for c in range(chunks):
            steps.append((start + pace * (d - 1 + (c + 1) / chunks), functools.partial(hop, d, c)))
    for e in range(1, X):
        for dz in range(Z):
            level = lax.rem(z + dz, Z)
            for c in range(chunks):
                when = start + pace * (Z + e + (dz * chunks + c) / (Z * chunks))
                steps.append((when, functools.partial(across, e, level, c)))
    steps.append((start + pace * (Z + X + 1), finish))
    return steps


def scatter_slots(dims):
    Z, X = dims
    if X == 1:
        return Z, 1
    if X == 2:
        return Z, Z
    return Z * X, Z * (X + 1)


def scatter_scratch(dims, chunks, rows, width, kind):
    Z, X = dims
    held, across = scatter_slots(dims)
    return [
        pltpu.VMEM((held, chunks, rows, width), kind),
        pltpu.VMEM((across, chunks, rows, width), kind),
        pltpu.VMEM((Z + 1, chunks, rows, width), kind),
        DMA((held,)),
        DMA((Z * X, chunks)),
        DMA((across, chunks)),
        DMA((Z, chunks)),
        DMA((Z + 1, chunks)),
    ]


STEP = 16


def stride(rows):
    return max(n for n in (16, 32, 64) if rows % n == 0 and n <= BIG)


BIG = 64


def far_first(count, at):
    order = []
    for k in range(count - 1):
        order += [place for place, here in ((count - 1 - k, count - 1 - k > at), (k, k < at)) if here]
    return order + [at]


def scatter_steps(
    line, chunks, block, piece, scratch, store, done, start, pace, launches=None, lag=0.0
):
    mine, from_x, from_z, load_sem, xs_sem, xr_sem, zs_sem, zr_sem = scratch
    Z, X, z, x = line.Z, line.X, line.z, line.x
    exists = line.exists
    rows = mine.shape[2]
    step = stride(rows)

    def spot(zz, xx):
        return zz if X <= 2 else zz * X + xx

    def load(zz, xx):
        at = spot(zz, xx)
        return pltpu.make_async_copy(block(line.slot(zz, xx)), mine.at[at], load_sem.at[at])

    def x_landing(zz, xx, right, receiver):
        if X <= 2:
            return zz
        return zz * (X + 1) + (xx if right else jnp.where(xx == receiver, X, xx))

    def x_copy(right, zz, xx, c):
        landing = x_landing(zz, xx, right, x + 1 if right else x - 1)
        src = piece(line.slot(zz, xx), c) if X <= 2 else mine.at[spot(zz, xx), c]
        return remote(
            src,
            from_x.at[landing, c],
            xs_sem.at[zz * X + xx, c],
            xr_sem.at[landing, c],
            line.to(RIGHT if right else LEFT),
        )

    def z_copy(up, zz, c):
        landing = zz if up else jnp.where(zz == z - 1, Z, zz)
        return remote(
            mine.at[spot(zz, x), c],
            from_z.at[landing, c],
            zs_sem.at[zz, c],
            zr_sem.at[landing, c],
            line.to(UP if up else DOWN),
        )

    def wait_in(buffer, sem, at, c):
        in_place(buffer.at[at, c], sem.at[at, c]).wait()

    def add_in(at, buffer, landing, c):
        def body(i, carry):
            part = pl.ds(pl.multiple_of(i * step, step), step)
            mine[at, c, part] = (
                mine[at, c, part].astype(jnp.float32) + buffer[landing, c, part].astype(jnp.float32)
            ).astype(mine.dtype)
            return carry

        lax.fori_loop(0, rows // step, body, 0)

    def x_line(zz):
        for k in range(X - 1):
            for right, xx, here in ((True, X - 1 - k, X - 1 - k > x), (False, k, k < x)):

                @pl.when(here)
                def _(right=right, xx=xx):
                    if X > 2:
                        load(zz, xx).wait()
                    for c in range(chunks):
                        if X > 2:

                            @pl.when(exists[LEFT if right else RIGHT])
                            def _(c=c):
                                landing = x_landing(zz, xx, right, jnp.int32(-1))
                                wait_in(from_x, xr_sem, landing, c)
                                add_in(spot(zz, xx), from_x, landing, c)

                        x_copy(right, zz, xx, c).start()

    def x_join(zz, c):
        at = spot(zz, x)
        if X == 2:
            wait_in(from_x, xr_sem, zz, c)
            add_in(at, from_x, zz, c)
        elif X > 2:
            for right in (True, False):

                @pl.when(exists[LEFT if right else RIGHT])
                def _(right=right):
                    landing = zz * (X + 1) + (x if right else X)
                    wait_in(from_x, xr_sem, landing, c)
                    add_in(at, from_x, landing, c)

    def ways(k):
        return ((True, Z - 1 - k, Z - 1 - k > z), (False, k, k < z))

    def begin():
        for zz in range(Z):
            for xx in range(X):
                if X > 2:
                    load(zz, xx).start()
            if X <= 2:
                load(zz, x).start()
        for k in range(Z - 1):
            for up, zz, here in ways(k):

                @pl.when(here)
                def _(zz=zz):
                    x_line(zz)

        x_line(z)

    def pass_on(k, c):
        for up, zz, here in ways(k):

            @pl.when(here)
            def _(up=up, zz=zz):
                if c == 0:
                    load(zz, x).wait()
                x_join(zz, c)

                @pl.when(exists[DOWN if up else UP])
                def _():
                    wait_in(from_z, zr_sem, zz, c)
                    add_in(spot(zz, x), from_z, zz, c)

                z_copy(up, zz, c).start()

    def settle(c):
        if c == 0:
            load(z, x).wait()
        x_join(z, c)

        @pl.when(exists[DOWN])
        def _():
            wait_in(from_z, zr_sem, z, c)

        @pl.when(exists[UP])
        def _():
            wait_in(from_z, zr_sem, Z, c)

        def body(i, carry):
            part = pl.ds(pl.multiple_of(i * step, step), step)
            total = mine[spot(z, x), c, part].astype(jnp.float32)
            below = from_z[z, c, part].astype(jnp.float32)
            above = from_z[Z, c, part].astype(jnp.float32)
            total = total + jnp.where(z > 0, below, 0.0)
            total = total + jnp.where(z < Z - 1, above, 0.0)
            store(c, part, total)
            return carry

        lax.fori_loop(0, rows // step, body, 0)
        done(c)

    def finish():
        for zz in range(Z):
            for c in range(chunks):
                for xx in range(X):

                    @pl.when(xx != x)
                    def _(zz=zz, xx=xx, c=c):
                        x_copy(True, zz, xx, c).wait_send()

                @pl.when(zz != z)
                def _(zz=zz, c=c):
                    z_copy(True, zz, c).wait_send()

    tables = []
    for at in range(Z):
        tables.append(far_first(Z, at))

    def visited(i):
        return sum(jnp.where(z == at, tables[at][i], 0) for at in range(Z))

    def launch(i):
        if i < Z:
            x_line(visited(i))
        else:
            load(visited(i - Z), x).start()

    if launches is not None:
        launches.append((visited, launch))
    steps = [] if launches is not None else [(start, begin)]
    for k in range(Z - 1):
        for c in range(chunks):
            steps.append(
                (start + pace * (k + (c + 1) / chunks), functools.partial(pass_on, k, c))
            )
    for c in range(chunks):
        when = start + lag + pace * (Z - 1 + (c + 1) / chunks)
        steps.append((when, functools.partial(settle, c)))
    steps.append((start + lag + pace * (Z + 2), finish))
    return steps


class Gather:
    def __init__(self, axis, block, chunks, start=0.0, pace=21.0, beside=False, turned=False):
        self.axis, self.chunks, self.start, self.pace = axis, chunks, start, pace
        self.beside, self.turned = beside, turned
        self.inputs = [block]
        self.everyone = ()
        count = lax.axis_size(axis)
        rows, width = block.shape
        shape = (rows, count * width) if beside else (count, rows, width)
        self.outputs = [(ANY, jax.ShapeDtypeStruct(shape, block.dtype))]
        self.scratch = [pltpu.VMEM(block.shape, block.dtype), DMA((2,))]
        self.scratch += gather_sems(axis, chunks - turned)
        if turned:
            self.scratch += gather_sems(axis, 1)

    def steps(self, lines, ins, outs, scratch):
        line, (x_ref,), (out_ref,) = lines[self.axis], ins, outs
        held, own_sems, *sems = scratch
        rows, width = x_ref.shape[0] // self.chunks, x_ref.shape[1]

        def view(origin, part):
            if self.beside:
                return out_ref.at[part, pl.ds(pl.multiple_of(origin * width, HD), width)]
            return out_ref.at[origin, part]

        begin, turn, end = staged(x_ref, view(line.me, pl.ds(0, x_ref.shape[0])), held, own_sems)

        def part_steps(line, first, count, sems, start):
            def part(c):
                return pl.ds((first + c) * rows, rows)

            return gather_steps(
                line,
                count,
                lambda origin, c: view(origin, part(c)),
                lambda c: x_ref.at[part(c)],
                lambda c: None,
                sems,
                start,
                self.pace,
            )

        straight = self.chunks - self.turned
        steps = part_steps(line, 0, straight, sems[:2], self.start)
        if self.turned:
            steps += part_steps(Turned(line), straight, 1, sems[2:], self.start + 0.9 * self.pace)
        return [(self.start, begin), (self.start + 0.95 * self.pace, turn)] + steps + [(steps[-1][0], end)]


class Scatter:
    def __init__(self, axis, terms, chunks, start=0.0, pace=21.0, turned=False, column=False):
        self.axis, self.chunks, self.start, self.pace = axis, chunks, start, pace
        self.turned, self.column = turned, column
        dims = grid_of(axis)
        if column:
            dims = (dims[0], 1)
        count = dims[0] * dims[1]
        rows, width = terms.shape[0] // count // chunks, terms.shape[1]
        self.inputs = [terms.reshape(count, chunks, rows, width)]
        self.everyone = ()
        self.outputs = [(VMEM, jax.ShapeDtypeStruct((chunks * rows, width), jnp.float32))]
        self.scratch = scatter_scratch(dims, chunks - turned, rows, width, terms.dtype)
        self.half = len(self.scratch)
        if turned:
            self.scratch += scatter_scratch(dims[::-1], 1, rows, width, terms.dtype)

    def steps(self, lines, ins, outs, scratch):
        (p_ref,), (out_ref,) = ins, outs
        rows = p_ref.shape[2]

        def part_steps(line, first, count, scratch, start):
            def store(c, part, total):
                at = pl.multiple_of((first + c) * rows + part.start, STEP)
                out_ref[pl.ds(at, part.size)] = total

            return scatter_steps(
                line,
                count,
                lambda slot: p_ref.at[slot, pl.ds(first, count)],
                lambda slot, c: p_ref.at[slot, first + c],
                scratch,
                store,
                lambda c: None,
                start,
                self.pace,
            )

        line, straight = lines[self.axis], self.chunks - self.turned
        if self.column:
            line = Column(line)
        steps = part_steps(line, 0, straight, scratch[: self.half], self.start)
        if self.turned:
            steps += part_steps(Turned(line), straight, 1, scratch[self.half :], self.start + 0.01)
        return steps


class Computed(Scatter):
    def __init__(self, axis, rows, width, kind, chunks, start=0.0, pace=21.0):
        self.axis, self.chunks, self.start, self.pace = axis, chunks, start, pace
        self.everyone, self.inputs = (), []
        dims = grid_of(axis)
        count = dims[0] * dims[1]
        self.outputs = [(VMEM, jax.ShapeDtypeStruct((rows, width), jnp.float32))]
        self.scratch = [pltpu.VMEM((count, chunks, rows // chunks, width), kind)]
        self.scratch += scatter_scratch(dims, chunks, rows // chunks, width, kind)

    def steps(self, lines, ins, outs, scratch):
        terms, *rest = scratch
        (out_ref,) = outs
        line = lines[self.axis]
        rows = terms.shape[2]
        launches = []

        def store(c, part, total):
            out_ref[pl.ds(pl.multiple_of(c * rows + part.start, STEP), part.size)] = total

        steps = scatter_steps(
            line,
            self.chunks,
            lambda slot: terms.at[slot],
            lambda slot, c: terms.at[slot, c],
            rest,
            store,
            lambda c: None,
            self.start,
            self.pace,
            launches,
        )
        visited, self.launch = launches[0]

        def slot(i):
            other = i < line.Z
            return line.slot(visited(i % line.Z), 1 - line.x if other else line.x)

        self.slot, self.terms = slot, terms
        return steps


class Spread:
    def __init__(self, weights, window, first, start=0.0, pace=6.0):
        self.inputs = list(weights)
        self.window, self.first, self.start, self.pace = window, first, start, pace
        self.everyone = ("shard",)
        shards, replicas = lax.axis_size("shard"), lax.axis_size("replica")
        self.part = weights[0].shape[0] // replicas
        wide = len(weights) * window
        shape = (shards, replicas, self.part, wide)
        self.outputs = [(ANY, jax.ShapeDtypeStruct(shape, weights[0].dtype))]
        self.scratch = [
            DMA((len(weights),)),
            DMA((len(weights), shards)),
            DMA((len(weights), shards)),
        ] + gather_sems("replica", shards)

    def steps(self, lines, ins, outs, scratch):
        own_sem, deal_send, deal_recv, *sems = scratch
        (out_ref,) = outs
        group, copies = lines["shard"], lines["replica"]
        rows = pl.ds(pl.multiple_of(copies.me * self.part, self.part), self.part)
        kinds = range(len(ins))

        def source(kind, target):
            return ins[kind].at[rows, pl.ds(pl.multiple_of(self.first(target), 128), self.window)]

        def landing(kind, origin):
            return out_ref.at[origin, copies.me, :, pl.ds(kind * self.window, self.window)]

        def own(kind):
            return pltpu.make_async_copy(
                source(kind, group.me), landing(kind, group.me), own_sem.at[kind]
            )

        def deal(kind, k):
            target = group.other(k)
            return remote(
                source(kind, target),
                landing(kind, group.me),
                deal_send.at[kind, k],
                deal_recv.at[kind, group.me],
                {"shard": target},
            )

        def begin():
            for k in range(1, group.count):
                for kind in kinds:
                    deal(kind, k).start()
            for kind in kinds:
                own(kind).start()

        def ready(c):
            @pl.when(c == group.me)
            def _():
                for kind in kinds:
                    own(kind).wait()

            @pl.when(c != group.me)
            def _():
                for kind in kinds:
                    in_place(landing(kind, c), deal_recv.at[kind, c]).wait()

        def finish():
            for k in range(1, group.count):
                for kind in kinds:
                    deal(kind, k).wait_send()

        steps = gather_steps(
            copies,
            group.count,
            lambda origin, c: out_ref.at[c, origin],
            lambda c: out_ref.at[c, copies.me],
            ready,
            sems,
            self.start + 2 * self.pace,
            2 * self.pace,
        )
        return [(self.start, begin)] + steps + [(steps[-1][0], finish)]


class Trade:
    def __init__(self, block, first, width, start=0.0, pace=6.0):
        self.inputs = [block]
        self.first, self.width, self.start, self.pace = first, width, start, pace
        self.everyone = ()
        shards, part, _ = block.shape
        shape = (shards, lax.axis_size("replica"), part, width)
        self.outputs = [(ANY, jax.ShapeDtypeStruct(shape, block.dtype))]
        self.scratch = [pltpu.VMEM((shards, part, width), block.dtype), DMA((2,))]
        self.scratch += gather_sems("replica", shards)

    def steps(self, lines, ins, outs, scratch):
        held, own_sems, *sems = scratch
        (x_ref,), (out_ref,) = ins, outs
        copies = lines["replica"]
        cols = pl.ds(self.first, self.width)
        begin, turn, end = staged(
            x_ref.at[:, :, cols], out_ref.at[:, copies.me], held, own_sems
        )
        steps = gather_steps(
            copies,
            x_ref.shape[0],
            lambda origin, c: out_ref.at[c, origin],
            lambda c: x_ref.at[c, :, cols],
            lambda c: None,
            sems,
            self.start,
            self.pace,
        )
        return [(self.start, begin), (self.start + 3.0, turn)] + steps + [(steps[-1][0], end)]


class Sum:
    def __init__(self, terms, start=0.0, pace=6.0, lag=0.0):
        shards, replicas = lax.axis_size("shard"), lax.axis_size("replica")
        part, wide = terms.shape[0] // shards // replicas, terms.shape[1]
        self.inputs = [terms.reshape(shards, replicas, part, wide)]
        self.start, self.pace, self.lag = start, pace, lag
        self.everyone = ()
        self.outputs = [(VMEM, jax.ShapeDtypeStruct((shards, part, wide), terms.dtype))]
        self.scratch = scatter_scratch(grid_of("replica"), shards, part, wide, terms.dtype)

    def steps(self, lines, ins, outs, scratch):
        (p_ref,), (out_ref,) = ins, outs

        def store(c, part, total):
            out_ref[c, part] = total.astype(out_ref.dtype)

        return scatter_steps(
            lines["replica"],
            out_ref.shape[0],
            lambda slot: p_ref.at[:, slot],
            lambda slot, c: p_ref.at[c, slot],
            scratch,
            store,
            lambda c: None,
            self.start,
            self.pace,
            lag=self.lag,
        )


class Deliver:
    def __init__(self, sums, start=0.0, again=30.0, pace=24.0):
        self.inputs = [sums]
        self.start, self.again, self.pace = start, again, pace
        self.everyone = ("shard",)
        shards, replicas = lax.axis_size("shard"), lax.axis_size("replica")
        self.outputs = [(ANY, jax.ShapeDtypeStruct((replicas,) + sums.shape, sums.dtype))]
        self.scratch = [DMA, DMA((shards,)), DMA((shards,))] + gather_sems("replica", shards)

    def steps(self, lines, ins, outs, scratch):
        own_sem, send_sem, recv_sem, *sems = scratch
        (x_ref,), (out_ref,) = ins, outs
        group, copies = lines["shard"], lines["replica"]
        own = pltpu.make_async_copy(
            x_ref.at[group.me], out_ref.at[copies.me, group.me], own_sem
        )

        def deal(k):
            target = group.other(k)
            return remote(
                x_ref.at[target],
                out_ref.at[copies.me, group.me],
                send_sem.at[k],
                recv_sem.at[group.me],
                {"shard": target},
            )

        def begin():
            own.start()
            for k in range(1, group.count):
                deal(k).start()

        def ready(c):
            @pl.when(c == group.me)
            def _():
                own.wait()

            @pl.when(c != group.me)
            def _():
                in_place(out_ref.at[copies.me, c], recv_sem.at[c]).wait()

        def finish():
            for k in range(1, group.count):
                deal(k).wait_send()

        steps = gather_steps(
            copies,
            group.count,
            lambda origin, c: out_ref.at[origin, c],
            lambda c: out_ref.at[copies.me, c],
            ready,
            sems,
            self.again,
            self.pace,
        )
        return [(self.start, begin)] + steps + [(steps[-1][0], finish)]


class Total:
    def __init__(self, terms, start=0.0, pace=6.0, again=60.0, lag=0.0):
        replicas = lax.axis_size("replica")
        share, wide = terms.shape[0] // replicas, terms.shape[1]
        chunks = max(n for n in (1, 2, 3, 4) if share % (n * STEP) == 0)
        rows = share // chunks
        self.inputs = [terms.reshape(replicas, chunks, rows, wide)]
        self.start, self.pace, self.again, self.chunks = start, pace, again, chunks
        self.lag = lag
        self.everyone = ()
        kind = terms.dtype
        self.outputs = [(ANY, jax.ShapeDtypeStruct((replicas, chunks, rows, wide), kind))]
        self.scratch = [pltpu.VMEM((chunks, rows, wide), kind), DMA((chunks,))]
        self.scratch += gather_sems("replica", chunks)
        self.scratch += scatter_scratch(grid_of("replica"), chunks, rows, wide, kind)

    def steps(self, lines, ins, outs, scratch):
        (p_ref,), (out_ref,) = ins, outs
        total_ref, own_sem = scratch[:2]
        copies = lines["replica"]

        def own(c):
            return pltpu.make_async_copy(
                total_ref.at[c], out_ref.at[copies.me, c], own_sem.at[c]
            )

        def store(c, part, total):
            total_ref[c, part] = total.astype(total_ref.dtype)

        def finish():
            for c in range(self.chunks):
                own(c).wait()

        summing = scatter_steps(
            copies,
            self.chunks,
            lambda slot: p_ref.at[slot],
            lambda slot, c: p_ref.at[slot, c],
            scratch[4:],
            store,
            lambda c: own(c).start(),
            self.start,
            self.pace,
            lag=self.lag,
        )
        sharing = gather_steps(
            copies,
            self.chunks,
            lambda origin, c: out_ref.at[origin, c],
            lambda c: total_ref.at[c],
            lambda c: None,
            scratch[2:4],
            self.again,
            self.pace,
        )
        return summing + sharing + [(sharing[-1][0], finish)]


class Small:
    def __init__(self, dealt, shared, start=0.0):
        shards, replicas = lax.axis_size("shard"), lax.axis_size("replica")
        self.inputs = [dealt, shared]
        self.start = start
        self.everyone = ("shard", "replica")
        one = dealt.shape[1:]
        self.outputs = [
            (VMEM, jax.ShapeDtypeStruct(one, jnp.float32)),
            (VMEM, jax.ShapeDtypeStruct(shared.shape, jnp.float32)),
        ]
        self.scratch = [
            pltpu.VMEM((shards,) + one, jnp.float32),
            pltpu.VMEM((replicas,) + one, jnp.float32),
            pltpu.VMEM((replicas,) + shared.shape, jnp.float32),
            DMA((shards,)), DMA((shards,)),
            DMA((2, replicas)), DMA((2, replicas)), DMA((2,)),
        ]

    def steps(self, lines, ins, outs, scratch):
        dealt, shared = ins
        out_one, out_rows = outs
        got, got_one, got_rows, send, recv, send2, recv2, own = scratch
        group, copies = lines["shard"], lines["replica"]

        def deal(k):
            target = group.other(k)
            return remote(
                dealt.at[target], got.at[group.me], send.at[k], recv.at[group.me], {"shard": target}
            )

        def share(which, k):
            buffer = (got_one, got_rows)[which]
            return remote(
                buffer.at[copies.me] if which == 0 else shared,
                buffer.at[copies.me],
                send2.at[which, k],
                recv2.at[which, copies.me],
                {"replica": copies.other(k)},
            )

        def keep():
            return pltpu.make_async_copy(dealt.at[group.me], got.at[group.me], own.at[0])

        def keep_rows():
            return pltpu.make_async_copy(shared, got_rows.at[copies.me], own.at[1])

        def begin():
            keep().start()
            keep_rows().start()
            for k in range(1, group.count):
                deal(k).start()
            for k in range(1, copies.count):
                share(1, k).start()

        def middle():
            keep().wait()
            for k in range(1, group.count):
                origin = group.other(k)
                in_place(got.at[origin], recv.at[origin]).wait()
            total = got[0]
            for s in range(1, group.count):
                total = total + got[s]
            got_one[copies.me] = total
            for k in range(1, copies.count):
                share(0, k).start()

        def end():
            keep_rows().wait()
            for k in range(1, copies.count):
                origin = copies.other(k)
                in_place(got_one.at[origin], recv2.at[0, origin]).wait()
                in_place(got_rows.at[origin], recv2.at[1, origin]).wait()
            one, rows = got_one[0], got_rows[0]
            for r in range(1, copies.count):
                one, rows = one + got_one[r], rows + got_rows[r]
            out_one[...] = one
            out_rows[...] = rows
            for k in range(1, group.count):
                deal(k).wait_send()
            for k in range(1, copies.count):
                share(0, k).wait_send()
                share(1, k).wait_send()

        return [(-0.5, begin), (self.start, middle), (self.start + 40.0, end)]


def layout_of(tasks):
    inputs, outputs, scratch, spans = [], [], [], []
    for task in tasks:
        spans.append((len(inputs), len(outputs), len(scratch)))
        inputs += task.inputs
        outputs += task.outputs
        scratch += task.scratch
    return inputs, outputs, scratch, spans


def task_steps(tasks, spans, axes, ins, outs, scratch):
    lines = {axis: Lines(axis) for axis in axes}
    everyone = {axis for task in tasks for axis in task.everyone}
    steps = []
    for task, (i, o, s) in zip(tasks, spans):
        steps += task.steps(
            lines,
            ins[i : i + len(task.inputs)],
            outs[o : o + len(task.outputs)],
            scratch[s : s + len(task.scratch)],
        )
    steps.sort(key=lambda step: step[0])
    return [(-1.0, lambda: greet(list(lines.values()), everyone))] + steps


def exchange(tasks, axes, ident):
    inputs, outputs, scratch, spans = layout_of(tasks)

    def kernel(*refs):
        ins = refs[: len(inputs)]
        outs = refs[len(inputs) : len(inputs) + len(outputs)]
        rest = refs[len(inputs) + len(outputs) :]
        for _, step in task_steps(tasks, spans, axes, ins, outs, rest):
            step()

    return pl.pallas_call(
        kernel,
        in_specs=[ANY] * len(inputs),
        out_specs=[spec for spec, _ in outputs],
        out_shape=[shape for _, shape in outputs],
        scratch_shapes=scratch,
        compiler_params=pltpu.CompilerParams(
            collective_id=ident, has_side_effects=True, vmem_limit_bytes=60 * 1024 * 1024
        ),
    )(*inputs)


HD = 128
TAPS = 4
KINDS = 3


def dot_nn(a, b):
    return lax.dot_general(
        a.astype(jnp.bfloat16),
        b.astype(jnp.bfloat16),
        (((1,), (0,)), ((), ())),
        preferred_element_type=jnp.float32,
    )


def dot_nt(a, b):
    return lax.dot_general(
        a.astype(jnp.bfloat16),
        b.astype(jnp.bfloat16),
        (((1,), (1,)), ((), ())),
        preferred_element_type=jnp.float32,
    )


def dot_tn(a, b):
    return lax.dot_general(
        a.astype(jnp.bfloat16),
        b.astype(jnp.bfloat16),
        (((0,), (0,)), ((), ())),
        preferred_element_type=jnp.float32,
    )


def time_of(shape, dim, lanes):
    index = lax.broadcasted_iota(jnp.int32, shape, dim)
    return lax.rem(index, 8) * lanes + lax.div(index, 8)


def lower_inverses(lowers, lanes):
    size = lowers[0].shape[0]
    row_t = time_of((size, size), 0, lanes)
    col_t = time_of((size, size), 1, lanes)
    eye = jnp.where(row_t == col_t, 1.0, 0.0)

    def same(width):
        return lax.div(row_t, width) == lax.div(col_t, width)

    first = [jnp.where(same(8), a, 0.0) for a in lowers]
    second = [dot_nn(f, f) for f in first]
    inverse = [eye + f + s + dot_nn(f, s) for f, s in zip(first, second)]
    fourth = [dot_nn(s, s) for s in second]
    inverse = [t + dot_nn(t, f) for t, f in zip(inverse, fourth)]
    width = 16
    while width <= size:
        fresh = same(width) & jnp.logical_not(same(width // 2))
        left = [dot_nn(t, jnp.where(fresh, a, 0.0)) for t, a in zip(inverse, lowers)]
        inverse = [t + dot_nn(l, t) for t, l in zip(inverse, left)]
        width *= 2
    return inverse


def rounded(values):
    return values.astype(jnp.bfloat16).astype(jnp.float32)


def sigmoid(values):
    return 1.0 / (1.0 + jnp.exp(-values))


def unit_scale(pre):
    return lax.rsqrt(jnp.sum(pre * pre, axis=1, keepdims=True) + 1e-6)


def mean_scale(values):
    return lax.rsqrt(jnp.mean(values * values, axis=1, keepdims=True) + 1e-5)


def delta_forward(
    lanes, heads, group, proj_ref, taps_ref, gain_ref, low_ref, off_ref, rem_ref,
    zed_ref, mixed_ref, sums_ref, s_ref, t_ref, mk_ref, mv_ref, u_ref,
    state, last, unit,
):
    size = lanes * 8
    rows = group * 8
    wide = heads * HD
    scale = HD ** (-0.5)

    @pl.when(pl.program_id(0) == 0)
    def _():
        state[...] = jnp.zeros_like(state)
        last[...] = jnp.zeros_like(last)

    top = lax.broadcasted_iota(jnp.int32, (rows, HD), 0) == 0
    for kind in range(KINDS):
        for h in range(heads):
            cols = pl.ds(kind * wide + h * HD, HD)
            signal = [rounded(proj_ref[s, :, cols]) for s in range(lanes)]
            moved = {}
            for back in range(1, TAPS):
                lane = lanes - back
                edge = last[kind * heads + h, back, 0:1]
                moved[lane] = jnp.where(top, edge, pltpu.roll(signal[lane], 1, 0))
            for back in range(1, TAPS):
                last[kind * heads + h, back, 0:1] = signal[lanes - back][rows - 1 : rows]
            for s in range(lanes):
                off = off_ref[s]
                total = signal[s] * taps_ref[kind * TAPS : kind * TAPS + 1, h * HD : (h + 1) * HD]
                for hop in range(1, TAPS):
                    earlier = signal[s - hop] if s >= hop else moved[lanes + s - hop]
                    tap = taps_ref[kind * TAPS + hop : kind * TAPS + hop + 1, h * HD : (h + 1) * HD]
                    total = total + jnp.where(off >= hop, earlier, 0.0) * tap
                sums_ref[s, :, cols] = total
                pre = total * sigmoid(total)
                if kind < 2:
                    pre = pre * unit_scale(pre)
                unit[s, :, cols] = pre

    row_t = time_of((size, size), 0, lanes)
    col_t = time_of((size, size), 1, lanes)
    local_t = time_of((size, HD), 0, lanes).astype(jnp.float32)
    pairs = [(g, h) for g in range(group) for h in range(heads)]

    def span(g):
        return pl.ds(g * 8, 8)

    def flat(ref, g, first, count=HD):
        return ref[:, span(g), first : first + count].reshape(size, count)

    gates = {}
    for g in range(group):
        logits = flat(proj_ref, g, 4 * wide)
        strength = sigmoid(rounded(logits))
        for h in range(heads):
            gates[g, h] = jnp.broadcast_to(strength[:, h : h + 1], (size, HD))
    keys = {p: flat(unit, p[0], wide + p[1] * HD) for p in pairs}
    kbs = {p: gates[p] * keys[p] for p in pairs}
    lows = {g: low_ref[g].astype(jnp.float32) for g in range(group)}
    lowers = [
        -jnp.where(row_t == col_t, 0.0, lows[p[0]]) * dot_nt(kbs[p], keys[p]) for p in pairs
    ]
    inverses = dict(zip(pairs, lower_inverses(lowers, lanes)))
    mks = {p: dot_nn(inverses[p], kbs[p]) for p in pairs}
    mvs = {
        p: dot_nn(inverses[p], gates[p] * flat(unit, p[0], 2 * wide + p[1] * HD))
        for p in pairs
    }
    queries = {p: flat(unit, p[0], p[1] * HD) for p in pairs}
    scores = {p: lows[p[0]] * dot_nt(queries[p], keys[p]) for p in pairs}
    for g, h in pairs:
        t_ref[g, h] = inverses[g, h].astype(t_ref.dtype)
        mk_ref[g, h] = mks[g, h].astype(mk_ref.dtype)
        mv_ref[g, h] = mvs[g, h].astype(mv_ref.dtype)
    for g in range(group):
        carry = jnp.where(flat(off_ref, g, 0) > local_t, 1.0, 0.0)
        keep = jnp.where(flat(rem_ref, g, 0) + local_t >= size, 1.0, 0.0)
        for h in range(heads):
            p = (g, h)
            held = state[h]
            s_ref[g, h] = held.astype(s_ref.dtype)
            u = mvs[p] - carry * dot_nn(mks[p], held)
            u_ref[g, h] = u.astype(u_ref.dtype)
            state[h] = (carry[0:1] * keep[0:1]) * held + dot_tn(keys[p], keep * u)
            out = (carry * dot_nn(queries[p], held) + dot_nn(scores[p], u)) * scale
            mixed = rounded(out)
            gate = flat(proj_ref, g, 3 * wide + h * HD)
            zed = mixed * mean_scale(mixed) * gain_ref[...] * (gate * sigmoid(gate))
            mixed_ref[:, span(g), h * HD : (h + 1) * HD] = mixed.reshape(lanes, 8, HD).astype(
                mixed_ref.dtype
            )
            zed_ref[:, span(g), h * HD : (h + 1) * HD] = zed.reshape(lanes, 8, HD).astype(
                zed_ref.dtype
            )


def delta_backward(
    lanes, heads, group, proj_ref, sums_ref, mixed_ref, dzed_ref, taps_ref, gain_ref,
    low_ref, off_ref, rem_ref, s_ref, t_ref, mk_ref, mv_ref, u_ref,
    dproj_ref, gtaps_ref, ghead_ref,
    state, edge, edge_off, errs, taps_sum, head_sum,
):
    size = lanes * 8
    rows = group * 8
    wide = heads * HD
    scale = HD ** (-0.5)

    @pl.when(pl.program_id(0) == 0)
    def _():
        state[...] = jnp.zeros_like(state)
        edge[...] = jnp.zeros_like(edge)
        edge_off[...] = jnp.zeros_like(edge_off)
        taps_sum[...] = jnp.zeros_like(taps_sum)
        head_sum[...] = jnp.zeros_like(head_sum)

    row_t = time_of((size, size), 0, lanes)
    col_t = time_of((size, size), 1, lanes)
    local_t = time_of((size, HD), 0, lanes).astype(jnp.float32)
    lane_id = lax.broadcasted_iota(jnp.int32, (size, HD), 1)
    pairs = [(g, h) for g in range(group) for h in range(heads)]

    def span(g):
        return pl.ds(g * 8, 8)

    def flat(ref, g, first, count=HD):
        return ref[:, span(g), first : first + count].reshape(size, count)

    def put(ref, g, first, value):
        ref[:, span(g), first : first + HD] = value.reshape(lanes, 8, HD).astype(ref.dtype)

    gain = gain_ref[...]
    d_out, q, k, v, beta = {}, {}, {}, {}, {}
    pre, scales, slopes = {}, {}, {}
    head_total = jnp.zeros((size, HD), jnp.float32)
    strengths = {}
    carries, keeps, lows = {}, {}, {}
    for g in range(group):
        carries[g] = jnp.where(flat(off_ref, g, 0) > local_t, 1.0, 0.0)
        keeps[g] = jnp.where(flat(rem_ref, g, 0) + local_t >= size, 1.0, 0.0)
        lows[g] = low_ref[g].astype(jnp.float32)
        strengths[g] = sigmoid(rounded(flat(proj_ref, g, 4 * wide)))
    for g, h in pairs:
        p = (g, h)
        mixed = flat(mixed_ref, g, h * HD).astype(jnp.float32)
        gate = flat(proj_ref, g, 3 * wide + h * HD)
        dzed = flat(dzed_ref, g, h * HD)
        s = sigmoid(gate)
        r = mean_scale(mixed)
        through = dzed * (gate * s)
        head_total = head_total + through * mixed * r
        inner = jnp.mean(mixed * gain * through, axis=1, keepdims=True)
        d_mixed = rounded(r * gain * through - mixed * (r * r * r) * inner)
        put(dproj_ref, g, 3 * wide + h * HD, dzed * (mixed * r * gain) * (s * (1.0 + gate * (1.0 - s))))
        d_out[p] = d_mixed * scale
        for kind, store in ((0, q), (1, k), (2, v)):
            total = flat(sums_ref, g, kind * wide + h * HD)
            s = sigmoid(total)
            value = total * s
            slopes[kind, g, h] = s * (1.0 + total * (1.0 - s))
            if kind < 2:
                pre[kind, g, h] = value
                scales[kind, g, h] = unit_scale(value)
                value = value * scales[kind, g, h]
            store[p] = value
        beta[p] = jnp.broadcast_to(strengths[g][:, h : h + 1], (size, HD))
    head_sum[...] += head_total

    scores = {p: lows[p[0]] * dot_nt(q[p], k[p]) for p in pairs}
    du = {p: dot_tn(scores[p], d_out[p]) for p in pairs}
    ds = {p: lows[p[0]] * dot_nt(d_out[p], u_ref[p[0], p[1]]) for p in pairs}
    cdo = {p: carries[p[0]] * d_out[p] for p in pairs}
    dq = {p: dot_nt(cdo[p], s_ref[p[0], p[1]]) + dot_nn(ds[p], k[p]) for p in pairs}
    dk = {p: dot_tn(ds[p], q[p]) for p in pairs}
    lift = {p: dot_tn(q[p], cdo[p]) for p in pairs}
    later = {}
    for g in reversed(range(group)):
        for h in range(heads):
            p = (g, h)
            later[p] = state[h]
            du[p] = du[p] + keeps[g] * dot_nn(k[p], later[p])
            mk = carries[g] * mk_ref[g, h].astype(jnp.float32)
            state[h] = (carries[g][0:1] * keeps[g][0:1]) * later[p] + lift[p] - dot_tn(mk, du[p])
    for p in pairs:
        dk[p] = dk[p] + dot_nt(keeps[p[0]] * u_ref[p[0], p[1]].astype(jnp.float32), later[p])
    dmk = {p: -carries[p[0]] * dot_nt(du[p], s_ref[p[0], p[1]]) for p in pairs}
    xx = {p: dot_tn(t_ref[p[0], p[1]], dmk[p]) for p in pairs}
    yy = {p: dot_tn(t_ref[p[0], p[1]], du[p]) for p in pairs}
    da = {
        p: jnp.where(row_t == col_t, 0.0, lows[p[0]])
        * (dot_nt(xx[p], mk_ref[p[0], p[1]]) + dot_nt(yy[p], mv_ref[p[0], p[1]]))
        for p in pairs
    }
    dkb = {p: xx[p] - dot_nn(da[p], k[p]) for p in pairs}
    dk = {p: dk[p] - dot_tn(da[p], beta[p] * k[p]) + beta[p] * dkb[p] for p in pairs}
    for g in range(group):
        d_logits = jnp.zeros((size, HD), jnp.float32)
        for h in range(heads):
            p = (g, h)
            db = jnp.sum(dkb[p] * k[p] + yy[p] * v[p], axis=1, keepdims=True)
            d_logits = d_logits + jnp.where(lane_id == h, db * beta[p] * (1.0 - beta[p]), 0.0)
            for kind, grad in ((0, dq[p]), (1, dk[p])):
                r, raw = scales[kind, g, h], pre[kind, g, h]
                inner = jnp.sum(raw * grad, axis=1, keepdims=True)
                err = (r * grad - raw * (r * r * r) * inner) * slopes[kind, g, h]
                put(errs, g, kind * wide + h * HD, err)
            put(errs, g, 2 * wide + h * HD, beta[p] * yy[p] * slopes[2, g, h])
        put(dproj_ref, g, 4 * wide, d_logits)

    bottom = lax.broadcasted_iota(jnp.int32, (rows, HD), 0) == rows - 1
    for kind in range(KINDS):
        for h in range(heads):
            at = kind * wide + h * HD
            cols = pl.ds(at, HD)
            err = [errs[s, :, cols] for s in range(lanes)]
            taps = [
                taps_ref[kind * TAPS + hop : kind * TAPS + hop + 1, h * HD : (h + 1) * HD]
                for hop in range(TAPS)
            ]
            sums = [jnp.zeros((rows, HD), jnp.float32) for _ in range(TAPS)]
            live = {}
            for hop in range(1, TAPS):
                for s in range(lanes):
                    live[hop, s] = jnp.where(off_ref[s] >= hop, err[s], 0.0)
            for hop in range(1, TAPS):
                for s in range(hop):
                    row = jnp.where(edge_off[s, 0:1] >= hop, edge[kind * heads + h, s, 0:1], 0.0)
                    live[hop, lanes + s] = jnp.where(
                        bottom, row, pltpu.roll(live[hop, s], rows - 1, 0)
                    )
            for s in range(lanes):
                signal = rounded(proj_ref[s, :, cols])
                total = err[s] * taps[0]
                sums[0] = sums[0] + err[s] * signal
                for hop in range(1, TAPS):
                    total = total + live[hop, s + hop] * taps[hop]
                    sums[hop] = sums[hop] + live[hop, s + hop] * signal
                dproj_ref[s, :, cols] = total.astype(dproj_ref.dtype)
            for s in range(TAPS - 1):
                edge[kind * heads + h, s, 0:1] = err[s][0:1]
            for hop in range(TAPS):
                folded = sums[hop].reshape(group, 8, HD)
                taps_sum[kind * TAPS + hop, :, h * HD : (h + 1) * HD] += jnp.sum(folded, axis=0)
    for s in range(TAPS - 1):
        edge_off[s, 0:1] = off_ref[s][0:1]

    @pl.when(pl.program_id(0) == pl.num_programs(0) - 1)
    def _():
        gtaps_ref[...] = jnp.sum(taps_sum[...], axis=1)
        ghead_ref[...] = jnp.sum(head_sum[...], axis=0, keepdims=True)


def mixer_specs(lanes, heads, group, flip):
    size = lanes * 8
    at = (lambda i: flip - 1 - i) if flip else (lambda i: i)

    def token(width):
        return pl.BlockSpec((lanes, 8 * group, width), lambda i: (0, at(i), 0))

    def saved(first, second):
        return pl.BlockSpec((group, heads, first, second), lambda i: (at(i), 0, 0, 0))

    square = pl.BlockSpec((group, size, size), lambda i: (at(i), 0, 0))
    return token, saved, square


def fixed(shape):
    return pl.BlockSpec(shape, lambda i: (0,) * len(shape))


def saved_shapes(lanes, heads, blocks):
    size = lanes * 8
    kind = jnp.bfloat16
    return [
        jax.ShapeDtypeStruct((blocks, heads, HD, HD), kind),
        jax.ShapeDtypeStruct((blocks, heads, size, size), kind),
        jax.ShapeDtypeStruct((blocks, heads, size, HD), kind),
        jax.ShapeDtypeStruct((blocks, heads, size, HD), kind),
        jax.ShapeDtypeStruct((blocks, heads, size, HD), kind),
    ]


def mixer_forward(proj, taps, gain, low, off, rem, heads, group=4):
    lanes, tokens, width = proj.shape
    blocks, wide = tokens // 8, heads * HD
    size = lanes * 8
    token, saved, square = mixer_specs(lanes, heads, group, 0)
    return pl.pallas_call(
        functools.partial(delta_forward, lanes, heads, group),
        grid=(blocks // group,),
        in_specs=[token(width), fixed(taps.shape), fixed(gain.shape), square, token(HD), token(HD)],
        out_specs=[
            token(wide), token(wide), token(KINDS * wide),
            saved(HD, HD), saved(size, size), saved(size, HD), saved(size, HD), saved(size, HD),
        ],
        out_shape=[
            jax.ShapeDtypeStruct((lanes, tokens, wide), jnp.bfloat16),
            jax.ShapeDtypeStruct((lanes, tokens, wide), jnp.bfloat16),
            jax.ShapeDtypeStruct((lanes, tokens, KINDS * wide), jnp.float32),
        ] + saved_shapes(lanes, heads, blocks),
        scratch_shapes=[
            pltpu.VMEM((heads, HD, HD), jnp.float32),
            pltpu.VMEM((KINDS * heads, TAPS, 8, HD), jnp.float32),
            pltpu.VMEM((lanes, 8 * group, KINDS * wide), jnp.float32),
        ],
        compiler_params=pltpu.CompilerParams(vmem_limit_bytes=48 * 1024 * 1024),
        cost_estimate=pl.CostEstimate(flops=35 * 10**9, bytes_accessed=40 * 10**6, transcendentals=0),
    )(proj, taps, gain, low, off, rem)


def mixer_backward(
    proj, sums, mixed, dzed, taps, gain, low, off, rem, saves, heads, group=4
):
    lanes, tokens, width = proj.shape
    blocks, wide = tokens // 8, heads * HD
    size = lanes * 8
    token, saved, square = mixer_specs(lanes, heads, group, blocks // group)
    return pl.pallas_call(
        functools.partial(delta_backward, lanes, heads, group),
        grid=(blocks // group,),
        in_specs=[
            token(width), token(KINDS * wide), token(wide), token(wide),
            fixed(taps.shape), fixed(gain.shape), square, token(HD), token(HD),
            saved(HD, HD), saved(size, size), saved(size, HD), saved(size, HD), saved(size, HD),
        ],
        out_specs=[token(width), fixed(taps.shape), fixed(gain.shape)],
        out_shape=[
            jax.ShapeDtypeStruct((lanes, tokens, width), jnp.bfloat16),
            jax.ShapeDtypeStruct(taps.shape, jnp.float32),
            jax.ShapeDtypeStruct(gain.shape, jnp.float32),
        ],
        scratch_shapes=[
            pltpu.VMEM((heads, HD, HD), jnp.float32),
            pltpu.VMEM((KINDS * heads, TAPS, 8, HD), jnp.float32),
            pltpu.VMEM((TAPS, 8, HD), jnp.float32),
            pltpu.VMEM((lanes, 8 * group, KINDS * wide), jnp.float32),
            pltpu.VMEM((taps.shape[0], 8, wide), jnp.float32),
            pltpu.VMEM((size, HD), jnp.float32),
        ],
        compiler_params=pltpu.CompilerParams(vmem_limit_bytes=48 * 1024 * 1024),
        cost_estimate=pl.CostEstimate(flops=35 * 10**9, bytes_accessed=40 * 10**6, transcendentals=0),
    )(proj, sums, mixed, dzed, taps, gain, low, off, rem, *saves)


def segment_masks(lengths_grid, order_row, lanes, tokens):
    slots = order_row.shape[0]
    flat = lengths_grid.reshape(slots)
    first = lax.broadcasted_iota(jnp.int32, (slots, slots), 0)
    second = lax.broadcasted_iota(jnp.int32, (slots, slots), 1)
    run_len = jnp.sum(jnp.where(order_row[:, None] == second, flat[None, :], 0), axis=1)
    ends = jnp.sum(jnp.where(first >= second, run_len[None, :], 0), axis=1)
    starts = ends - run_len
    size = lanes * 8
    blocks = tokens // 8
    lane = lax.broadcasted_iota(jnp.int32, (lanes, tokens), 0)
    step = lax.broadcasted_iota(jnp.int32, (lanes, tokens), 1)
    place = step * lanes + lane
    inside = (starts[:, None, None] <= place[None]) & (place[None] < ends[:, None, None])
    start_at = jnp.sum(jnp.where(inside, starts[:, None, None], 0), axis=0)
    end_at = jnp.sum(jnp.where(inside, ends[:, None, None], 0), axis=0)

    def blocked(values):
        return values.reshape(lanes, blocks, 8).transpose(1, 0, 2).reshape(blocks, size)

    start_b, place_b = blocked(start_at), blocked(place)
    low = (start_b[:, :, None] == start_b[:, None, :]) & (place_b[:, :, None] >= place_b[:, None, :])

    def spread(values):
        return jnp.broadcast_to(values.astype(jnp.float32)[:, :, None], (lanes, tokens, HD))

    return low.astype(jnp.bfloat16), spread(place - start_at), spread(end_at - place)


def exchange_beside(tasks, axes, ident, compute, grid, pace, operands, results, scratch, flops):
    inputs, outputs, own_scratch, spans = layout_of(tasks)
    counts = (len(inputs), len(operands), len(outputs), len(results), len(own_scratch), len(scratch))

    def kernel(*refs):
        groups, at = [], 0
        for count in counts:
            groups.append(refs[at : at + count])
            at += count
        task_ins, ins, task_outs, outs, task_scratch, rest = groups
        steps = task_steps(tasks, spans, axes, task_ins, task_outs, task_scratch)
        due = [min(max(int(when // pace), 0), grid) for when, _ in steps]
        for i in range(grid):
            if i in due:

                @pl.when(pl.program_id(0) == i)
                def _(i=i):
                    for turn, (_, step) in zip(due, steps):
                        if turn == i:
                            step()

        compute(*ins, *outs, *rest)

        @pl.when(pl.program_id(0) == grid - 1)
        def _():
            for turn, (_, step) in zip(due, steps):
                if turn == grid:
                    step()

    return pl.pallas_call(
        kernel,
        grid=(grid,),
        in_specs=[ANY] * len(inputs) + [spec for _, spec in operands],
        out_specs=[spec for spec, _ in outputs] + [spec for spec, _ in results],
        out_shape=[shape for _, shape in outputs] + [shape for _, shape in results],
        scratch_shapes=own_scratch + list(scratch),
        compiler_params=pltpu.CompilerParams(
            collective_id=ident, has_side_effects=True, vmem_limit_bytes=60 * 1024 * 1024
        ),
        cost_estimate=pl.CostEstimate(flops=flops, bytes_accessed=60 * 10**6, transcendentals=0),
    )(*inputs, *[array for array, _ in operands])


def exchange_computed(task, tasks, axes, ident, fill, compute, grid, pace, operands, results, flops):
    slots = lax.axis_size(task.axis)
    everything = [task] + tasks
    inputs, outputs, own_scratch, spans = layout_of(everything)
    counts = (len(inputs), len(operands), len(outputs), len(results), len(own_scratch))

    def kernel(*refs):
        groups, at = [], 0
        for count in counts:
            groups.append(refs[at : at + count])
            at += count
        task_ins, ins, task_outs, outs, task_scratch = groups
        steps = task_steps(everything, spans, axes, task_ins, task_outs, task_scratch)
        due = [min(max(int(when // pace), 0), grid + slots) for when, _ in steps]
        now = pl.program_id(0)
        for i in range(slots + grid):

            @pl.when(now == i)
            def _(i=i):
                for turn, (_, step) in zip(due, steps):
                    if turn == i:
                        step()
                if i < slots:
                    fill(task.slot(i), task.terms, *ins, *outs)
                    task.launch(i)
                else:
                    compute(*ins, *outs)

        @pl.when(now == slots + grid - 1)
        def _():
            for turn, (_, step) in zip(due, steps):
                if turn == slots + grid:
                    step()

    return pl.pallas_call(
        kernel,
        grid=(slots + grid,),
        in_specs=[ANY] * len(inputs) + [spec for _, spec in operands],
        out_specs=[spec for spec, _ in outputs] + [spec for spec, _ in results],
        out_shape=[shape for _, shape in outputs] + [shape for _, shape in results],
        scratch_shapes=own_scratch,
        compiler_params=pltpu.CompilerParams(
            collective_id=ident, has_side_effects=True, vmem_limit_bytes=60 * 1024 * 1024
        ),
        cost_estimate=pl.CostEstimate(flops=flops, bytes_accessed=60 * 10**6, transcendentals=0),
    )(*inputs, *[array for array, _ in operands])


def fill_input_terms(slot, terms, proj_ref, weights_ref):
    chunks, rows, width = terms.shape[1:]
    own = proj_ref[pl.ds(pl.multiple_of(slot * chunks * rows, chunks * rows), chunks * rows)]
    wide = 512
    for n in range(0, width, wide):
        part = dot_nt(own, weights_ref[n : n + wide])
        terms[slot, :, :, n : n + wide] = part.reshape(chunks, rows, wide).astype(terms.dtype)


def feed_forward(
    rows, window, zed_ref, source_ref, wo_ref, wi_ref, wd_ref, gain_ref,
    hidden_ref, in_ref, product_ref, slopes_ref, out_ref, held,
):
    width = source_ref.shape[1]
    wide = 512
    squares = jnp.zeros((rows, 1), jnp.float32)
    for n in range(0, width, wide):
        cols = slice(n, n + wide)
        part = source_ref[:, cols].astype(jnp.float32) + dot_nn(zed_ref[...], wo_ref[:, cols])
        held[:, cols] = part
        squares = squares + jnp.sum(part * part, axis=1, keepdims=True)
    scale = lax.rsqrt(squares / width + 1e-6)
    for n in range(0, width, wide):
        cols = slice(n, n + wide)
        in_ref[:, cols] = (held[:, cols] * scale * gain_ref[:, cols]).astype(in_ref.dtype)

    @pl.when(pl.program_id(0) == lax.axis_index("shard"))
    def _():
        hidden_ref[...] = held[...]

    wide = 256
    for n in range(0, window, wide):
        cols = slice(n, n + wide)
        ups = slice(window + n, window + n + wide)
        gate = dot_nn(in_ref[...], wi_ref[:, cols])
        up = dot_nn(in_ref[...], wi_ref[:, ups])
        s = sigmoid(gate)
        silu = gate * s
        product_ref[:, cols] = (silu * up).astype(product_ref.dtype)
        slopes_ref[:, cols] = (up * s * (1.0 + gate * (1.0 - s))).astype(slopes_ref.dtype)
        slopes_ref[:, ups] = silu.astype(slopes_ref.dtype)
    wide = 512
    for n in range(0, width, wide):
        cols = slice(n, n + wide)
        out_ref[:, cols] = dot_nn(product_ref[...], wd_ref[:, cols]).astype(out_ref.dtype)


def feed_backward(window, dy_ref, slopes_ref, wi_ref, wd_ref, dlin_ref, dterm_ref):
    width = dy_ref.shape[1]
    wide = 256
    for n in range(0, window, wide):
        cols = slice(n, n + wide)
        ups = slice(window + n, window + n + wide)
        d_product = dot_nt(dy_ref[...], wd_ref[cols])
        for part in (cols, ups):
            slope = slopes_ref[:, part].astype(jnp.float32)
            dlin_ref[:, part] = (d_product * slope).astype(dlin_ref.dtype)
    wide = 512
    for n in range(0, width, wide):
        cols = slice(n, n + wide)
        dterm_ref[:, cols] = dot_nt(dlin_ref[...], wi_ref[cols]).astype(dterm_ref.dtype)


def whole(array):
    return pl.BlockSpec(array.shape, lambda i: (0, 0), pipeline_mode=pl.Buffered(1))


def run_feed_forward(tasks, axes, ident, zed, source, w_output, w_in, w_down, gain, rows):
    tokens, width = source.shape
    window = w_down.shape[0]

    def token(columns):
        return pl.BlockSpec((rows, columns), lambda i: (i, 0))

    results = [(fixed((rows, width)), jax.ShapeDtypeStruct((rows, width), jnp.float32))]
    for columns in (width, window, 2 * window, width):
        results.append((token(columns), jax.ShapeDtypeStruct((tokens, columns), zed.dtype)))
    return exchange_beside(
        tasks,
        axes,
        ident,
        functools.partial(feed_forward, rows, window),
        tokens // rows,
        6.0,
        [(zed, token(width)), (source, token(width))]
        + [(a, whole(a)) for a in (w_output, w_in, w_down, gain)],
        results,
        [pltpu.VMEM((rows, width), jnp.float32)],
        90 * 10**9,
    )


def run_feed_backward(dy, slopes, w_in, w_down, rows):
    tokens, width = dy.shape
    window = w_down.shape[0]

    def token(columns):
        return pl.BlockSpec((rows, columns), lambda i: (i, 0))

    columns = (2 * window, width)
    return pl.pallas_call(
        functools.partial(feed_backward, window),
        grid=(tokens // rows,),
        in_specs=[token(width), token(2 * window), whole(w_in), whole(w_down)],
        out_specs=[token(c) for c in columns],
        out_shape=[jax.ShapeDtypeStruct((tokens, c), dy.dtype) for c in columns],
        compiler_params=pltpu.CompilerParams(vmem_limit_bytes=60 * 1024 * 1024),
        cost_estimate=pl.CostEstimate(flops=30 * 10**9, bytes_accessed=40 * 10**6, transcendentals=0),
    )(dy, slopes, w_in, w_down)


def feed_gradients(in_ref, dlin_ref, product_ref, dy_ref, glin_ref, gdown_ref):
    glin_ref[...] = dot_tn(in_ref[...], dlin_ref[...]).astype(glin_ref.dtype)
    gdown_ref[...] = dot_tn(product_ref[...], dy_ref[...]).astype(gdown_ref.dtype)


def run_feed_gradients(tasks, axes, ident, mlp_in, d_lin, product, dy):
    tokens, width = mlp_in.shape
    window = product.shape[1]
    wide = 256
    if tokens > 2048:
        kind = mlp_in.dtype
        return (
            *exchange(tasks, axes, ident),
            contract_rows(mlp_in, d_lin).astype(kind),
            contract_rows(product, dy).astype(kind),
        )

    def columns(rows):
        return pl.BlockSpec((rows, wide), lambda i: (0, i))

    return exchange_beside(
        tasks,
        axes,
        ident,
        feed_gradients,
        width // wide,
        4.0,
        [
            (mlp_in, columns(tokens)),
            (d_lin, whole(d_lin)),
            (product, whole(product)),
            (dy, columns(tokens)),
        ],
        [
            (
                pl.BlockSpec((wide, 2 * window), lambda i: (i, 0)),
                jax.ShapeDtypeStruct((width, 2 * window), mlp_in.dtype),
            ),
            (columns(window), jax.ShapeDtypeStruct((window, width), mlp_in.dtype)),
        ],
        [],
        90 * 10**9,
    )


def project(left_side, right_side):
    return jnp.dot(left_side, right_side, preferred_element_type=jnp.float32)


def times_t(left_side, right_side):
    return lax.dot_general(
        left_side, right_side, (((1,), (1,)), ((), ())), preferred_element_type=jnp.float32
    )


def contract_rows(left_side, right_side):
    return lax.dot_general(
        left_side, right_side, (((0,), (0,)), ((), ())), preferred_element_type=jnp.float32
    )


def rms(values, gain, eps):
    return values * lax.rsqrt(jnp.mean(values * values, axis=-1, keepdims=True) + eps) * gain


def rms_back(values, gain, eps, grad):
    r = lax.rsqrt(jnp.mean(values * values, axis=-1, keepdims=True) + eps)
    inner = jnp.mean(values * gain * grad, axis=-1, keepdims=True)
    return r * gain * grad - values * (r * r * r) * inner, grad * values * r


def deal(stacked):
    return lax.all_to_all(stacked, "shard", split_axis=0, concat_axis=0, tiled=True)


def cross(blocks):
    shards = lax.axis_size("shard")
    return lax.ppermute(blocks, "shard", [(s, s ^ 1) for s in range(shards)])


def column_windows(columns, shards):
    own = columns // shards
    tiles = columns // HD
    width = 1
    while any(min(s * own // HD, tiles - width) * HD + width * HD < (s + 1) * own for s in range(shards)):
        width += 1

    def first(s):
        if isinstance(s, int):
            return min(s * own // HD, tiles - width) * HD
        return jnp.minimum(lax.div(s * own, HD), tiles - width) * HD

    return first, width * HD


def place_windows(kinds, shards, columns, window, first, own, in_ref, *out_refs):
    for kind, out_ref in zip(range(kinds), out_refs):
        for tile in range(columns // HD):
            total = None
            for s in range(shards):
                low = max(tile * HD, s * own)
                high = min((tile + 1) * HD, (s + 1) * own)
                if low < high:
                    at = kind * window + tile * HD - first(s)
                    term = in_ref[0, s, :, at : at + HD].astype(jnp.float32)
                    total = term if total is None else total + term
            out_ref[:, tile * HD : (tile + 1) * HD] = total


def widen(collected, kinds, columns, window, first):
    replicas, shards, part, wide = collected.shape
    return pl.pallas_call(
        functools.partial(place_windows, kinds, shards, columns, window, first, columns // shards),
        grid=(replicas,),
        in_specs=[pl.BlockSpec((1, shards, part, wide), lambda i: (i, 0, 0, 0))],
        out_specs=[pl.BlockSpec((part, columns), lambda i: (i, 0))] * kinds,
        out_shape=[jax.ShapeDtypeStruct((replicas * part, columns), jnp.float32)] * kinds,
        compiler_params=pltpu.CompilerParams(vmem_limit_bytes=48 * 1024 * 1024),
    )(collected)


def body(
    layer_input,
    out_cotangent,
    seq_lengths,
    seq_order,
    w_query,
    w_key,
    w_value,
    w_beta,
    w_outgate,
    w_output,
    conv_query,
    conv_key,
    conv_value,
    attn_gain,
    head_gain,
    mlp_gain,
    w_gate,
    w_up,
    w_down,
):
    bf16, f32 = jnp.bfloat16, jnp.float32
    shards = lax.axis_size("shard")
    shard = lax.axis_index("shard")
    both, group = ("shard", "replica"), ("shard",)
    rows, width = layer_input.shape
    tokens = shards * rows
    weight_rows = w_query.shape[0]
    own = w_output.shape[0]
    heads = own // HD
    hidden_own = w_down.shape[0]
    ffn = w_gate.shape[1]
    ffn_first, ffn_window = column_windows(ffn, shards)
    col_first, col_window = column_windows(width, shards)
    shift = shard * hidden_own - ffn_first(shard)

    total_heads = w_beta.shape[1]
    head_part = jnp.pad(head_gain, (0, weight_rows - head_gain.shape[0]))
    little = jnp.concatenate([w_beta, jnp.stack([attn_gain, mlp_gain, head_part], axis=1)], axis=1)
    little = jnp.pad(little, ((0, 0), (0, HD - little.shape[1])))
    attn_weights, all_source, little = exchange(
        [
            Spread((w_query, w_key, w_value, w_outgate), col_window, col_first, -0.5, 13.0),
            Gather("shard", layer_input, 8, turned=True),
            Gather("shard", little, 1, 0.0, 20.0),
        ],
        both,
        0,
    )
    full_attn_gain = little[:, :, total_heads].reshape(width).astype(f32)
    full_mlp_gain = little[:, :, total_heads + 1].reshape(width).astype(f32)
    head_row = little[:, : head_gain.shape[0], total_heads + 2].reshape(1, HD).astype(f32)
    beta = lax.dynamic_slice_in_dim(little.reshape(width, HD), shard * heads, heads, axis=1)
    attn_weights = jnp.concatenate(
        [attn_weights.reshape(width, 4 * own), jnp.pad(beta, ((0, 0), (0, HD - heads)))], axis=1
    )
    replicas = lax.axis_size("replica")
    part = weight_rows // replicas
    at = lax.axis_index("replica") * part
    windows = [
        lax.slice_in_dim(w, ffn_first(s), ffn_first(s) + ffn_window, axis=1)
        for s in range(shards)
        for w in (
            lax.dynamic_slice_in_dim(w_gate, at, part),
            lax.dynamic_slice_in_dim(w_up, at, part),
        )
    ]
    mlp_weights = jnp.stack(
        [jnp.concatenate(windows[2 * s : 2 * s + 2], axis=1) for s in range(shards)]
    )
    full_output = jnp.broadcast_to(
        lax.dynamic_slice_in_dim(w_output, at, part)[None], (shards, part, width)
    )
    later_weights = jnp.concatenate([mlp_weights, full_output], axis=2)
    later_weights, all_source = lax.optimization_barrier((later_weights, all_source))
    later_weights = deal(later_weights)
    low, off, rem = segment_masks(seq_lengths[0], seq_order[0], shards, rows)

    source = layer_input.astype(f32)
    all_source = all_source.reshape(tokens, width)
    normed = rms(all_source.astype(f32), full_attn_gain, 1e-6).astype(bf16)
    projected = project(normed, attn_weights).reshape(shards, rows, -1)
    taps = jnp.concatenate([conv_query, conv_key, conv_value], axis=0).astype(f32)
    zed, mixed, sums, *saves = mixer_forward(projected, taps, head_row, low, off, rem, heads)
    all_zed, mlp_weights, full_output = exchange(
        [
            Gather("shard", zed.reshape(tokens, own), 8, 0.0, 21.0, True, True),
            Trade(later_weights, 0, 2 * ffn_window, 0.2, 76.0),
            Trade(later_weights, 2 * ffn_window, width, 0.1, 76.0),
        ],
        both,
        2,
    )
    zed = zed.reshape(tokens, own)
    mlp_weights = mlp_weights.reshape(width, 2 * ffn_window)
    w_down = lax.dynamic_update_slice(jnp.zeros((ffn_window, width), bf16), w_down, (shift, 0))
    dy, hidden, mlp_in, product, slopes, out_terms = run_feed_forward(
        [Gather("shard", out_cotangent, 8, turned=True)],
        group,
        3,
        all_zed,
        all_source,
        full_output.reshape(width, width),
        mlp_weights,
        w_down,
        full_mlp_gain[None, :],
        rows,
    )
    dy = dy.reshape(tokens, width)
    d_lin, d_terms = run_feed_backward(dy, slopes, mlp_weights, w_down, rows)
    d_mlp_in, g_lin, g_down = run_feed_gradients(
        [Scatter("shard", d_terms, 4)], group, 4, mlp_in, d_lin, product, dy
    )
    d_hidden_norm, g_mlp_rows = rms_back(hidden, full_mlp_gain, 1e-6, d_mlp_in)
    d_hidden = out_cotangent.astype(f32) + d_hidden_norm

    d_attn, g_lin, g_down = exchange(
        [
            Gather("shard", d_hidden.astype(bf16), 8, turned=True),
            Sum(g_lin, 0.5, 26.0),
            Total(g_down, 0.1, 10.0, 62.0),
        ],
        both,
        5,
    )
    g_lin, d_attn = lax.optimization_barrier((g_lin, d_attn))
    g_lin = deal(g_lin)
    d_attn = d_attn.reshape(tokens, width)
    g_output = contract_rows(zed, d_attn).astype(bf16)
    d_zed = times_t(d_attn, w_output).reshape(shards, rows, own)
    d_proj, g_taps, g_head = mixer_backward(
        projected, sums, mixed, d_zed, taps, head_row, low, off, rem, saves, heads
    )
    d_proj = d_proj.reshape(tokens, -1)
    g_proj = contract_rows(normed, d_proj).astype(bf16)
    beside = [
        Sum(g_proj, 0.1, 10.0, 20.0),
        Total(g_output, 0.05, 6.0, 70.0, 12.0),
        Gather("replica", g_lin.reshape(-1, 2 * ffn_window), 4, 20.0, 46.0),
    ]
    if grid_of("shard")[1] == 2:
        d_normed, g_proj, g_output, g_lin = exchange_computed(
            Computed("shard", rows, width, bf16, 4, 12.0),
            beside,
            both,
            6,
            fill_input_terms,
            None,
            0,
            2.0,
            [(d_proj, whole(d_proj)), (attn_weights, whole(attn_weights))],
            [],
            90 * 10**9,
        )
    else:
        d_terms = times_t(d_proj, attn_weights).astype(bf16)
        d_normed, g_proj, g_output, g_lin = exchange(
            [Scatter("shard", d_terms, 4)] + beside, both, 6
        )
    d_source, g_attn_rows = rms_back(source, full_attn_gain, 1e-6, d_normed)

    def dealt(values):
        return values.reshape(shards, -1)

    small = jnp.concatenate(
        [dealt(jnp.sum(g_attn_rows, axis=0)), dealt(jnp.sum(g_mlp_rows, axis=0)), dealt(g_head)], axis=1
    )
    small = jnp.pad(small, ((0, 0), (0, -small.shape[1] % HD)))
    small = jnp.broadcast_to(small[:, None, :], (shards, 8, small.shape[1]))
    out_terms, g_proj, small, g_taps = exchange(
        [
            Scatter("shard", out_terms, 4),
            Deliver(g_proj, -0.4, 60.0, 24.0),
            Small(small, jnp.pad(g_taps, ((0, 16 - g_taps.shape[0]), (0, 0))), 50.0),
        ],
        both,
        7,
    )
    g_lin = g_lin.reshape(replicas, shards, -1, 2 * ffn_window)
    g_query, g_key, g_value, g_outgate = widen(g_proj, 4, width, col_window, col_first)
    g_gate, g_up = widen(g_lin, 2, ffn, ffn_window, ffn_first)
    g_beta = g_proj[..., 4 * own : 4 * own + heads].transpose(0, 2, 1, 3)
    g_down = lax.dynamic_slice_in_dim(g_down.reshape(-1, width), shift, hidden_own)
    gains = width // shards
    return (
        (hidden + out_terms).astype(bf16),
        (d_hidden + d_source).astype(bf16),
        g_query,
        g_key,
        g_value,
        g_beta.reshape(weight_rows, total_heads).astype(f32),
        g_outgate,
        g_output.reshape(own, width).astype(f32),
        g_taps[:TAPS],
        g_taps[TAPS : 2 * TAPS],
        g_taps[2 * TAPS : 3 * TAPS],
        small[0, :gains],
        small[0, 2 * gains : 2 * gains + head_gain.shape[0]],
        small[0, gains : 2 * gains],
        g_gate,
        g_up,
        g_down.astype(f32),
    )


def solution(mesh):
    tokens = P(("replica", "shard"), None)
    whole, columns, vector = P("shard", None), P(None, "shard"), P("shard")
    in_specs = (tokens, tokens, P("replica", None, None), P("replica", None)) + (whole,) * 6
    in_specs += (columns,) * 3 + (vector,) * 3 + (whole,) * 3
    out_specs = (tokens, tokens) + (whole,) * 6 + (columns,) * 3 + (vector,) * 3 + (whole,) * 3
    return jax.shard_map(body, mesh=mesh, in_specs=in_specs, out_specs=out_specs, check_vma=False)
```

```python
import functools

import jax
import jax.numpy as jnp
from jax import lax
from jax.experimental import pallas as pl
from jax.experimental.pallas import tpu as pltpu
from jax.sharding import PartitionSpec as P

MESH = pl.DeviceIdType.MESH
ANY = pl.BlockSpec(memory_space=pl.ANY)
VMEM = pl.BlockSpec(memory_space=pltpu.VMEM)
DMA = pltpu.SemaphoreType.DMA
UP, DOWN, RIGHT, LEFT = range(4)


def grid_of(axis):
    count = lax.axis_size(axis)
    if axis == "replica":
        across = 2 if count % 2 == 0 else 1
        return count // across, across
    depth = 4 if count % 4 == 0 else count
    return depth, count // depth


class Lines:
    def __init__(self, axis):
        self.axis = axis
        self.Z, self.X = grid_of(axis)
        self.count = self.Z * self.X
        self.me = lax.axis_index(axis)
        self.z, self.x = lax.div(self.me, self.X), lax.rem(self.me, self.X)
        z, x, X = self.z, self.x, self.X
        self.targets = ((z + 1) * X + x, (z - 1) * X + x, z * X + x + 1, z * X + x - 1)
        self.exists = (z < self.Z - 1, z > 0, x < X - 1, x > 0)

    def to(self, way):
        return {self.axis: self.targets[way]}

    def other(self, k):
        return lax.rem(self.me + k, self.count)

    def slot(self, zz, xx):
        return zz * self.X + xx


class Turned(Lines):
    def __init__(self, line):
        self.axis, self.count, self.me = line.axis, line.count, line.me
        self.Z, self.X, self.z, self.x = line.X, line.Z, line.x, line.z
        self.targets = line.targets[2:] + line.targets[:2]
        self.exists = line.exists[2:] + line.exists[:2]

    def slot(self, zz, xx):
        return xx * self.Z + zz


class Column(Lines):
    def __init__(self, line):
        self.axis, self.count, self.me = line.axis, line.Z, line.z
        self.Z, self.X, self.z, self.x = line.Z, 1, line.z, jnp.int32(0)
        self.targets = line.targets
        self.exists = line.exists[:2] + (jnp.bool_(False),) * 2

    def slot(self, zz, xx):
        return zz


def greet(lines, everyone):
    barrier = pltpu.get_barrier_semaphore()
    count = jnp.int32(0)
    for line in lines:
        if line.axis in everyone:
            for k in range(1, line.count):
                pl.semaphore_signal(
                    barrier, inc=1, device_id={line.axis: line.other(k)}, device_id_type=MESH
                )
            count = count + (line.count - 1)
            continue
        for way in range(4):

            @pl.when(line.exists[way])
            def _(line=line, way=way):
                pl.semaphore_signal(barrier, inc=1, device_id=line.to(way), device_id_type=MESH)

            count = count + jnp.where(line.exists[way], 1, 0)
    pl.semaphore_wait(barrier, count)


def remote(src, dst, send_sem, recv_sem, device):
    return pltpu.make_async_remote_copy(
        src_ref=src,
        dst_ref=dst,
        send_sem=send_sem,
        recv_sem=recv_sem,
        device_id=device,
        device_id_type=MESH,
    )


def in_place(view, sem):
    return pltpu.make_async_copy(view, view, sem)


def staged(src, dst, held, sems):
    load = pltpu.make_async_copy(src, held, sems.at[0])
    save = pltpu.make_async_copy(held, dst, sems.at[1])

    def turn():
        load.wait()
        save.start()

    return load.start, turn, save.wait


def gather_sems(axis, chunks):
    Z, X = grid_of(axis)
    return [DMA((4, Z * X, chunks)), DMA((Z * X, chunks))]


def gather_steps(line, chunks, view, source, ready, sems, start, pace):
    send_sem, recv_sem = sems
    Z, X, z, x, me = line.Z, line.X, line.z, line.x, line.me
    exists = line.exists

    def copy(way, origin, c, src=None):
        spot = view(origin, c)
        return remote(
            spot if src is None else src,
            spot,
            send_sem.at[way, origin, c],
            recv_sem.at[origin, c],
            line.to(way),
        )

    def first(c):
        ready(c)
        for way in range(4):

            @pl.when(exists[way])
            def _(way=way):
                copy(way, me, c, source(c)).start()

    def hop(d, c):
        for way, here in ((UP, z - d >= 0), (DOWN, z + d < Z)):

            @pl.when(here)
            def _(way=way):
                origin = line.slot(z - d if way == UP else z + d, x)
                copy(way, origin, c).wait_recv()
                for onward in (way, RIGHT, LEFT):

                    @pl.when(exists[onward])
                    def _(onward=onward):
                        copy(onward, origin, c).start()

    def across(e, level, c):
        for way, here in ((RIGHT, x - e >= 0), (LEFT, x + e < X)):

            @pl.when(here)
            def _(way=way):
                origin = line.slot(level, x - e if way == RIGHT else x + e)
                copy(way, origin, c).wait_recv()
                if X > 2:

                    @pl.when(exists[way])
                    def _():
                        copy(way, origin, c).start()

    def finish():
        for c in range(chunks):
            for zz in range(Z):
                for way, here in ((UP, zz <= z), (DOWN, zz >= z)):

                    @pl.when(exists[way] & here)
                    def _(way=way, zz=zz, c=c):
                        copy(way, line.slot(zz, x), c).wait_send()

                for xx in range(X):
                    for way, here in ((RIGHT, xx <= x), (LEFT, xx >= x)):

                        @pl.when(exists[way] & here)
                        def _(way=way, zz=zz, xx=xx, c=c):
                            copy(way, line.slot(zz, xx), c).wait_send()

    steps = []
    for c in range(chunks):
        steps.append((start + pace * c / chunks, functools.partial(first, c)))
    for d in range(1, Z):
        for c in range(chunks):
            steps.append((start + pace * (d - 1 + (c + 1) / chunks), functools.partial(hop, d, c)))
    for e in range(1, X):
        for dz in range(Z):
            level = lax.rem(z + dz, Z)
            for c in range(chunks):
                when = start + pace * (Z + e + (dz * chunks + c) / (Z * chunks))
                steps.append((when, functools.partial(across, e, level, c)))
    steps.append((start + pace * (Z + X + 1), finish))
    return steps


def scatter_slots(dims):
    Z, X = dims
    if X == 1:
        return Z, 1
    if X == 2:
        return Z, Z
    return Z * X, Z * (X + 1)


def scatter_scratch(dims, chunks, rows, width, kind):
    Z, X = dims
    held, across = scatter_slots(dims)
    return [
        pltpu.VMEM((held, chunks, rows, width), kind),
        pltpu.VMEM((across, chunks, rows, width), kind),
        pltpu.VMEM((Z + 1, chunks, rows, width), kind),
        DMA((held,)),
        DMA((Z * X, chunks)),
        DMA((across, chunks)),
        DMA((Z, chunks)),
        DMA((Z + 1, chunks)),
    ]


STEP = 16


def stride(rows):
    return max(n for n in (16, 32, 64) if rows % n == 0 and n <= BIG)


BIG = 64


def far_first(count, at):
    order = []
    for k in range(count - 1):
        order += [place for place, here in ((count - 1 - k, count - 1 - k > at), (k, k < at)) if here]
    return order + [at]


def scatter_steps(
    line, chunks, block, piece, scratch, store, done, start, pace, launches=None, lag=0.0
):
    mine, from_x, from_z, load_sem, xs_sem, xr_sem, zs_sem, zr_sem = scratch
    Z, X, z, x = line.Z, line.X, line.z, line.x
    exists = line.exists
    rows = mine.shape[2]
    step = stride(rows)

    def spot(zz, xx):
        return zz if X <= 2 else zz * X + xx

    def load(zz, xx):
        at = spot(zz, xx)
        return pltpu.make_async_copy(block(line.slot(zz, xx)), mine.at[at], load_sem.at[at])

    def x_landing(zz, xx, right, receiver):
        if X <= 2:
            return zz
        return zz * (X + 1) + (xx if right else jnp.where(xx == receiver, X, xx))

    def x_copy(right, zz, xx, c):
        landing = x_landing(zz, xx, right, x + 1 if right else x - 1)
        src = piece(line.slot(zz, xx), c) if X <= 2 else mine.at[spot(zz, xx), c]
        return remote(
            src,
            from_x.at[landing, c],
            xs_sem.at[zz * X + xx, c],
            xr_sem.at[landing, c],
            line.to(RIGHT if right else LEFT),
        )

    def z_copy(up, zz, c):
        landing = zz if up else jnp.where(zz == z - 1, Z, zz)
        return remote(
            mine.at[spot(zz, x), c],
            from_z.at[landing, c],
            zs_sem.at[zz, c],
            zr_sem.at[landing, c],
            line.to(UP if up else DOWN),
        )

    def wait_in(buffer, sem, at, c):
        in_place(buffer.at[at, c], sem.at[at, c]).wait()

    def add_in(at, buffer, landing, c):
        def body(i, carry):
            part = pl.ds(pl.multiple_of(i * step, step), step)
            mine[at, c, part] = (
                mine[at, c, part].astype(jnp.float32) + buffer[landing, c, part].astype(jnp.float32)
            ).astype(mine.dtype)
            return carry

        lax.fori_loop(0, rows // step, body, 0)

    def x_line(zz):
        for k in range(X - 1):
            for right, xx, here in ((True, X - 1 - k, X - 1 - k > x), (False, k, k < x)):

                @pl.when(here)
                def _(right=right, xx=xx):
                    if X > 2:
                        load(zz, xx).wait()
                    for c in range(chunks):
                        if X > 2:

                            @pl.when(exists[LEFT if right else RIGHT])
                            def _(c=c):
                                landing = x_landing(zz, xx, right, jnp.int32(-1))
                                wait_in(from_x, xr_sem, landing, c)
                                add_in(spot(zz, xx), from_x, landing, c)

                        x_copy(right, zz, xx, c).start()

    def x_join(zz, c):
        at = spot(zz, x)
        if X == 2:
            wait_in(from_x, xr_sem, zz, c)
            add_in(at, from_x, zz, c)
        elif X > 2:
            for right in (True, False):

                @pl.when(exists[LEFT if right else RIGHT])
                def _(right=right):
                    landing = zz * (X + 1) + (x if right else X)
                    wait_in(from_x, xr_sem, landing, c)
                    add_in(at, from_x, landing, c)

    def ways(k):
        return ((True, Z - 1 - k, Z - 1 - k > z), (False, k, k < z))

    def begin():
        for zz in range(Z):
            for xx in range(X):
                if X > 2:
                    load(zz, xx).start()
            if X <= 2:
                load(zz, x).start()
        for k in range(Z - 1):
            for up, zz, here in ways(k):

                @pl.when(here)
                def _(zz=zz):
                    x_line(zz)

        x_line(z)

    def pass_on(k, c):
        for up, zz, here in ways(k):

            @pl.when(here)
            def _(up=up, zz=zz):
                if c == 0:
                    load(zz, x).wait()
                x_join(zz, c)

                @pl.when(exists[DOWN if up else UP])
                def _():
                    wait_in(from_z, zr_sem, zz, c)
                    add_in(spot(zz, x), from_z, zz, c)

                z_copy(up, zz, c).start()

    def settle(c):
        if c == 0:
            load(z, x).wait()
        x_join(z, c)

        @pl.when(exists[DOWN])
        def _():
            wait_in(from_z, zr_sem, z, c)

        @pl.when(exists[UP])
        def _():
            wait_in(from_z, zr_sem, Z, c)

        def body(i, carry):
            part = pl.ds(pl.multiple_of(i * step, step), step)
            total = mine[spot(z, x), c, part].astype(jnp.float32)
            below = from_z[z, c, part].astype(jnp.float32)
            above = from_z[Z, c, part].astype(jnp.float32)
            total = total + jnp.where(z > 0, below, 0.0)
            total = total + jnp.where(z < Z - 1, above, 0.0)
            store(c, part, total)
            return carry

        lax.fori_loop(0, rows // step, body, 0)
        done(c)

    def finish():
        for zz in range(Z):
            for c in range(chunks):
                for xx in range(X):

                    @pl.when(xx != x)
                    def _(zz=zz, xx=xx, c=c):
                        x_copy(True, zz, xx, c).wait_send()

                @pl.when(zz != z)
                def _(zz=zz, c=c):
                    z_copy(True, zz, c).wait_send()

    tables = []
    for at in range(Z):
        tables.append(far_first(Z, at))

    def visited(i):
        return sum(jnp.where(z == at, tables[at][i], 0) for at in range(Z))

    def launch(i):
        if i < Z:
            x_line(visited(i))
        else:
            load(visited(i - Z), x).start()

    if launches is not None:
        launches.append((visited, launch))
    steps = [] if launches is not None else [(start, begin)]
    for k in range(Z - 1):
        for c in range(chunks):
            steps.append(
                (start + pace * (k + (c + 1) / chunks), functools.partial(pass_on, k, c))
            )
    for c in range(chunks):
        when = start + lag + pace * (Z - 1 + (c + 1) / chunks)
        steps.append((when, functools.partial(settle, c)))
    steps.append((start + lag + pace * (Z + 2), finish))
    return steps


class Gather:
    def __init__(self, axis, block, chunks, start=0.0, pace=21.0, beside=False, turned=False):
        self.axis, self.chunks, self.start, self.pace = axis, chunks, start, pace
        self.beside, self.turned = beside, turned
        self.inputs = [block]
        self.everyone = ()
        count = lax.axis_size(axis)
        rows, width = block.shape
        shape = (rows, count * width) if beside else (count, rows, width)
        self.outputs = [(ANY, jax.ShapeDtypeStruct(shape, block.dtype))]
        self.scratch = [pltpu.VMEM(block.shape, block.dtype), DMA((2,))]
        self.scratch += gather_sems(axis, chunks - turned)
        if turned:
            self.scratch += gather_sems(axis, 1)

    def steps(self, lines, ins, outs, scratch):
        line, (x_ref,), (out_ref,) = lines[self.axis], ins, outs
        held, own_sems, *sems = scratch
        rows, width = x_ref.shape[0] // self.chunks, x_ref.shape[1]

        def view(origin, part):
            if self.beside:
                return out_ref.at[part, pl.ds(pl.multiple_of(origin * width, HD), width)]
            return out_ref.at[origin, part]

        begin, turn, end = staged(x_ref, view(line.me, pl.ds(0, x_ref.shape[0])), held, own_sems)

        def part_steps(line, first, count, sems, start):
            def part(c):
                return pl.ds((first + c) * rows, rows)

            return gather_steps(
                line,
                count,
                lambda origin, c: view(origin, part(c)),
                lambda c: x_ref.at[part(c)],
                lambda c: None,
                sems,
                start,
                self.pace,
            )

        straight = self.chunks - self.turned
        steps = part_steps(line, 0, straight, sems[:2], self.start)
        if self.turned:
            steps += part_steps(Turned(line), straight, 1, sems[2:], self.start + 0.9 * self.pace)
        return [(self.start, begin), (self.start + 0.95 * self.pace, turn)] + steps + [(steps[-1][0], end)]


class Scatter:
    def __init__(self, axis, terms, chunks, start=0.0, pace=21.0, turned=False, column=False):
        self.axis, self.chunks, self.start, self.pace = axis, chunks, start, pace
        self.turned, self.column = turned, column
        dims = grid_of(axis)
        if column:
            dims = (dims[0], 1)
        count = dims[0] * dims[1]
        rows, width = terms.shape[0] // count // chunks, terms.shape[1]
        self.inputs = [terms.reshape(count, chunks, rows, width)]
        self.everyone = ()
        self.outputs = [(VMEM, jax.ShapeDtypeStruct((chunks * rows, width), jnp.float32))]
        self.scratch = scatter_scratch(dims, chunks - turned, rows, width, terms.dtype)
        self.half = len(self.scratch)
        if turned:
            self.scratch += scatter_scratch(dims[::-1], 1, rows, width, terms.dtype)

    def steps(self, lines, ins, outs, scratch):
        (p_ref,), (out_ref,) = ins, outs
        rows = p_ref.shape[2]

        def part_steps(line, first, count, scratch, start):
            def store(c, part, total):
                at = pl.multiple_of((first + c) * rows + part.start, STEP)
                out_ref[pl.ds(at, part.size)] = total

            return scatter_steps(
                line,
                count,
                lambda slot: p_ref.at[slot, pl.ds(first, count)],
                lambda slot, c: p_ref.at[slot, first + c],
                scratch,
                store,
                lambda c: None,
                start,
                self.pace,
            )

        line, straight = lines[self.axis], self.chunks - self.turned
        if self.column:
            line = Column(line)
        steps = part_steps(line, 0, straight, scratch[: self.half], self.start)
        if self.turned:
            steps += part_steps(Turned(line), straight, 1, scratch[self.half :], self.start + 0.01)
        return steps


class Computed(Scatter):
    def __init__(self, axis, rows, width, kind, chunks, start=0.0, pace=21.0):
        self.axis, self.chunks, self.start, self.pace = axis, chunks, start, pace
        self.everyone, self.inputs = (), []
        dims = grid_of(axis)
        count = dims[0] * dims[1]
        self.outputs = [(VMEM, jax.ShapeDtypeStruct((rows, width), jnp.float32))]
        self.scratch = [pltpu.VMEM((count, chunks, rows // chunks, width), kind)]
        self.scratch += scatter_scratch(dims, chunks, rows // chunks, width, kind)

    def steps(self, lines, ins, outs, scratch):
        terms, *rest = scratch
        (out_ref,) = outs
        line = lines[self.axis]
        rows = terms.shape[2]
        launches = []

        def store(c, part, total):
            out_ref[pl.ds(pl.multiple_of(c * rows + part.start, STEP), part.size)] = total

        steps = scatter_steps(
            line,
            self.chunks,
            lambda slot: terms.at[slot],
            lambda slot, c: terms.at[slot, c],
            rest,
            store,
            lambda c: None,
            self.start,
            self.pace,
            launches,
        )
        visited, self.launch = launches[0]

        def slot(i):
            other = i < line.Z
            return line.slot(visited(i % line.Z), 1 - line.x if other else line.x)

        self.slot, self.terms = slot, terms
        return steps


class Spread:
    def __init__(self, weights, window, first, start=0.0, pace=6.0):
        self.inputs = list(weights)
        self.window, self.first, self.start, self.pace = window, first, start, pace
        self.everyone = ("shard",)
        shards, replicas = lax.axis_size("shard"), lax.axis_size("replica")
        self.part = weights[0].shape[0] // replicas
        wide = len(weights) * window
        shape = (shards, replicas, self.part, wide)
        self.outputs = [(ANY, jax.ShapeDtypeStruct(shape, weights[0].dtype))]
        self.scratch = [
            DMA((len(weights),)),
            DMA((len(weights), shards)),
            DMA((len(weights), shards)),
        ] + gather_sems("replica", shards)

    def steps(self, lines, ins, outs, scratch):
        own_sem, deal_send, deal_recv, *sems = scratch
        (out_ref,) = outs
        group, copies = lines["shard"], lines["replica"]
        rows = pl.ds(pl.multiple_of(copies.me * self.part, self.part), self.part)
        kinds = range(len(ins))

        def source(kind, target):
            return ins[kind].at[rows, pl.ds(pl.multiple_of(self.first(target), 128), self.window)]

        def landing(kind, origin):
            return out_ref.at[origin, copies.me, :, pl.ds(kind * self.window, self.window)]

        def own(kind):
            return pltpu.make_async_copy(
                source(kind, group.me), landing(kind, group.me), own_sem.at[kind]
            )

        def deal(kind, k):
            target = group.other(k)
            return remote(
                source(kind, target),
                landing(kind, group.me),
                deal_send.at[kind, k],
                deal_recv.at[kind, group.me],
                {"shard": target},
            )

        def begin():
            for k in range(1, group.count):
                for kind in kinds:
                    deal(kind, k).start()
            for kind in kinds:
                own(kind).start()

        def ready(c):
            @pl.when(c == group.me)
            def _():
                for kind in kinds:
                    own(kind).wait()

            @pl.when(c != group.me)
            def _():
                for kind in kinds:
                    in_place(landing(kind, c), deal_recv.at[kind, c]).wait()

        def finish():
            for k in range(1, group.count):
                for kind in kinds:
                    deal(kind, k).wait_send()

        steps = gather_steps(
            copies,
            group.count,
            lambda origin, c: out_ref.at[c, origin],
            lambda c: out_ref.at[c, copies.me],
            ready,
            sems,
            self.start + 2 * self.pace,
            2 * self.pace,
        )
        return [(self.start, begin)] + steps + [(steps[-1][0], finish)]


class Trade:
    def __init__(self, block, first, width, start=0.0, pace=6.0):
        self.inputs = [block]
        self.first, self.width, self.start, self.pace = first, width, start, pace
        self.everyone = ()
        shards, part, _ = block.shape
        shape = (shards, lax.axis_size("replica"), part, width)
        self.outputs = [(ANY, jax.ShapeDtypeStruct(shape, block.dtype))]
        self.scratch = [pltpu.VMEM((shards, part, width), block.dtype), DMA((2,))]
        self.scratch += gather_sems("replica", shards)

    def steps(self, lines, ins, outs, scratch):
        held, own_sems, *sems = scratch
        (x_ref,), (out_ref,) = ins, outs
        copies = lines["replica"]
        cols = pl.ds(self.first, self.width)
        begin, turn, end = staged(
            x_ref.at[:, :, cols], out_ref.at[:, copies.me], held, own_sems
        )
        steps = gather_steps(
            copies,
            x_ref.shape[0],
            lambda origin, c: out_ref.at[c, origin],
            lambda c: x_ref.at[c, :, cols],
            lambda c: None,
            sems,
            self.start,
            self.pace,
        )
        return [(self.start, begin), (self.start + 3.0, turn)] + steps + [(steps[-1][0], end)]


class Sum:
    def __init__(self, terms, start=0.0, pace=6.0, lag=0.0):
        shards, replicas = lax.axis_size("shard"), lax.axis_size("replica")
        part, wide = terms.shape[0] // shards // replicas, terms.shape[1]
        self.inputs = [terms.reshape(shards, replicas, part, wide)]
        self.start, self.pace, self.lag = start, pace, lag
        self.everyone = ()
        self.outputs = [(VMEM, jax.ShapeDtypeStruct((shards, part, wide), terms.dtype))]
        self.scratch = scatter_scratch(grid_of("replica"), shards, part, wide, terms.dtype)

    def steps(self, lines, ins, outs, scratch):
        (p_ref,), (out_ref,) = ins, outs

        def store(c, part, total):
            out_ref[c, part] = total.astype(out_ref.dtype)

        return scatter_steps(
            lines["replica"],
            out_ref.shape[0],
            lambda slot: p_ref.at[:, slot],
            lambda slot, c: p_ref.at[c, slot],
            scratch,
            store,
            lambda c: None,
            self.start,
            self.pace,
            lag=self.lag,
        )


class Deliver:
    def __init__(self, sums, start=0.0, again=30.0, pace=24.0):
        self.inputs = [sums]
        self.start, self.again, self.pace = start, again, pace
        self.everyone = ("shard",)
        shards, replicas = lax.axis_size("shard"), lax.axis_size("replica")
        self.outputs = [(ANY, jax.ShapeDtypeStruct((replicas,) + sums.shape, sums.dtype))]
        self.scratch = [DMA, DMA((shards,)), DMA((shards,))] + gather_sems("replica", shards)

    def steps(self, lines, ins, outs, scratch):
        own_sem, send_sem, recv_sem, *sems = scratch
        (x_ref,), (out_ref,) = ins, outs
        group, copies = lines["shard"], lines["replica"]
        own = pltpu.make_async_copy(
            x_ref.at[group.me], out_ref.at[copies.me, group.me], own_sem
        )

        def deal(k):
            target = group.other(k)
            return remote(
                x_ref.at[target],
                out_ref.at[copies.me, group.me],
                send_sem.at[k],
                recv_sem.at[group.me],
                {"shard": target},
            )

        def begin():
            own.start()
            for k in range(1, group.count):
                deal(k).start()

        def ready(c):
            @pl.when(c == group.me)
            def _():
                own.wait()

            @pl.when(c != group.me)
            def _():
                in_place(out_ref.at[copies.me, c], recv_sem.at[c]).wait()

        def finish():
            for k in range(1, group.count):
                deal(k).wait_send()

        steps = gather_steps(
            copies,
            group.count,
            lambda origin, c: out_ref.at[origin, c],
            lambda c: out_ref.at[copies.me, c],
            ready,
            sems,
            self.again,
            self.pace,
        )
        return [(self.start, begin)] + steps + [(steps[-1][0], finish)]


class Total:
    def __init__(self, terms, start=0.0, pace=6.0, again=60.0, lag=0.0):
        replicas = lax.axis_size("replica")
        share, wide = terms.shape[0] // replicas, terms.shape[1]
        chunks = max(n for n in (1, 2, 3, 4) if share % (n * STEP) == 0)
        rows = share // chunks
        self.inputs = [terms.reshape(replicas, chunks, rows, wide)]
        self.start, self.pace, self.again, self.chunks = start, pace, again, chunks
        self.lag = lag
        self.everyone = ()
        kind = terms.dtype
        self.outputs = [(ANY, jax.ShapeDtypeStruct((replicas, chunks, rows, wide), kind))]
        self.scratch = [pltpu.VMEM((chunks, rows, wide), kind), DMA((chunks,))]
        self.scratch += gather_sems("replica", chunks)
        self.scratch += scatter_scratch(grid_of("replica"), chunks, rows, wide, kind)

    def steps(self, lines, ins, outs, scratch):
        (p_ref,), (out_ref,) = ins, outs
        total_ref, own_sem = scratch[:2]
        copies = lines["replica"]

        def own(c):
            return pltpu.make_async_copy(
                total_ref.at[c], out_ref.at[copies.me, c], own_sem.at[c]
            )

        def store(c, part, total):
            total_ref[c, part] = total.astype(total_ref.dtype)

        def finish():
            for c in range(self.chunks):
                own(c).wait()

        summing = scatter_steps(
            copies,
            self.chunks,
            lambda slot: p_ref.at[slot],
            lambda slot, c: p_ref.at[slot, c],
            scratch[4:],
            store,
            lambda c: own(c).start(),
            self.start,
            self.pace,
            lag=self.lag,
        )
        sharing = gather_steps(
            copies,
            self.chunks,
            lambda origin, c: out_ref.at[origin, c],
            lambda c: total_ref.at[c],
            lambda c: None,
            scratch[2:4],
            self.again,
            self.pace,
        )
        return summing + sharing + [(sharing[-1][0], finish)]


class Small:
    def __init__(self, dealt, shared, start=0.0):
        shards, replicas = lax.axis_size("shard"), lax.axis_size("replica")
        self.inputs = [dealt, shared]
        self.start = start
        self.everyone = ("shard", "replica")
        one = dealt.shape[1:]
        self.outputs = [
            (VMEM, jax.ShapeDtypeStruct(one, jnp.float32)),
            (VMEM, jax.ShapeDtypeStruct(shared.shape, jnp.float32)),
        ]
        self.scratch = [
            pltpu.VMEM((shards,) + one, jnp.float32),
            pltpu.VMEM((replicas,) + one, jnp.float32),
            pltpu.VMEM((replicas,) + shared.shape, jnp.float32),
            DMA((shards,)), DMA((shards,)),
            DMA((2, replicas)), DMA((2, replicas)), DMA((2,)),
        ]

    def steps(self, lines, ins, outs, scratch):
        dealt, shared = ins
        out_one, out_rows = outs
        got, got_one, got_rows, send, recv, send2, recv2, own = scratch
        group, copies = lines["shard"], lines["replica"]

        def deal(k):
            target = group.other(k)
            return remote(
                dealt.at[target], got.at[group.me], send.at[k], recv.at[group.me], {"shard": target}
            )

        def share(which, k):
            buffer = (got_one, got_rows)[which]
            return remote(
                buffer.at[copies.me] if which == 0 else shared,
                buffer.at[copies.me],
                send2.at[which, k],
                recv2.at[which, copies.me],
                {"replica": copies.other(k)},
            )

        def keep():
            return pltpu.make_async_copy(dealt.at[group.me], got.at[group.me], own.at[0])

        def keep_rows():
            return pltpu.make_async_copy(shared, got_rows.at[copies.me], own.at[1])

        def begin():
            keep().start()
            keep_rows().start()
            for k in range(1, group.count):
                deal(k).start()
            for k in range(1, copies.count):
                share(1, k).start()

        def middle():
            keep().wait()
            for k in range(1, group.count):
                origin = group.other(k)
                in_place(got.at[origin], recv.at[origin]).wait()
            total = got[0]
            for s in range(1, group.count):
                total = total + got[s]
            got_one[copies.me] = total
            for k in range(1, copies.count):
                share(0, k).start()

        def end():
            keep_rows().wait()
            for k in range(1, copies.count):
                origin = copies.other(k)
                in_place(got_one.at[origin], recv2.at[0, origin]).wait()
                in_place(got_rows.at[origin], recv2.at[1, origin]).wait()
            one, rows = got_one[0], got_rows[0]
            for r in range(1, copies.count):
                one, rows = one + got_one[r], rows + got_rows[r]
            out_one[...] = one
            out_rows[...] = rows
            for k in range(1, group.count):
                deal(k).wait_send()
            for k in range(1, copies.count):
                share(0, k).wait_send()
                share(1, k).wait_send()

        return [(-0.5, begin), (self.start, middle), (self.start + 40.0, end)]


def layout_of(tasks):
    inputs, outputs, scratch, spans = [], [], [], []
    for task in tasks:
        spans.append((len(inputs), len(outputs), len(scratch)))
        inputs += task.inputs
        outputs += task.outputs
        scratch += task.scratch
    return inputs, outputs, scratch, spans


def task_steps(tasks, spans, axes, ins, outs, scratch):
    lines = {axis: Lines(axis) for axis in axes}
    everyone = {axis for task in tasks for axis in task.everyone}
    steps = []
    for task, (i, o, s) in zip(tasks, spans):
        steps += task.steps(
            lines,
            ins[i : i + len(task.inputs)],
            outs[o : o + len(task.outputs)],
            scratch[s : s + len(task.scratch)],
        )
    steps.sort(key=lambda step: step[0])
    return [(-1.0, lambda: greet(list(lines.values()), everyone))] + steps


def exchange(tasks, axes, ident):
    inputs, outputs, scratch, spans = layout_of(tasks)

    def kernel(*refs):
        ins = refs[: len(inputs)]
        outs = refs[len(inputs) : len(inputs) + len(outputs)]
        rest = refs[len(inputs) + len(outputs) :]
        for _, step in task_steps(tasks, spans, axes, ins, outs, rest):
            step()

    return pl.pallas_call(
        kernel,
        in_specs=[ANY] * len(inputs),
        out_specs=[spec for spec, _ in outputs],
        out_shape=[shape for _, shape in outputs],
        scratch_shapes=scratch,
        compiler_params=pltpu.CompilerParams(
            collective_id=ident, has_side_effects=True, vmem_limit_bytes=60 * 1024 * 1024
        ),
    )(*inputs)


HD = 128
TAPS = 4
KINDS = 3


def dot_nn(a, b):
    return lax.dot_general(
        a.astype(jnp.bfloat16),
        b.astype(jnp.bfloat16),
        (((1,), (0,)), ((), ())),
        preferred_element_type=jnp.float32,
    )


def dot_nt(a, b):
    return lax.dot_general(
        a.astype(jnp.bfloat16),
        b.astype(jnp.bfloat16),
        (((1,), (1,)), ((), ())),
        preferred_element_type=jnp.float32,
    )


def dot_tn(a, b):
    return lax.dot_general(
        a.astype(jnp.bfloat16),
        b.astype(jnp.bfloat16),
        (((0,), (0,)), ((), ())),
        preferred_element_type=jnp.float32,
    )


def time_of(shape, dim, lanes):
    index = lax.broadcasted_iota(jnp.int32, shape, dim)
    return lax.rem(index, 8) * lanes + lax.div(index, 8)


def lower_inverses(lowers, lanes):
    size = lowers[0].shape[0]
    row_t = time_of((size, size), 0, lanes)
    col_t = time_of((size, size), 1, lanes)
    eye = jnp.where(row_t == col_t, 1.0, 0.0)

    def same(width):
        return lax.div(row_t, width) == lax.div(col_t, width)

    first = [jnp.where(same(8), a, 0.0) for a in lowers]
    second = [dot_nn(f, f) for f in first]
    inverse = [eye + f + s + dot_nn(f, s) for f, s in zip(first, second)]
    fourth = [dot_nn(s, s) for s in second]
    inverse = [t + dot_nn(t, f) for t, f in zip(inverse, fourth)]
    width = 16
    while width <= size:
        fresh = same(width) & jnp.logical_not(same(width // 2))
        left = [dot_nn(t, jnp.where(fresh, a, 0.0)) for t, a in zip(inverse, lowers)]
        inverse = [t + dot_nn(l, t) for t, l in zip(inverse, left)]
        width *= 2
    return inverse


def rounded(values):
    return values.astype(jnp.bfloat16).astype(jnp.float32)


def sigmoid(values):
    return 1.0 / (1.0 + jnp.exp(-values))


def unit_scale(pre):
    return lax.rsqrt(jnp.sum(pre * pre, axis=1, keepdims=True) + 1e-6)


def mean_scale(values):
    return lax.rsqrt(jnp.mean(values * values, axis=1, keepdims=True) + 1e-5)


def delta_forward(
    lanes, heads, group, proj_ref, taps_ref, gain_ref, low_ref, off_ref, rem_ref,
    zed_ref, mixed_ref, sums_ref, s_ref, t_ref, mk_ref, mv_ref, u_ref,
    state, last, unit,
):
    size = lanes * 8
    rows = group * 8
    wide = heads * HD
    scale = HD ** (-0.5)

    @pl.when(pl.program_id(0) == 0)
    def _():
        state[...] = jnp.zeros_like(state)
        last[...] = jnp.zeros_like(last)

    top = lax.broadcasted_iota(jnp.int32, (rows, HD), 0) == 0
    for kind in range(KINDS):
        for h in range(heads):
            cols = pl.ds(kind * wide + h * HD, HD)
            signal = [rounded(proj_ref[s, :, cols]) for s in range(lanes)]
            moved = {}
            for back in range(1, TAPS):
                lane = lanes - back
                edge = last[kind * heads + h, back, 0:1]
                moved[lane] = jnp.where(top, edge, pltpu.roll(signal[lane], 1, 0))
            for back in range(1, TAPS):
                last[kind * heads + h, back, 0:1] = signal[lanes - back][rows - 1 : rows]
            for s in range(lanes):
                off = off_ref[s]
                total = signal[s] * taps_ref[kind * TAPS : kind * TAPS + 1, h * HD : (h + 1) * HD]
                for hop in range(1, TAPS):
                    earlier = signal[s - hop] if s >= hop else moved[lanes + s - hop]
                    tap = taps_ref[kind * TAPS + hop : kind * TAPS + hop + 1, h * HD : (h + 1) * HD]
                    total = total + jnp.where(off >= hop, earlier, 0.0) * tap
                sums_ref[s, :, cols] = total
                pre = total * sigmoid(total)
                if kind < 2:
                    pre = pre * unit_scale(pre)
                unit[s, :, cols] = pre

    row_t = time_of((size, size), 0, lanes)
    col_t = time_of((size, size), 1, lanes)
    local_t = time_of((size, HD), 0, lanes).astype(jnp.float32)
    pairs = [(g, h) for g in range(group) for h in range(heads)]

    def span(g):
        return pl.ds(g * 8, 8)

    def flat(ref, g, first, count=HD):
        return ref[:, span(g), first : first + count].reshape(size, count)

    gates = {}
    for g in range(group):
        logits = flat(proj_ref, g, 4 * wide)
        strength = sigmoid(rounded(logits))
        for h in range(heads):
            gates[g, h] = jnp.broadcast_to(strength[:, h : h + 1], (size, HD))
    keys = {p: flat(unit, p[0], wide + p[1] * HD) for p in pairs}
    kbs = {p: gates[p] * keys[p] for p in pairs}
    lows = {g: low_ref[g].astype(jnp.float32) for g in range(group)}
    lowers = [
        -jnp.where(row_t == col_t, 0.0, lows[p[0]]) * dot_nt(kbs[p], keys[p]) for p in pairs
    ]
    inverses = dict(zip(pairs, lower_inverses(lowers, lanes)))
    mks = {p: dot_nn(inverses[p], kbs[p]) for p in pairs}
    mvs = {
        p: dot_nn(inverses[p], gates[p] * flat(unit, p[0], 2 * wide + p[1] * HD))
        for p in pairs
    }
    queries = {p: flat(unit, p[0], p[1] * HD) for p in pairs}
    scores = {p: lows[p[0]] * dot_nt(queries[p], keys[p]) for p in pairs}
    for g, h in pairs:
        t_ref[g, h] = inverses[g, h].astype(t_ref.dtype)
        mk_ref[g, h] = mks[g, h].astype(mk_ref.dtype)
        mv_ref[g, h] = mvs[g, h].astype(mv_ref.dtype)
    for g in range(group):
        carry = jnp.where(flat(off_ref, g, 0) > local_t, 1.0, 0.0)
        keep = jnp.where(flat(rem_ref, g, 0) + local_t >= size, 1.0, 0.0)
        for h in range(heads):
            p = (g, h)
            held = state[h]
            s_ref[g, h] = held.astype(s_ref.dtype)
            u = mvs[p] - carry * dot_nn(mks[p], held)
            u_ref[g, h] = u.astype(u_ref.dtype)
            state[h] = (carry[0:1] * keep[0:1]) * held + dot_tn(keys[p], keep * u)
            out = (carry * dot_nn(queries[p], held) + dot_nn(scores[p], u)) * scale
            mixed = rounded(out)
            gate = flat(proj_ref, g, 3 * wide + h * HD)
            zed = mixed * mean_scale(mixed) * gain_ref[...] * (gate * sigmoid(gate))
            mixed_ref[:, span(g), h * HD : (h + 1) * HD] = mixed.reshape(lanes, 8, HD).astype(
                mixed_ref.dtype
            )
            zed_ref[:, span(g), h * HD : (h + 1) * HD] = zed.reshape(lanes, 8, HD).astype(
                zed_ref.dtype
            )


def delta_backward(
    lanes, heads, group, proj_ref, sums_ref, mixed_ref, dzed_ref, taps_ref, gain_ref,
    low_ref, off_ref, rem_ref, s_ref, t_ref, mk_ref, mv_ref, u_ref,
    dproj_ref, gtaps_ref, ghead_ref,
    state, edge, edge_off, errs, taps_sum, head_sum,
):
    size = lanes * 8
    rows = group * 8
    wide = heads * HD
    scale = HD ** (-0.5)

    @pl.when(pl.program_id(0) == 0)
    def _():
        state[...] = jnp.zeros_like(state)
        edge[...] = jnp.zeros_like(edge)
        edge_off[...] = jnp.zeros_like(edge_off)
        taps_sum[...] = jnp.zeros_like(taps_sum)
        head_sum[...] = jnp.zeros_like(head_sum)

    row_t = time_of((size, size), 0, lanes)
    col_t = time_of((size, size), 1, lanes)
    local_t = time_of((size, HD), 0, lanes).astype(jnp.float32)
    lane_id = lax.broadcasted_iota(jnp.int32, (size, HD), 1)
    pairs = [(g, h) for g in range(group) for h in range(heads)]

    def span(g):
        return pl.ds(g * 8, 8)

    def flat(ref, g, first, count=HD):
        return ref[:, span(g), first : first + count].reshape(size, count)

    def put(ref, g, first, value):
        ref[:, span(g), first : first + HD] = value.reshape(lanes, 8, HD).astype(ref.dtype)

    gain = gain_ref[...]
    d_out, q, k, v, beta = {}, {}, {}, {}, {}
    pre, scales, slopes = {}, {}, {}
    head_total = jnp.zeros((size, HD), jnp.float32)
    strengths = {}
    carries, keeps, lows = {}, {}, {}
    for g in range(group):
        carries[g] = jnp.where(flat(off_ref, g, 0) > local_t, 1.0, 0.0)
        keeps[g] = jnp.where(flat(rem_ref, g, 0) + local_t >= size, 1.0, 0.0)
        lows[g] = low_ref[g].astype(jnp.float32)
        strengths[g] = sigmoid(rounded(flat(proj_ref, g, 4 * wide)))
    for g, h in pairs:
        p = (g, h)
        mixed = flat(mixed_ref, g, h * HD).astype(jnp.float32)
        gate = flat(proj_ref, g, 3 * wide + h * HD)
        dzed = flat(dzed_ref, g, h * HD)
        s = sigmoid(gate)
        r = mean_scale(mixed)
        through = dzed * (gate * s)
        head_total = head_total + through * mixed * r
        inner = jnp.mean(mixed * gain * through, axis=1, keepdims=True)
        d_mixed = rounded(r * gain * through - mixed * (r * r * r) * inner)
        put(dproj_ref, g, 3 * wide + h * HD, dzed * (mixed * r * gain) * (s * (1.0 + gate * (1.0 - s))))
        d_out[p] = d_mixed * scale
        for kind, store in ((0, q), (1, k), (2, v)):
            total = flat(sums_ref, g, kind * wide + h * HD)
            s = sigmoid(total)
            value = total * s
            slopes[kind, g, h] = s * (1.0 + total * (1.0 - s))
            if kind < 2:
                pre[kind, g, h] = value
                scales[kind, g, h] = unit_scale(value)
                value = value * scales[kind, g, h]
            store[p] = value
        beta[p] = jnp.broadcast_to(strengths[g][:, h : h + 1], (size, HD))
    head_sum[...] += head_total

    scores = {p: lows[p[0]] * dot_nt(q[p], k[p]) for p in pairs}
    du = {p: dot_tn(scores[p], d_out[p]) for p in pairs}
    ds = {p: lows[p[0]] * dot_nt(d_out[p], u_ref[p[0], p[1]]) for p in pairs}
    cdo = {p: carries[p[0]] * d_out[p] for p in pairs}
    dq = {p: dot_nt(cdo[p], s_ref[p[0], p[1]]) + dot_nn(ds[p], k[p]) for p in pairs}
    dk = {p: dot_tn(ds[p], q[p]) for p in pairs}
    lift = {p: dot_tn(q[p], cdo[p]) for p in pairs}
    later = {}
    for g in reversed(range(group)):
        for h in range(heads):
            p = (g, h)
            later[p] = state[h]
            du[p] = du[p] + keeps[g] * dot_nn(k[p], later[p])
            mk = carries[g] * mk_ref[g, h].astype(jnp.float32)
            state[h] = (carries[g][0:1] * keeps[g][0:1]) * later[p] + lift[p] - dot_tn(mk, du[p])
    for p in pairs:
        dk[p] = dk[p] + dot_nt(keeps[p[0]] * u_ref[p[0], p[1]].astype(jnp.float32), later[p])
    dmk = {p: -carries[p[0]] * dot_nt(du[p], s_ref[p[0], p[1]]) for p in pairs}
    xx = {p: dot_tn(t_ref[p[0], p[1]], dmk[p]) for p in pairs}
    yy = {p: dot_tn(t_ref[p[0], p[1]], du[p]) for p in pairs}
    da = {
        p: jnp.where(row_t == col_t, 0.0, lows[p[0]])
        * (dot_nt(xx[p], mk_ref[p[0], p[1]]) + dot_nt(yy[p], mv_ref[p[0], p[1]]))
        for p in pairs
    }
    dkb = {p: xx[p] - dot_nn(da[p], k[p]) for p in pairs}
    dk = {p: dk[p] - dot_tn(da[p], beta[p] * k[p]) + beta[p] * dkb[p] for p in pairs}
    for g in range(group):
        d_logits = jnp.zeros((size, HD), jnp.float32)
        for h in range(heads):
            p = (g, h)
            db = jnp.sum(dkb[p] * k[p] + yy[p] * v[p], axis=1, keepdims=True)
            d_logits = d_logits + jnp.where(lane_id == h, db * beta[p] * (1.0 - beta[p]), 0.0)
            for kind, grad in ((0, dq[p]), (1, dk[p])):
                r, raw = scales[kind, g, h], pre[kind, g, h]
                inner = jnp.sum(raw * grad, axis=1, keepdims=True)
                err = (r * grad - raw * (r * r * r) * inner) * slopes[kind, g, h]
                put(errs, g, kind * wide + h * HD, err)
            put(errs, g, 2 * wide + h * HD, beta[p] * yy[p] * slopes[2, g, h])
        put(dproj_ref, g, 4 * wide, d_logits)

    bottom = lax.broadcasted_iota(jnp.int32, (rows, HD), 0) == rows - 1
    for kind in range(KINDS):
        for h in range(heads):
            at = kind * wide + h * HD
            cols = pl.ds(at, HD)
            err = [errs[s, :, cols] for s in range(lanes)]
            taps = [
                taps_ref[kind * TAPS + hop : kind * TAPS + hop + 1, h * HD : (h + 1) * HD]
                for hop in range(TAPS)
            ]
            sums = [jnp.zeros((rows, HD), jnp.float32) for _ in range(TAPS)]
            live = {}
            for hop in range(1, TAPS):
                for s in range(lanes):
                    live[hop, s] = jnp.where(off_ref[s] >= hop, err[s], 0.0)
            for hop in range(1, TAPS):
                for s in range(hop):
                    row = jnp.where(edge_off[s, 0:1] >= hop, edge[kind * heads + h, s, 0:1], 0.0)
                    live[hop, lanes + s] = jnp.where(
                        bottom, row, pltpu.roll(live[hop, s], rows - 1, 0)
                    )
            for s in range(lanes):
                signal = rounded(proj_ref[s, :, cols])
                total = err[s] * taps[0]
                sums[0] = sums[0] + err[s] * signal
                for hop in range(1, TAPS):
                    total = total + live[hop, s + hop] * taps[hop]
                    sums[hop] = sums[hop] + live[hop, s + hop] * signal
                dproj_ref[s, :, cols] = total.astype(dproj_ref.dtype)
            for s in range(TAPS - 1):
                edge[kind * heads + h, s, 0:1] = err[s][0:1]
            for hop in range(TAPS):
                folded = sums[hop].reshape(group, 8, HD)
                taps_sum[kind * TAPS + hop, :, h * HD : (h + 1) * HD] += jnp.sum(folded, axis=0)
    for s in range(TAPS - 1):
        edge_off[s, 0:1] = off_ref[s][0:1]

    @pl.when(pl.program_id(0) == pl.num_programs(0) - 1)
    def _():
        gtaps_ref[...] = jnp.sum(taps_sum[...], axis=1)
        ghead_ref[...] = jnp.sum(head_sum[...], axis=0, keepdims=True)


def mixer_specs(lanes, heads, group, flip):
    size = lanes * 8
    at = (lambda i: flip - 1 - i) if flip else (lambda i: i)

    def token(width):
        return pl.BlockSpec((lanes, 8 * group, width), lambda i: (0, at(i), 0))

    def saved(first, second):
        return pl.BlockSpec((group, heads, first, second), lambda i: (at(i), 0, 0, 0))

    square = pl.BlockSpec((group, size, size), lambda i: (at(i), 0, 0))
    return token, saved, square


def fixed(shape):
    return pl.BlockSpec(shape, lambda i: (0,) * len(shape))


def saved_shapes(lanes, heads, blocks):
    size = lanes * 8
    kind = jnp.bfloat16
    return [
        jax.ShapeDtypeStruct((blocks, heads, HD, HD), kind),
        jax.ShapeDtypeStruct((blocks, heads, size, size), kind),
        jax.ShapeDtypeStruct((blocks, heads, size, HD), kind),
        jax.ShapeDtypeStruct((blocks, heads, size, HD), kind),
        jax.ShapeDtypeStruct((blocks, heads, size, HD), kind),
    ]


def mixer_forward(proj, taps, gain, low, off, rem, heads, group=4):
    lanes, tokens, width = proj.shape
    blocks, wide = tokens // 8, heads * HD
    size = lanes * 8
    token, saved, square = mixer_specs(lanes, heads, group, 0)
    return pl.pallas_call(
        functools.partial(delta_forward, lanes, heads, group),
        grid=(blocks // group,),
        in_specs=[token(width), fixed(taps.shape), fixed(gain.shape), square, token(HD), token(HD)],
        out_specs=[
            token(wide), token(wide), token(KINDS * wide),
            saved(HD, HD), saved(size, size), saved(size, HD), saved(size, HD), saved(size, HD),
        ],
        out_shape=[
            jax.ShapeDtypeStruct((lanes, tokens, wide), jnp.bfloat16),
            jax.ShapeDtypeStruct((lanes, tokens, wide), jnp.bfloat16),
            jax.ShapeDtypeStruct((lanes, tokens, KINDS * wide), jnp.float32),
        ] + saved_shapes(lanes, heads, blocks),
        scratch_shapes=[
            pltpu.VMEM((heads, HD, HD), jnp.float32),
            pltpu.VMEM((KINDS * heads, TAPS, 8, HD), jnp.float32),
            pltpu.VMEM((lanes, 8 * group, KINDS * wide), jnp.float32),
        ],
        compiler_params=pltpu.CompilerParams(vmem_limit_bytes=48 * 1024 * 1024),
        cost_estimate=pl.CostEstimate(flops=35 * 10**9, bytes_accessed=40 * 10**6, transcendentals=0),
    )(proj, taps, gain, low, off, rem)


def mixer_backward(
    proj, sums, mixed, dzed, taps, gain, low, off, rem, saves, heads, group=4
):
    lanes, tokens, width = proj.shape
    blocks, wide = tokens // 8, heads * HD
    size = lanes * 8
    token, saved, square = mixer_specs(lanes, heads, group, blocks // group)
    return pl.pallas_call(
        functools.partial(delta_backward, lanes, heads, group),
        grid=(blocks // group,),
        in_specs=[
            token(width), token(KINDS * wide), token(wide), token(wide),
            fixed(taps.shape), fixed(gain.shape), square, token(HD), token(HD),
            saved(HD, HD), saved(size, size), saved(size, HD), saved(size, HD), saved(size, HD),
        ],
        out_specs=[token(width), fixed(taps.shape), fixed(gain.shape)],
        out_shape=[
            jax.ShapeDtypeStruct((lanes, tokens, width), jnp.bfloat16),
            jax.ShapeDtypeStruct(taps.shape, jnp.float32),
            jax.ShapeDtypeStruct(gain.shape, jnp.float32),
        ],
        scratch_shapes=[
            pltpu.VMEM((heads, HD, HD), jnp.float32),
            pltpu.VMEM((KINDS * heads, TAPS, 8, HD), jnp.float32),
            pltpu.VMEM((TAPS, 8, HD), jnp.float32),
            pltpu.VMEM((lanes, 8 * group, KINDS * wide), jnp.float32),
            pltpu.VMEM((taps.shape[0], 8, wide), jnp.float32),
            pltpu.VMEM((size, HD), jnp.float32),
        ],
        compiler_params=pltpu.CompilerParams(vmem_limit_bytes=48 * 1024 * 1024),
        cost_estimate=pl.CostEstimate(flops=35 * 10**9, bytes_accessed=40 * 10**6, transcendentals=0),
    )(proj, sums, mixed, dzed, taps, gain, low, off, rem, *saves)


def segment_masks(lengths_grid, order_row, lanes, tokens):
    slots = order_row.shape[0]
    flat = lengths_grid.reshape(slots)
    first = lax.broadcasted_iota(jnp.int32, (slots, slots), 0)
    second = lax.broadcasted_iota(jnp.int32, (slots, slots), 1)
    run_len = jnp.sum(jnp.where(order_row[:, None] == second, flat[None, :], 0), axis=1)
    ends = jnp.sum(jnp.where(first >= second, run_len[None, :], 0), axis=1)
    starts = ends - run_len
    size = lanes * 8
    blocks = tokens // 8
    lane = lax.broadcasted_iota(jnp.int32, (lanes, tokens), 0)
    step = lax.broadcasted_iota(jnp.int32, (lanes, tokens), 1)
    place = step * lanes + lane
    inside = (starts[:, None, None] <= place[None]) & (place[None] < ends[:, None, None])
    start_at = jnp.sum(jnp.where(inside, starts[:, None, None], 0), axis=0)
    end_at = jnp.sum(jnp.where(inside, ends[:, None, None], 0), axis=0)

    def blocked(values):
        return values.reshape(lanes, blocks, 8).transpose(1, 0, 2).reshape(blocks, size)

    start_b, place_b = blocked(start_at), blocked(place)
    low = (start_b[:, :, None] == start_b[:, None, :]) & (place_b[:, :, None] >= place_b[:, None, :])

    def spread(values):
        return jnp.broadcast_to(values.astype(jnp.float32)[:, :, None], (lanes, tokens, HD))

    return low.astype(jnp.bfloat16), spread(place - start_at), spread(end_at - place)


def exchange_beside(tasks, axes, ident, compute, grid, pace, operands, results, scratch, flops):
    inputs, outputs, own_scratch, spans = layout_of(tasks)
    counts = (len(inputs), len(operands), len(outputs), len(results), len(own_scratch), len(scratch))

    def kernel(*refs):
        groups, at = [], 0
        for count in counts:
            groups.append(refs[at : at + count])
            at += count
        task_ins, ins, task_outs, outs, task_scratch, rest = groups
        steps = task_steps(tasks, spans, axes, task_ins, task_outs, task_scratch)
        due = [min(max(int(when // pace), 0), grid) for when, _ in steps]
        for i in range(grid):
            if i in due:

                @pl.when(pl.program_id(0) == i)
                def _(i=i):
                    for turn, (_, step) in zip(due, steps):
                        if turn == i:
                            step()

        compute(*ins, *outs, *rest)

        @pl.when(pl.program_id(0) == grid - 1)
        def _():
            for turn, (_, step) in zip(due, steps):
                if turn == grid:
                    step()

    return pl.pallas_call(
        kernel,
        grid=(grid,),
        in_specs=[ANY] * len(inputs) + [spec for _, spec in operands],
        out_specs=[spec for spec, _ in outputs] + [spec for spec, _ in results],
        out_shape=[shape for _, shape in outputs] + [shape for _, shape in results],
        scratch_shapes=own_scratch + list(scratch),
        compiler_params=pltpu.CompilerParams(
            collective_id=ident, has_side_effects=True, vmem_limit_bytes=60 * 1024 * 1024
        ),
        cost_estimate=pl.CostEstimate(flops=flops, bytes_accessed=60 * 10**6, transcendentals=0),
    )(*inputs, *[array for array, _ in operands])


def exchange_computed(task, tasks, axes, ident, fill, compute, grid, pace, operands, results, flops):
    slots = lax.axis_size(task.axis)
    everything = [task] + tasks
    inputs, outputs, own_scratch, spans = layout_of(everything)
    counts = (len(inputs), len(operands), len(outputs), len(results), len(own_scratch))

    def kernel(*refs):
        groups, at = [], 0
        for count in counts:
            groups.append(refs[at : at + count])
            at += count
        task_ins, ins, task_outs, outs, task_scratch = groups
        steps = task_steps(everything, spans, axes, task_ins, task_outs, task_scratch)
        due = [min(max(int(when // pace), 0), grid + slots) for when, _ in steps]
        now = pl.program_id(0)
        for i in range(slots + grid):

            @pl.when(now == i)
            def _(i=i):
                for turn, (_, step) in zip(due, steps):
                    if turn == i:
                        step()
                if i < slots:
                    fill(task.slot(i), task.terms, *ins, *outs)
                    task.launch(i)
                else:
                    compute(*ins, *outs)

        @pl.when(now == slots + grid - 1)
        def _():
            for turn, (_, step) in zip(due, steps):
                if turn == slots + grid:
                    step()

    return pl.pallas_call(
        kernel,
        grid=(slots + grid,),
        in_specs=[ANY] * len(inputs) + [spec for _, spec in operands],
        out_specs=[spec for spec, _ in outputs] + [spec for spec, _ in results],
        out_shape=[shape for _, shape in outputs] + [shape for _, shape in results],
        scratch_shapes=own_scratch,
        compiler_params=pltpu.CompilerParams(
            collective_id=ident, has_side_effects=True, vmem_limit_bytes=60 * 1024 * 1024
        ),
        cost_estimate=pl.CostEstimate(flops=flops, bytes_accessed=60 * 10**6, transcendentals=0),
    )(*inputs, *[array for array, _ in operands])


def fill_input_terms(slot, terms, proj_ref, weights_ref):
    chunks, rows, width = terms.shape[1:]
    own = proj_ref[pl.ds(pl.multiple_of(slot * chunks * rows, chunks * rows), chunks * rows)]
    wide = 512
    for n in range(0, width, wide):
        part = dot_nt(own, weights_ref[n : n + wide])
        terms[slot, :, :, n : n + wide] = part.reshape(chunks, rows, wide).astype(terms.dtype)


def feed_forward(
    rows, window, zed_ref, source_ref, wo_ref, wi_ref, wd_ref, gain_ref,
    hidden_ref, in_ref, product_ref, slopes_ref, out_ref, held,
):
    width = source_ref.shape[1]
    wide = 512
    squares = jnp.zeros((rows, 1), jnp.float32)
    for n in range(0, width, wide):
        cols = slice(n, n + wide)
        part = source_ref[:, cols].astype(jnp.float32) + dot_nn(zed_ref[...], wo_ref[:, cols])
        held[:, cols] = part
        squares = squares + jnp.sum(part * part, axis=1, keepdims=True)
    scale = lax.rsqrt(squares / width + 1e-6)
    for n in range(0, width, wide):
        cols = slice(n, n + wide)
        in_ref[:, cols] = (held[:, cols] * scale * gain_ref[:, cols]).astype(in_ref.dtype)

    @pl.when(pl.program_id(0) == lax.axis_index("shard"))
    def _():
        hidden_ref[...] = held[...]

    wide = 256
    for n in range(0, window, wide):
        cols = slice(n, n + wide)
        ups = slice(window + n, window + n + wide)
        gate = dot_nn(in_ref[...], wi_ref[:, cols])
        up = dot_nn(in_ref[...], wi_ref[:, ups])
        s = sigmoid(gate)
        silu = gate * s
        product_ref[:, cols] = (silu * up).astype(product_ref.dtype)
        slopes_ref[:, cols] = (up * s * (1.0 + gate * (1.0 - s))).astype(slopes_ref.dtype)
        slopes_ref[:, ups] = silu.astype(slopes_ref.dtype)
    wide = 512
    for n in range(0, width, wide):
        cols = slice(n, n + wide)
        out_ref[:, cols] = dot_nn(product_ref[...], wd_ref[:, cols]).astype(out_ref.dtype)


def feed_backward(window, dy_ref, slopes_ref, wi_ref, wd_ref, dlin_ref, dterm_ref):
    width = dy_ref.shape[1]
    wide = 256
    for n in range(0, window, wide):
        cols = slice(n, n + wide)
        ups = slice(window + n, window + n + wide)
        d_product = dot_nt(dy_ref[...], wd_ref[cols])
        for part in (cols, ups):
            slope = slopes_ref[:, part].astype(jnp.float32)
            dlin_ref[:, part] = (d_product * slope).astype(dlin_ref.dtype)
    wide = 512
    for n in range(0, width, wide):
        cols = slice(n, n + wide)
        dterm_ref[:, cols] = dot_nt(dlin_ref[...], wi_ref[cols]).astype(dterm_ref.dtype)


def whole(array):
    return pl.BlockSpec(array.shape, lambda i: (0, 0), pipeline_mode=pl.Buffered(1))


def run_feed_forward(tasks, axes, ident, zed, source, w_output, w_in, w_down, gain, rows):
    tokens, width = source.shape
    window = w_down.shape[0]

    def token(columns):
        return pl.BlockSpec((rows, columns), lambda i: (i, 0))

    results = [(fixed((rows, width)), jax.ShapeDtypeStruct((rows, width), jnp.float32))]
    for columns in (width, window, 2 * window, width):
        results.append((token(columns), jax.ShapeDtypeStruct((tokens, columns), zed.dtype)))
    return exchange_beside(
        tasks,
        axes,
        ident,
        functools.partial(feed_forward, rows, window),
        tokens // rows,
        6.0,
        [(zed, token(width)), (source, token(width))]
        + [(a, whole(a)) for a in (w_output, w_in, w_down, gain)],
        results,
        [pltpu.VMEM((rows, width), jnp.float32)],
        90 * 10**9,
    )


def run_feed_backward(dy, slopes, w_in, w_down, rows):
    tokens, width = dy.shape
    window = w_down.shape[0]

    def token(columns):
        return pl.BlockSpec((rows, columns), lambda i: (i, 0))

    columns = (2 * window, width)
    return pl.pallas_call(
        functools.partial(feed_backward, window),
        grid=(tokens // rows,),
        in_specs=[token(width), token(2 * window), whole(w_in), whole(w_down)],
        out_specs=[token(c) for c in columns],
        out_shape=[jax.ShapeDtypeStruct((tokens, c), dy.dtype) for c in columns],
        compiler_params=pltpu.CompilerParams(vmem_limit_bytes=60 * 1024 * 1024),
        cost_estimate=pl.CostEstimate(flops=30 * 10**9, bytes_accessed=40 * 10**6, transcendentals=0),
    )(dy, slopes, w_in, w_down)


def feed_gradients(in_ref, dlin_ref, product_ref, dy_ref, glin_ref, gdown_ref):
    glin_ref[...] = dot_tn(in_ref[...], dlin_ref[...]).astype(glin_ref.dtype)
    gdown_ref[...] = dot_tn(product_ref[...], dy_ref[...]).astype(gdown_ref.dtype)


def run_feed_gradients(tasks, axes, ident, mlp_in, d_lin, product, dy):
    tokens, width = mlp_in.shape
    window = product.shape[1]
    wide = 256
    if tokens > 2048:
        kind = mlp_in.dtype
        return (
            *exchange(tasks, axes, ident),
            contract_rows(mlp_in, d_lin).astype(kind),
            contract_rows(product, dy).astype(kind),
        )

    def columns(rows):
        return pl.BlockSpec((rows, wide), lambda i: (0, i))

    return exchange_beside(
        tasks,
        axes,
        ident,
        feed_gradients,
        width // wide,
        4.0,
        [
            (mlp_in, columns(tokens)),
            (d_lin, whole(d_lin)),
            (product, whole(product)),
            (dy, columns(tokens)),
        ],
        [
            (
                pl.BlockSpec((wide, 2 * window), lambda i: (i, 0)),
                jax.ShapeDtypeStruct((width, 2 * window), mlp_in.dtype),
            ),
            (columns(window), jax.ShapeDtypeStruct((window, width), mlp_in.dtype)),
        ],
        [],
        90 * 10**9,
    )


def project(left_side, right_side):
    return jnp.dot(left_side, right_side, preferred_element_type=jnp.float32)


def times_t(left_side, right_side):
    return lax.dot_general(
        left_side, right_side, (((1,), (1,)), ((), ())), preferred_element_type=jnp.float32
    )


def contract_rows(left_side, right_side):
    return lax.dot_general(
        left_side, right_side, (((0,), (0,)), ((), ())), preferred_element_type=jnp.float32
    )


def rms(values, gain, eps):
    return values * lax.rsqrt(jnp.mean(values * values, axis=-1, keepdims=True) + eps) * gain


def rms_back(values, gain, eps, grad):
    r = lax.rsqrt(jnp.mean(values * values, axis=-1, keepdims=True) + eps)
    inner = jnp.mean(values * gain * grad, axis=-1, keepdims=True)
    return r * gain * grad - values * (r * r * r) * inner, grad * values * r


def deal(stacked):
    return lax.all_to_all(stacked, "shard", split_axis=0, concat_axis=0, tiled=True)


def cross(blocks):
    shards = lax.axis_size("shard")
    return lax.ppermute(blocks, "shard", [(s, s ^ 1) for s in range(shards)])


def column_windows(columns, shards):
    own = columns // shards
    tiles = columns // HD
    width = 1
    while any(min(s * own // HD, tiles - width) * HD + width * HD < (s + 1) * own for s in range(shards)):
        width += 1

    def first(s):
        if isinstance(s, int):
            return min(s * own // HD, tiles - width) * HD
        return jnp.minimum(lax.div(s * own, HD), tiles - width) * HD

    return first, width * HD


def place_windows(kinds, shards, columns, window, first, own, in_ref, *out_refs):
    for kind, out_ref in zip(range(kinds), out_refs):
        for tile in range(columns // HD):
            total = None
            for s in range(shards):
                low = max(tile * HD, s * own)
                high = min((tile + 1) * HD, (s + 1) * own)
                if low < high:
                    at = kind * window + tile * HD - first(s)
                    term = in_ref[0, s, :, at : at + HD].astype(jnp.float32)
                    total = term if total is None else total + term
            out_ref[:, tile * HD : (tile + 1) * HD] = total


def widen(collected, kinds, columns, window, first):
    replicas, shards, part, wide = collected.shape
    return pl.pallas_call(
        functools.partial(place_windows, kinds, shards, columns, window, first, columns // shards),
        grid=(replicas,),
        in_specs=[pl.BlockSpec((1, shards, part, wide), lambda i: (i, 0, 0, 0))],
        out_specs=[pl.BlockSpec((part, columns), lambda i: (i, 0))] * kinds,
        out_shape=[jax.ShapeDtypeStruct((replicas * part, columns), jnp.float32)] * kinds,
        compiler_params=pltpu.CompilerParams(vmem_limit_bytes=48 * 1024 * 1024),
    )(collected)


def body(
    layer_input,
    out_cotangent,
    seq_lengths,
    seq_order,
    w_query,
    w_key,
    w_value,
    w_beta,
    w_outgate,
    w_output,
    conv_query,
    conv_key,
    conv_value,
    attn_gain,
    head_gain,
    mlp_gain,
    w_gate,
    w_up,
    w_down,
):
    bf16, f32 = jnp.bfloat16, jnp.float32
    shards = lax.axis_size("shard")
    shard = lax.axis_index("shard")
    both, group = ("shard", "replica"), ("shard",)
    rows, width = layer_input.shape
    tokens = shards * rows
    weight_rows = w_query.shape[0]
    own = w_output.shape[0]
    heads = own // HD
    hidden_own = w_down.shape[0]
    ffn = w_gate.shape[1]
    ffn_first, ffn_window = column_windows(ffn, shards)
    col_first, col_window = column_windows(width, shards)
    shift = shard * hidden_own - ffn_first(shard)

    total_heads = w_beta.shape[1]
    head_part = jnp.pad(head_gain, (0, weight_rows - head_gain.shape[0]))
    little = jnp.concatenate([w_beta, jnp.stack([attn_gain, mlp_gain, head_part], axis=1)], axis=1)
    little = jnp.pad(little, ((0, 0), (0, HD - little.shape[1])))
    attn_weights, all_source, little = exchange(
        [
            Spread((w_query, w_key, w_value, w_outgate), col_window, col_first, -0.5, 13.0),
            Gather("shard", layer_input, 8, turned=True),
            Gather("shard", little, 1, 0.0, 20.0),
        ],
        both,
        0,
    )
    full_attn_gain = little[:, :, total_heads].reshape(width).astype(f32)
    full_mlp_gain = little[:, :, total_heads + 1].reshape(width).astype(f32)
    head_row = little[:, : head_gain.shape[0], total_heads + 2].reshape(1, HD).astype(f32)
    beta = lax.dynamic_slice_in_dim(little.reshape(width, HD), shard * heads, heads, axis=1)
    attn_weights = jnp.concatenate(
        [attn_weights.reshape(width, 4 * own), jnp.pad(beta, ((0, 0), (0, HD - heads)))], axis=1
    )
    replicas = lax.axis_size("replica")
    part = weight_rows // replicas
    at = lax.axis_index("replica") * part
    windows = [
        lax.slice_in_dim(w, ffn_first(s), ffn_first(s) + ffn_window, axis=1)
        for s in range(shards)
        for w in (
            lax.dynamic_slice_in_dim(w_gate, at, part),
            lax.dynamic_slice_in_dim(w_up, at, part),
        )
    ]
    mlp_weights = jnp.stack(
        [jnp.concatenate(windows[2 * s : 2 * s + 2], axis=1) for s in range(shards)]
    )
    full_output = jnp.broadcast_to(
        lax.dynamic_slice_in_dim(w_output, at, part)[None], (shards, part, width)
    )
    later_weights = jnp.concatenate([mlp_weights, full_output], axis=2)
    later_weights, all_source = lax.optimization_barrier((later_weights, all_source))
    later_weights = deal(later_weights)
    low, off, rem = segment_masks(seq_lengths[0], seq_order[0], shards, rows)

    source = layer_input.astype(f32)
    all_source = all_source.reshape(tokens, width)
    normed = rms(all_source.astype(f32), full_attn_gain, 1e-6).astype(bf16)
    projected = project(normed, attn_weights).reshape(shards, rows, -1)
    taps = jnp.concatenate([conv_query, conv_key, conv_value], axis=0).astype(f32)
    zed, mixed, sums, *saves = mixer_forward(projected, taps, head_row, low, off, rem, heads)
    all_zed, mlp_weights, full_output = exchange(
        [
            Gather("shard", zed.reshape(tokens, own), 8, 0.0, 21.0, True, True),
            Trade(later_weights, 0, 2 * ffn_window, 0.2, 76.0),
            Trade(later_weights, 2 * ffn_window, width, 0.1, 76.0),
        ],
        both,
        2,
    )
    zed = zed.reshape(tokens, own)
    mlp_weights = mlp_weights.reshape(width, 2 * ffn_window)
    w_down = lax.dynamic_update_slice(jnp.zeros((ffn_window, width), bf16), w_down, (shift, 0))
    dy, hidden, mlp_in, product, slopes, out_terms = run_feed_forward(
        [Gather("shard", out_cotangent, 8, turned=True)],
        group,
        3,
        all_zed,
        all_source,
        full_output.reshape(width, width),
        mlp_weights,
        w_down,
        full_mlp_gain[None, :],
        rows,
    )
    dy = dy.reshape(tokens, width)
    d_lin, d_terms = run_feed_backward(dy, slopes, mlp_weights, w_down, rows)
    d_mlp_in, g_lin, g_down = run_feed_gradients(
        [Scatter("shard", d_terms, 4)], group, 4, mlp_in, d_lin, product, dy
    )
    d_hidden_norm, g_mlp_rows = rms_back(hidden, full_mlp_gain, 1e-6, d_mlp_in)
    d_hidden = out_cotangent.astype(f32) + d_hidden_norm

    d_attn, g_lin, g_down = exchange(
        [
            Gather("shard", d_hidden.astype(bf16), 8, turned=True),
            Sum(g_lin, 0.5, 26.0),
            Total(g_down, 0.1, 10.0, 62.0),
        ],
        both,
        5,
    )
    g_lin, d_attn = lax.optimization_barrier((g_lin, d_attn))
    g_lin = deal(g_lin)
    d_attn = d_attn.reshape(tokens, width)
    d_zed = times_t(d_attn, w_output).reshape(shards, rows, own)
    d_proj, g_taps, g_head = mixer_backward(
        projected, sums, mixed, d_zed, taps, head_row, low, off, rem, saves, heads
    )
    d_proj = d_proj.reshape(tokens, -1)
    g_proj = contract_rows(normed, d_proj).astype(bf16)
    beside = [
        Sum(g_proj, 0.1, 10.0, 20.0),
        Gather("replica", g_lin.reshape(-1, 2 * ffn_window), 4, 20.0, 46.0),
    ]
    if grid_of("shard")[1] == 2:
        d_normed, g_proj, g_lin = exchange_computed(
            Computed("shard", rows, width, bf16, 4, 12.0),
            beside,
            both,
            6,
            fill_input_terms,
            None,
            0,
            2.0,
            [(d_proj, whole(d_proj)), (attn_weights, whole(attn_weights))],
            [],
            90 * 10**9,
        )
    else:
        d_terms = times_t(d_proj, attn_weights).astype(bf16)
        d_normed, g_proj, g_lin = exchange(
            [Scatter("shard", d_terms, 4)] + beside, both, 6
        )

    g_proj = deal(g_proj)
    d_attn, d_normed = lax.optimization_barrier((d_attn, d_normed))
    g_output = contract_rows(zed, d_attn).astype(bf16)
    d_source, g_attn_rows = rms_back(source, full_attn_gain, 1e-6, d_normed)

    def dealt(values):
        return values.reshape(shards, -1)

    small = jnp.concatenate(
        [dealt(jnp.sum(g_attn_rows, axis=0)), dealt(jnp.sum(g_mlp_rows, axis=0)), dealt(g_head)], axis=1
    )
    small = jnp.pad(small, ((0, 0), (0, -small.shape[1] % HD)))
    small = jnp.broadcast_to(small[:, None, :], (shards, 8, small.shape[1]))
    out_terms, g_proj, g_output, small, g_taps = exchange(
        [
            Scatter("shard", out_terms, 4),
            Gather("replica", g_proj.reshape(-1, 4 * own + HD), 4, 0.3, 34.0),
            Total(g_output, 0.1, 8.0, 70.0, 25.0),
            Small(small, jnp.pad(g_taps, ((0, 16 - g_taps.shape[0]), (0, 0))), 50.0),
        ],
        both,
        7,
    )
    g_proj = g_proj.reshape(replicas, shards, -1, 4 * own + HD)
    g_lin = g_lin.reshape(replicas, shards, -1, 2 * ffn_window)
    g_query, g_key, g_value, g_outgate = widen(g_proj, 4, width, col_window, col_first)
    g_gate, g_up = widen(g_lin, 2, ffn, ffn_window, ffn_first)
    g_beta = g_proj[..., 4 * own : 4 * own + heads].transpose(0, 2, 1, 3)
    g_down = lax.dynamic_slice_in_dim(g_down.reshape(-1, width), shift, hidden_own)
    gains = width // shards
    return (
        (hidden + out_terms).astype(bf16),
        (d_hidden + d_source).astype(bf16),
        g_query,
        g_key,
        g_value,
        g_beta.reshape(weight_rows, total_heads).astype(f32),
        g_outgate,
        g_output.reshape(own, width).astype(f32),
        g_taps[:TAPS],
        g_taps[TAPS : 2 * TAPS],
        g_taps[2 * TAPS : 3 * TAPS],
        small[0, :gains],
        small[0, 2 * gains : 2 * gains + head_gain.shape[0]],
        small[0, gains : 2 * gains],
        g_gate,
        g_up,
        g_down.astype(f32),
    )


def solution(mesh):
    tokens = P(("replica", "shard"), None)
    whole, columns, vector = P("shard", None), P(None, "shard"), P("shard")
    in_specs = (tokens, tokens, P("replica", None, None), P("replica", None)) + (whole,) * 6
    in_specs += (columns,) * 3 + (vector,) * 3 + (whole,) * 3
    out_specs = (tokens, tokens) + (whole,) * 6 + (columns,) * 3 + (vector,) * 3 + (whole,) * 3
    return jax.shard_map(body, mesh=mesh, in_specs=in_specs, out_specs=out_specs, check_vma=False)
```
